32 devices in a mesh: head: 4 (over x, core), blk: 8 (over z, y).
Axes of the slice: x: 2, y: 2, z: 4, core: 2. Of those that a mesh axis runs over, the one named last changes fastest.
Arguments:
- layer_in: bfloat16 [4096, 2048], P(('head', 'blk')), may hold values from -6 to 6
- out_grad: bfloat16 [4096, 2048], P(('head', 'blk')), may hold values from -6 to 6
- norm_gain: bfloat16 [2048], P(('head', 'blk')), may hold values from 0.25 to 1.75
- norm_bias: bfloat16 [2048], P(('head', 'blk')), may hold values from -1.796875 to 1.796875
- w_qkv: bfloat16 [3, 2048, 2048], P(None, ('head', 'blk')), may hold values from -0.125 to 0.125
- b_qkv: bfloat16 [3, 2048], P(None, ('head', 'blk')), may hold values from -0.29882812 to 0.29882812
- w_out: bfloat16 [2048, 2048], P(('head', 'blk')), may hold values from -4 to 4
- b_out: bfloat16 [2048], P(('head', 'blk')), may hold values from -1.796875 to 1.796875
- w_up: bfloat16 [8192, 2048], P(('head', 'blk')), may hold values from -0.125 to 0.125
- b_up: bfloat16 [8192], P(('head', 'blk')), may hold values from -1.796875 to 1.796875
- w_down: bfloat16 [8192, 2048], P(('head', 'blk')), may hold values from -0.0625 to 0.0625
- b_down: bfloat16 [2048], P(('head', 'blk')), may hold values from -1.796875 to 1.796875
- seq_lengths: int32 [4], replicated, may hold values from 1 to 2048, 4096 in all
- token_place: int32 [4096], replicated, may hold values from 0 to 4095, as said below
Outputs:
- layer_out: bfloat16 [4096, 2048], P(('head', 'blk'))
- layer_in_grad: bfloat16 [4096, 2048], P(('head', 'blk'))
- norm_gain_grad: float32 [2048], P(('head', 'blk'))
- norm_bias_grad: float32 [2048], P(('head', 'blk'))
- w_qkv_grad: float32 [3, 2048, 2048], P(None, ('head', 'blk'))
- b_qkv_grad: float32 [3, 2048], P(None, ('head', 'blk'))
- w_out_grad: float32 [2048, 2048], P(('head', 'blk'))
- b_out_grad: float32 [2048], P(('head', 'blk'))
- w_up_grad: float32 [8192, 2048], P(('head', 'blk'))
- b_up_grad: float32 [8192], P(('head', 'blk'))
- w_down_grad: float32 [8192, 2048], P(('head', 'blk'))
- b_down_grad: float32 [2048], P(('head', 'blk'))
The draws below stay inside these ranges and needn't reach their ends.
Inputs may be any that keep to these rules, and one draw needn't show every extreme that they name: `seq_lengths`: sequence i fills the packed positions after those of sequences 0 to i - 1; the lengths add up to 4096. A permutation of the packed positions: row r of every row array is packed position token_place[r]. The 128 rows of each device hold one position of each aligned run of 32 packed positions.
All inputs are finite; a program needn't handle non-finite values.
Results may differ from the reference program's by a relative error of at most 0.014.
Values may be sent and summed in bfloat16 or wider, within the bound.
No kernel may reach another device: no remote copies, remote signals or barrier semaphores. Data moves between devices by JAX's collectives and lax.ppermute only.
A program may use at most 512 MiB of HBM per device.

```python
import math
import jax
import jax.numpy as jnp
import numpy as np
from jax import lax

HEAD_DIM = 64
ROT = 32
FF = 8192
TOK_DEV = 128
NSEQ = 4
D = 2048
TOKENS = 4096
MAXLEN = 2048


def draw_token_place(key, part):
    key = jax.random.fold_in(key, 11)
    device_count = TOKENS // TOK_DEV
    shift_key, order_key = jax.random.split(key)
    shifts = jax.random.randint(shift_key, (TOK_DEV,), 0, device_count)
    order_keys = jax.random.split(order_key, device_count)
    orders = jax.vmap(lambda one_key: jax.random.permutation(one_key, TOK_DEV))(order_keys).astype(jnp.int32)
    devices = jnp.arange(device_count, dtype=jnp.int32)[:, None]
    placed = orders * device_count + (devices - shifts[orders]) % device_count
    return placed.reshape(-1).astype(jnp.int32)


def block_levels(rng, shape, shards, least, high):
    loudness, own = 1.0, jax.random.fold_in(rng, 6)
    for position, blocks in shards:
        heights = jnp.exp(jax.random.uniform(jax.random.fold_in(own, position), (blocks,), jnp.float32, least / len(shards), high / len(shards)))
        loudness = loudness * jnp.repeat(heights, shape[position] // blocks).reshape([-1 if axis == position else 1 for axis in range(len(shape))])
    return loudness


def split_up(amount, total, most, slope):
    loads = [(1 << 20) // math.isqrt(grade ** slope) + 1 for grade in range(2, amount + 1)]
    spare, holding = total - most - (amount - 1), [1] * (amount - 1)
    while spare > 0:
        candidates = [i for i in range(amount - 1) if holding[i] < most]
        mass, left = sum([loads[i] for i in candidates]), spare
        for i in candidates:
            extra = min(most - holding[i], max(1, left * loads[i] // mass), spare)
            holding[i] = holding[i] + extra
            spare = spare - extra
    return np.array([most] + holding)


def uneven(rng, number_of, total, limit, lean):
    if number_of == 2:
        one = jax.random.randint(rng, (), max(1, total - limit), min(limit, total - 1) + 1)
        return jnp.stack([one, total - one])
    sizes = jnp.asarray(split_up(number_of, total, limit, lean), jnp.int32)
    couples = (number_of - 1) // 2
    giver, sink = sizes[1:1 + 2 * couples:2], sizes[2:2 + 2 * couples:2]
    margin = jnp.minimum(giver - 1, limit - sink)
    passed = jax.random.randint(jax.random.fold_in(rng, 1), (couples,), 0, 1 << 20) % (margin + 1)
    sizes = sizes.at[1:1 + 2 * couples:2].set(giver - passed).at[2:2 + 2 * couples:2].set(sink + passed)
    return sizes[jax.random.permutation(jax.random.fold_in(rng, 2), number_of)]


def bell_draw(stream_key, dims, deviation, reach, cuts=(), kind=jnp.bfloat16):
    values = jax.random.normal(stream_key, dims, jnp.float32) * deviation
    if len(cuts) > 0:
        values = block_levels(stream_key, dims, cuts, -0.22, 0.18) * values
    return jnp.clip(values, min=-reach, max=reach).astype(kind)


def setup_inputs(seed: int = 0) -> dict:
    arg_keys = jax.random.split(jax.random.key(seed), 15)
    return {
        "layer_in": bell_draw(arg_keys[0], (TOKENS, D), 1.0, 6.0, ((0, 32),)),
        "out_grad": bell_draw(arg_keys[1], (TOKENS, D), 1.0, 6.0, ((0, 32),)),
        "norm_gain": jnp.clip(1.0 + 0.15 * jax.random.normal(arg_keys[2], (D,), jnp.float32), 0.25, 1.75).astype(jnp.bfloat16),
        "norm_bias": bell_draw(arg_keys[3], (D,), 0.3, 1.796875, ((0, 32),)),
        "w_qkv": bell_draw(arg_keys[4], (3, D, D), D ** -0.5, 0.125, ((1, 32),)),
        "b_qkv": bell_draw(arg_keys[5], (3, D), 0.05, 0.29882812, ((1, 32),)),
        "w_out": bell_draw(arg_keys[6], (D, D), 2 ** -0.5, 4.0, ((0, 32),)),
        "b_out": bell_draw(arg_keys[7], (D,), 0.3, 1.796875, ((0, 32),)),
        "w_up": bell_draw(arg_keys[8], (FF, D), D ** -0.5, 0.125, ((0, 32),)),
        "b_up": bell_draw(arg_keys[9], (FF,), 0.3, 1.796875, ((0, 32),)),
        "w_down": bell_draw(arg_keys[10], (FF, D), FF ** -0.5, 0.0625, ((0, 32),)),
        "b_down": bell_draw(arg_keys[11], (D,), 0.3, 1.796875, ((0, 32),)),
        "seq_lengths": uneven(arg_keys[12], NSEQ, TOKENS, MAXLEN, 2).astype(jnp.int32),
        "token_place": draw_token_place(jax.random.fold_in(arg_keys[14], 71), 0),
    }


@jax.custom_vjp
def low(v):
    return lax.optimization_barrier(v.astype(jnp.bfloat16)).astype(jnp.float32)

@jax.custom_vjp
def low_back(v):
    return v

def low_keep(v):
    return (low(v), None)

def low_pass(kept, grad):
    return (grad,)

def back_keep(v):
    return (v, None)

def back_low(kept, grad):
    return (low(grad),)
low.defvjp(low_keep, low_pass)
low_back.defvjp(back_keep, back_low)

def seq_meta(packed, lengths):
    starts = (jnp.cumsum(lengths) - lengths).astype(jnp.int32)
    inside = packed[:, None] >= starts[None, :]
    segment = (lax.optimization_barrier(jnp.sum(inside.astype(jnp.int32), axis=1)) - 1).astype(jnp.int32)
    opening = lax.optimization_barrier(jnp.max(jnp.where(inside, starts[None, :], 0), axis=1)).astype(jnp.int32)
    return (segment, packed - opening)

def rotate(values, positions, direction):
    row_count = values.shape[0]
    split_heads = values.reshape(row_count, -1, HEAD_DIM)
    half_rot = ROT // 2
    lower_half = split_heads[:, :, :half_rot]
    upper_half = split_heads[:, :, half_rot:ROT]
    frequency = 10000.0 ** (-2.0 * jnp.arange(half_rot, dtype=jnp.float32) / ROT)
    angles = positions.astype(jnp.float32)[:, None] * frequency[None, :]
    cosine = jnp.cos(angles)[:, None, :]
    sine_part = direction * jnp.sin(angles)[:, None, :]
    turned = jnp.concatenate([lower_half * cosine - upper_half * sine_part, upper_half * cosine + lower_half * sine_part, split_heads[:, :, ROT:]], axis=2)
    return turned.reshape(row_count, -1)

def normalize(inputs, gain_vec, offset):
    center = lax.optimization_barrier(jnp.mean(inputs, axis=-1, keepdims=True))
    centered = inputs - center
    variance = lax.optimization_barrier(jnp.mean(centered * centered, axis=-1, keepdims=True))
    return centered * lax.rsqrt(variance + 1e-05) * gain_vec + offset

def attention(queries, key_rows, values, segment):
    block_rows = min(512, TOKENS)
    window = block_rows + MAXLEN
    head_count = queries.shape[1] // HEAD_DIM
    scaling = 1.0 / math.sqrt(HEAD_DIM)
    pad_rows = jnp.zeros((MAXLEN, queries.shape[1]), queries.dtype)
    keys_pad = jnp.concatenate([pad_rows, key_rows], axis=0)
    values_pad = jnp.concatenate([pad_rows, values], axis=0)
    seg_pad = jnp.concatenate([jnp.full((MAXLEN,), -1, jnp.int32), segment], axis=0)

    def one_block(first_row):
        query_blk = lax.dynamic_slice_in_dim(queries, first_row, block_rows, 0).reshape(block_rows, head_count, HEAD_DIM)
        key_blk = lax.dynamic_slice_in_dim(keys_pad, first_row, window, 0).reshape(window, head_count, HEAD_DIM)
        value_blk = lax.dynamic_slice_in_dim(values_pad, first_row, window, 0).reshape(window, head_count, HEAD_DIM)
        query_seg = lax.dynamic_slice_in_dim(segment, first_row, block_rows, 0)
        key_seg = lax.dynamic_slice_in_dim(seg_pad, first_row, window, 0)
        query_pos = first_row + jnp.arange(block_rows, dtype=jnp.int32)
        key_pos = first_row - MAXLEN + jnp.arange(window, dtype=jnp.int32)
        visible = (query_seg[:, None] == key_seg[None, :]) & (key_pos[None, :] <= query_pos[:, None])
        scores = low_back(jnp.einsum('qhd,khd->hqk', query_blk, key_blk, precision=lax.Precision.HIGHEST) * scaling)
        top_score = lax.optimization_barrier(jnp.max(jnp.where(visible[None], scores, -1e+30), axis=2, keepdims=True))
        expo = jnp.where(visible[None], jnp.exp(scores - top_score), 0.0)
        probs = expo / lax.optimization_barrier(jnp.sum(expo, axis=2, keepdims=True))
        mixed = jnp.einsum('hqk,khd->qhd', low(probs), value_blk, precision=lax.Precision.HIGHEST)
        return mixed.reshape(block_rows, -1)
    firsts = jnp.arange(TOKENS // block_rows, dtype=jnp.int32) * block_rows
    blocks = lax.map(jax.checkpoint(one_block), firsts)
    return blocks.reshape(TOKENS, -1)

def reference(layer_in, out_grad, norm_gain, norm_bias, w_qkv, b_qkv, w_out, b_out, w_up, b_up, w_down, b_down, seq_lengths, token_place):
    highest = lax.Precision.HIGHEST
    _, row_pos = seq_meta(token_place, seq_lengths)
    packed_seg, _ = seq_meta(jnp.arange(TOKENS, dtype=jnp.int32), seq_lengths)
    packing_order = jnp.argsort(token_place).astype(jnp.int32)

    def forward(inputs, gain_vec, offset, qkv_weight, qkv_bias, out_weight, out_bias, up_weight, up_bias, down_weight, down_bias):
        normed = low(normalize(inputs, gain_vec, offset))
        projected = low_back(jnp.einsum('ti,wci->twc', normed, qkv_weight, precision=highest) + qkv_bias[None])
        queries = low(rotate(projected[:, 0], row_pos, 1.0))
        key_rows = low(rotate(projected[:, 1], row_pos, 1.0))
        values = low(projected[:, 2])
        attended = attention(queries[packing_order], key_rows[packing_order], values[packing_order], packed_seg)
        attended_low = low(low_back(attended[token_place]))
        hidden = low_back(jnp.dot(normed, up_weight.T, precision=highest) + up_bias)
        active = low(jax.nn.gelu(hidden, approximate=True))
        branch = jnp.dot(attended_low, out_weight, precision=highest) + out_bias
        feed = jnp.dot(active, down_weight, precision=highest) + down_bias
        return inputs + branch + feed
    primals = [tensor.astype(jnp.float32) for tensor in (layer_in, norm_gain, norm_bias, w_qkv, b_qkv, w_out, b_out, w_up, b_up, w_down, b_down)]
    result, pullback = jax.vjp(forward, *primals)
    grads = pullback(out_grad.astype(jnp.float32))
    return (result.astype(jnp.bfloat16), grads[0].astype(jnp.bfloat16), grads[1], grads[2], grads[3], grads[4], grads[5], grads[6], grads[7], grads[8], grads[9], grads[10])
```

```python
import jax
import jax.numpy as jnp
from jax import lax
from jax.experimental import pallas as pl
from jax.experimental.pallas import tpu as pltpu
from jax.sharding import PartitionSpec as P

HEAD_DIM = 64
ROT = 32
AXES = ("head", "blk")
GROUP = 16
CHUNK = 512
NEG = -1e30
F32 = jnp.float32
BF16 = jnp.bfloat16


def swap(block, mask, count):
    return lax.ppermute(block, AXES, [(i, i ^ mask) for i in range(count)])


def dot_nn(a, b):
    return lax.dot_general(a, b, (((1,), (0,)), ((), ())), preferred_element_type=F32)


def dot_nt(a, b):
    return lax.dot_general(a, b, (((1,), (1,)), ((), ())), preferred_element_type=F32)


def dot_tn(a, b):
    return lax.dot_general(a, b, (((0,), (0,)), ((), ())), preferred_element_type=F32)


def seq_meta(packed, lengths):
    starts = jnp.cumsum(lengths) - lengths
    inside = packed[..., None] >= starts
    opening = jnp.max(jnp.where(inside, starts, 0), axis=-1)
    return opening, packed - opening


def plan_of(heads, blks):
    core = blks
    others = [1 << i for i in range((heads * blks).bit_length() - 1) if (1 << i) != core]
    if heads * blks == 32:
        y, z1, z2, x = others
        return core, [
            ((0, 48), (z2, z1, y, x)),
            ((48, 96), (z2, x, z1, y)),
            ((96, 128), (z2, y, x, z1)),
        ]
    turned = others[1:] + others[:1]
    return core, [((0, 64), tuple(others)), ((64, 128), tuple(turned))]


def slot_masks(core, order):
    masks = [0]
    for mask in tuple(order) + (core,):
        masks = masks + [m ^ mask for m in masks]
    return masks


def turn_rows(top, low, cosine, sine):
    return top * cosine - low * sine, low * cosine + top * sine


def rope_t(u, cosine, sine):
    half = ROT // 2
    first, second = turn_rows(u[:half], u[half:ROT], cosine, sine)
    return jnp.concatenate([first, second, u[ROT:]], axis=0)


def forward_kernel(
    lo_ref, mid_ref, z_ref, bias_ref, cos_ref, sin_ref, pq_ref, lq_ref, kp_ref,
    att_ref, ot_ref, lse_ref, q_ref, k_ref, v_ref, qt_ref, kt_ref, dvt_ref,
):
    t = pl.program_id(0)
    slots = z_ref.shape[0]
    tile = slots * GROUP
    chunk = q_ref.shape[1]
    per = tile // chunk
    z = z_ref[...].reshape(tile, 3 * HEAD_DIM) + bias_ref[...]
    for c in range(per):
        index = t * per + c
        cosine, sine = cos_ref[c], sin_ref[c]
        zt = z[c * chunk : (c + 1) * chunk].T
        qt = rope_t(zt[:HEAD_DIM], cosine, sine).astype(BF16).astype(F32)
        kt = rope_t(zt[HEAD_DIM : 2 * HEAD_DIM], cosine, sine).astype(BF16).astype(F32)
        vt = zt[2 * HEAD_DIM :].astype(BF16).astype(F32)
        q_ref[index] = qt.T.astype(BF16)
        k_ref[index] = kt.T.astype(BF16)
        v_ref[index] = vt.T.astype(BF16)
        qt_ref[index] = (qt * HEAD_DIM**-0.5).astype(BF16)
        kt_ref[index] = kt.astype(BF16)
        dvt_ref[index] = vt.astype(BF16)
    outs = []
    for c in range(per):
        qt = qt_ref[t * per + c]
        query_pos, query_lo = pq_ref[c], lq_ref[c]

        def step(kc, state, masked):
            run_max, run_sum, acc = state
            scores = dot_nn(k_ref[kc], qt)
            if masked:
                key_pos = kp_ref[kc]
                visible = (key_pos <= query_pos) & (key_pos >= query_lo)
                scores = jnp.where(visible, scores, NEG)
            new_max = jnp.maximum(run_max, jnp.max(scores, axis=0, keepdims=True))
            weights = jnp.exp(scores - new_max)
            if masked:
                weights = jnp.where(visible, weights, 0.0)
            rescale = jnp.exp(run_max - new_max)
            run_sum = run_sum * rescale + jnp.sum(weights, axis=0, keepdims=True)
            acc = acc * rescale + dot_nn(dvt_ref[kc], weights.astype(BF16))
            return new_max, run_sum, acc

        state = (
            jnp.full((1, chunk), NEG, F32),
            jnp.zeros((1, chunk), F32),
            jnp.zeros((HEAD_DIM, chunk), F32),
        )
        state = lax.fori_loop(lo_ref[t], mid_ref[t], lambda i, s: step(i, s, True), state)
        state = lax.fori_loop(mid_ref[t], t * per, lambda i, s: step(i, s, False), state)
        state = lax.fori_loop(t * per, (t + 1) * per, lambda i, s: step(i, s, True), state)
        run_max, run_sum, acc = state
        out = acc / run_sum
        ot_ref[c] = out
        lse_ref[c] = run_max + jnp.log(run_sum)
        outs.append(out.T)
    att = outs[0] if per == 1 else jnp.concatenate(outs, axis=0)
    att_ref[...] = att.astype(BF16).reshape(slots, GROUP, HEAD_DIM)


def backward_kernel(
    lo_ref, mid_ref, g_ref, cos_ref, sin_ref, pq_ref, lq_ref, kp_ref, ot_ref, lse_ref,
    q_ref, k_ref, v_ref, qt_ref, kt_ref, out_ref, dk_ref, dv_ref,
):
    t = pl.program_id(0)
    slots = g_ref.shape[0]
    tile = slots * GROUP
    chunk = q_ref.shape[1]
    per = tile // chunk
    scaling = HEAD_DIM**-0.5
    grads = g_ref[...].reshape(tile, HEAD_DIM)
    for c in range(per):
        dk_ref[t * per + c] = jnp.zeros((chunk, HEAD_DIM), F32)
        dv_ref[t * per + c] = jnp.zeros((chunk, HEAD_DIM), F32)
    parts = []
    for c in range(per):
        index = t * per + c
        do = grads[c * chunk : (c + 1) * chunk]
        dot32 = do.astype(F32).T
        dot16 = dot32.astype(BF16)
        delta = jnp.sum(dot32 * ot_ref[c], axis=0, keepdims=True)
        lse = lse_ref[c]
        q, qt = q_ref[index], qt_ref[index]
        query_pos, query_lo = pq_ref[c], lq_ref[c]

        def step(kc, dqt, masked):
            probs = jnp.exp(dot_nn(k_ref[kc], qt) - lse)
            if masked:
                key_pos = kp_ref[kc]
                visible = (key_pos <= query_pos) & (key_pos >= query_lo)
                probs = jnp.where(visible, probs, 0.0)
            dv_ref[kc] += dot_nn(probs.astype(BF16), do)
            prob_grad = dot_nn(v_ref[kc], dot16)
            score_grad = (probs * (prob_grad - delta)).astype(BF16)
            dk_ref[kc] += dot_nn(score_grad, q)
            return dqt + dot_nn(kt_ref[kc], score_grad)

        dqt = jnp.zeros((HEAD_DIM, chunk), F32)
        dqt = lax.fori_loop(lo_ref[t], mid_ref[t], lambda i, s: step(i, s, True), dqt)
        dqt = lax.fori_loop(mid_ref[t], t * per, lambda i, s: step(i, s, False), dqt)
        dqt = lax.fori_loop(t * per, (t + 1) * per, lambda i, s: step(i, s, True), dqt)
        parts.append(rope_t(dqt * scaling, cos_ref[index], -sin_ref[index]).T)
    dq = parts[0] if per == 1 else jnp.concatenate(parts, axis=0)
    here = pl.ds(pl.multiple_of(t * GROUP, GROUP), GROUP)
    out_ref[:, here, :HEAD_DIM] = dq.astype(BF16).reshape(slots, GROUP, HEAD_DIM)

    @pl.when(t == pl.num_programs(0) - 1)
    def _():
        def finish(u, carry):
            rows = []
            for c in range(per):
                index = u * per + c
                dkt = rope_t(dk_ref[index].T * scaling, cos_ref[index], -sin_ref[index])
                rows.append(jnp.concatenate([dkt.T, dv_ref[index]], axis=1))
            both = rows[0] if per == 1 else jnp.concatenate(rows, axis=0)
            place = pl.ds(pl.multiple_of(u * GROUP, GROUP), GROUP)
            out_ref[:, place, HEAD_DIM:] = both.astype(BF16).reshape(slots, GROUP, 2 * HEAD_DIM)
            return carry

        lax.fori_loop(0, pl.num_programs(0), finish, 0)


def whole_block(shape):
    zeros = (0,) * len(shape)
    return pl.BlockSpec(tuple(shape), lambda t, *refs: zeros)


def tile_block(shape, axis):
    def place(t, *refs):
        return tuple(t if i == axis else 0 for i in range(len(shape)))

    return pl.BlockSpec(tuple(shape), place)


def attention_meta(positions, seq_lengths, chunk):
    tiles, tile = positions.shape
    count = tiles * tile // chunk
    per = tile // chunk
    opening, place = seq_meta(positions, seq_lengths)
    frequency = 10000.0 ** (-2.0 * jnp.arange(ROT // 2, dtype=F32) / ROT)
    angles = place.astype(F32).reshape(count, 1, chunk) * frequency[None, :, None]
    ends = jnp.arange(tiles, dtype=jnp.int32) * tile
    first_open, _ = seq_meta(ends, seq_lengths)
    last_open, _ = seq_meta(ends + tile - 1, seq_lengths)
    own = jnp.arange(tiles, dtype=jnp.int32) * per
    low = (first_open // tile) * per
    middle = jnp.minimum(((last_open + tile - 1) // tile) * per, own)
    return dict(
        low=low.astype(jnp.int32),
        middle=middle.astype(jnp.int32),
        cosine=jnp.cos(angles),
        sine=jnp.sin(angles),
        query_pos=positions.reshape(count, 1, chunk),
        query_lo=opening.reshape(count, 1, chunk),
        key_pos=positions.reshape(count, chunk, 1),
    )


def attention_forward(zq, bias, meta):
    slots, rows, width = zq.shape
    tile = slots * GROUP
    tiles = rows // GROUP
    count, _, chunk = meta["query_pos"].shape
    per = tile // chunk
    half = ROT // 2
    nat = jax.ShapeDtypeStruct((count, chunk, HEAD_DIM), BF16)
    turned = jax.ShapeDtypeStruct((count, HEAD_DIM, chunk), BF16)
    shapes = [
        jax.ShapeDtypeStruct((slots, rows, HEAD_DIM), BF16),
        jax.ShapeDtypeStruct((count, HEAD_DIM, chunk), F32),
        jax.ShapeDtypeStruct((count, 1, chunk), F32),
        nat, nat, nat, turned, turned,
    ]
    return pl.pallas_call(
        forward_kernel,
        out_shape=shapes,
        grid_spec=pltpu.PrefetchScalarGridSpec(
            num_scalar_prefetch=2,
            grid=(tiles,),
            in_specs=[
                tile_block((slots, GROUP, width), 1),
                whole_block((1, width)),
                tile_block((per, half, chunk), 0),
                tile_block((per, half, chunk), 0),
                tile_block((per, 1, chunk), 0),
                tile_block((per, 1, chunk), 0),
                whole_block((count, chunk, 1)),
            ],
            out_specs=[
                tile_block((slots, GROUP, HEAD_DIM), 1),
                tile_block((per, HEAD_DIM, chunk), 0),
                tile_block((per, 1, chunk), 0),
                whole_block(nat.shape),
                whole_block(nat.shape),
                whole_block(nat.shape),
                whole_block(turned.shape),
                whole_block(turned.shape),
            ],
            scratch_shapes=[pltpu.VMEM(turned.shape, BF16)],
        ),
        compiler_params=pltpu.CompilerParams(
            dimension_semantics=("arbitrary",), vmem_limit_bytes=58 * 1024 * 1024
        ),
        cost_estimate=pl.CostEstimate(
            flops=30_000_000_000, bytes_accessed=12_000_000, transcendentals=6_000_000
        ),
        name="attention_forward",
    )(
        meta["low"], meta["middle"], zq, bias, meta["cosine"], meta["sine"],
        meta["query_pos"], meta["query_lo"], meta["key_pos"],
    )


def attention_backward(heads_grad, meta, saved):
    slots, rows, _ = heads_grad.shape
    tile = slots * GROUP
    tiles = rows // GROUP
    count, _, chunk = meta["query_pos"].shape
    per = tile // chunk
    half = ROT // 2
    ot, lse, q, k, v, qt, kt = saved
    return pl.pallas_call(
        backward_kernel,
        out_shape=jax.ShapeDtypeStruct((slots, rows, 3 * HEAD_DIM), BF16),
        grid_spec=pltpu.PrefetchScalarGridSpec(
            num_scalar_prefetch=2,
            grid=(tiles,),
            in_specs=[
                tile_block((slots, GROUP, HEAD_DIM), 1),
                whole_block((count, half, chunk)),
                whole_block((count, half, chunk)),
                tile_block((per, 1, chunk), 0),
                tile_block((per, 1, chunk), 0),
                whole_block((count, chunk, 1)),
                tile_block((per, HEAD_DIM, chunk), 0),
                tile_block((per, 1, chunk), 0),
                whole_block(q.shape),
                whole_block(k.shape),
                whole_block(v.shape),
                whole_block(qt.shape),
                whole_block(kt.shape),
            ],
            out_specs=whole_block((slots, rows, 3 * HEAD_DIM)),
            scratch_shapes=[
                pltpu.VMEM((count, chunk, HEAD_DIM), F32),
                pltpu.VMEM((count, chunk, HEAD_DIM), F32),
            ],
        ),
        compiler_params=pltpu.CompilerParams(
            dimension_semantics=("arbitrary",), vmem_limit_bytes=62 * 1024 * 1024
        ),
        cost_estimate=pl.CostEstimate(
            flops=60_000_000_000, bytes_accessed=12_000_000, transcendentals=6_000_000
        ),
        name="attention_backward",
    )(
        meta["low"], meta["middle"], heads_grad, meta["cosine"], meta["sine"],
        meta["query_pos"], meta["query_lo"], meta["key_pos"], ot, lse, q, k, v, qt, kt,
    )


def gather_rows(rows, core, pieces, count):
    found = []
    for (begin, end), order in pieces:
        held = rows[begin:end][None]
        for mask in order[:-1]:
            held = jnp.concatenate([held, swap(held, mask, count)], axis=0)
        last = swap(held, order[-1], count)
        found.append([held, last, swap(held, core, count), swap(last, core, count)])
    return found


def reduce_rows(sent, kept, order, count):
    for mask in order[::-1][:-1]:
        total = kept.astype(F32) + swap(sent, mask, count).astype(F32)
        middle = total.shape[0] // 2
        sent, kept = total[middle:].astype(BF16), total[:middle].astype(BF16)
    total = kept.astype(F32) + swap(sent, order[0], count).astype(F32)
    return total[0]


def gather_small(block, stages, count):
    for masks, axis_len in stages:
        parts = [block if m == 0 else swap(block, m, count) for m in masks]
        block = jnp.stack(parts, axis=0)
    return block.reshape((-1,) + block.shape[len(stages) :])


def reduce_small(block, stages, count):
    for masks, axis_len in stages[::-1]:
        block = block.reshape((len(masks), -1) + block.shape[1:])
        total = block[0]
        for i, m in enumerate(masks):
            if m:
                total = total + swap(block[i], m, count)
        block = total
    return block[0]


def gelu_tanh(values):
    return jax.nn.gelu(values, approximate=True)


def gelu_back(hidden, act_grad):
    _, pullback = jax.vjp(gelu_tanh, hidden)
    return pullback(act_grad)[0]


def pairwise(block, core, count):
    half = block.shape[0] // 2
    return block[:half], swap(block[half:], core, count)


def per_device(
    layer_in, out_grad, norm_gain, norm_bias, w_qkv, b_qkv, w_out, b_out, w_up, b_up,
    w_down, b_down, seq_lengths, token_place,
):
    heads, blks = lax.axis_size("head"), lax.axis_size("blk")
    count = heads * blks
    me = lax.axis_index("head") * blks + lax.axis_index("blk")
    rows, width = layer_in.shape
    features = w_qkv.shape[1]
    hidden_units = w_up.shape[0]
    owners = HEAD_DIM // features
    core, pieces = plan_of(heads, blks)
    stages = [
        ([m for m in range(blks)], blks),
        ([m * blks for m in range(heads)], heads),
    ]

    place = token_place.reshape(count, rows)
    own_place = lax.dynamic_slice_in_dim(place, me, 1, 0)[0]
    order_hot = (
        own_place[None, :] // count == jnp.arange(rows, dtype=jnp.int32)[:, None]
    ).astype(BF16)
    x_sorted = dot_nn(order_hot, layer_in)
    g_sorted = dot_nn(order_hot, out_grad).astype(BF16)

    vectors = jnp.stack([norm_gain, norm_bias, b_out, b_down])
    vectors = gather_small(vectors, stages, count)
    absolute = me ^ jnp.arange(count, dtype=jnp.int32)
    choose = (absolute[None, :] == jnp.arange(count, dtype=jnp.int32)[:, None]).astype(BF16)
    vectors = dot_nn(choose, vectors.reshape(count, -1)).reshape(count, 4, -1)
    vectors = jnp.transpose(vectors, (1, 0, 2)).reshape(4, width)
    gain, offset, out_bias, down_bias = (vectors[i][None] for i in range(4))

    center = jnp.mean(x_sorted, axis=-1, keepdims=True)
    centered = x_sorted - center
    variance = jnp.mean(centered * centered, axis=-1, keepdims=True)
    inverse = lax.rsqrt(variance + 1e-05)
    x_hat = centered * inverse
    normed = (x_hat * gain + offset).astype(BF16)

    normed_all = gather_rows(normed, core, pieces, count)
    g_all = gather_rows(g_sorted, core, pieces, count)

    inside = place // count
    sorted_place = jnp.sum(
        jnp.where(
            inside[:, None, :] == jnp.arange(rows, dtype=jnp.int32)[None, :, None],
            place[:, None, :],
            0,
        ),
        axis=2,
    )
    chunks = []
    for (begin, end), order in pieces:
        slots = me ^ jnp.array(slot_masks(core, order), dtype=jnp.int32)
        chunks.append(sorted_place[slots, begin:end])
    positions = jnp.concatenate(chunks, axis=1)
    tiles = rows // GROUP
    positions = jnp.transpose(positions.reshape(count, tiles, GROUP), (1, 0, 2))
    positions = positions.reshape(tiles, count * GROUP)
    meta = attention_meta(positions, seq_lengths, min(CHUNK, count * GROUP))

    w_in = jnp.concatenate([w_qkv.reshape(3 * features, width), w_up], axis=0)
    w_back = jnp.concatenate([w_out, w_down], axis=0)
    w_in_other = swap(w_in, core, count)
    w_back_other = swap(w_back, core, count)

    def all_rows(buffers, weight):
        found = []
        for (begin, end), parts in zip([p[0] for p in pieces], buffers):
            blocks = [
                dot_nt(b.reshape(-1, width), weight).reshape(-1, end - begin, weight.shape[0])
                for b in parts
            ]
            found.append(jnp.concatenate(blocks, axis=0))
        return jnp.concatenate(found, axis=1)

    z = all_rows(normed_all, w_in)
    zq, hidden = z[:, :, : 3 * features], z[:, :, 3 * features :]
    hidden = hidden + b_up.astype(F32)
    active = gelu_tanh(hidden).astype(BF16)
    bias = b_qkv.astype(F32)

    member = me % owners
    member_order = member ^ jnp.arange(owners, dtype=jnp.int32)

    def from_owners(block):
        found = [block]
        for extra in range(1, owners):
            other = swap(block, extra, count)
            flipped = []
            at = 0
            for (begin, end), order in pieces:
                masks = slot_masks(core, order)
                where = [masks.index(m ^ extra) for m in masks]
                flipped.append(other[jnp.array(where), begin:end])
            found.append(jnp.concatenate(flipped, axis=1))
        stacked = jnp.stack(found)[member_order]
        return jnp.moveaxis(stacked, 0, -2).reshape(block.shape[:-1] + (HEAD_DIM,))

    def own_features(block):
        if owners == 1:
            return block
        shape = block.shape
        split = block.reshape(shape[:2] + (-1, owners, features))
        return lax.dynamic_index_in_dim(split, member, 3, False).reshape(shape[:2] + (-1,))

    if owners > 1:
        zq = zq.reshape(zq.shape[:2] + (3, features)) + bias
        zq = from_owners(zq.astype(F32)).reshape(zq.shape[:2] + (3 * HEAD_DIM,))
        bias = jnp.zeros((3, HEAD_DIM), F32)
    attended, *saved = attention_forward(zq, bias.reshape(1, 3 * HEAD_DIM), meta)
    attended = own_features(attended)

    def partial_sums(first, second, own_weight, other_weight, cut):
        first_own, first_other = pairwise(first, core, count)
        second_own, second_other = pairwise(second, core, count)
        both = jnp.concatenate([first_own, first_other, second_own, second_other], axis=2)
        weight = jnp.concatenate(
            [own_weight[:cut], other_weight[:cut], own_weight[cut:], other_weight[cut:]], axis=0
        )
        middle = both.shape[0] // 2
        found = []
        for (begin, end), order in pieces:
            def product(part):
                flat = part[:, begin:end].reshape(-1, weight.shape[0])
                return dot_nn(flat, weight).astype(BF16).reshape(-1, end - begin, width)

            found.append(reduce_rows(product(both[middle:]), product(both[:middle]), order, count))
        return jnp.concatenate(found, axis=0)

    mixed = partial_sums(attended, active, w_back, w_back_other, features)

    back = all_rows(g_all, w_back)
    heads_grad = back[:, :, :features].astype(BF16)
    hidden_grad = gelu_back(hidden, back[:, :, features:]).astype(BF16)
    if owners > 1:
        heads_grad = from_owners(heads_grad[:, :, None, :]).reshape(heads_grad.shape[:2] + (HEAD_DIM,))
    qkv_grad = attention_backward(heads_grad, meta, saved[:7])
    qkv_grad = own_features(qkv_grad)
    normed_grad = partial_sums(qkv_grad, hidden_grad, w_in, w_in_other, 3 * features)

    def weight_sums(rows_left, buffers):
        total = 0.0
        for (begin, end), parts in zip([p[0] for p in pieces], buffers):
            left = rows_left[:, begin:end].reshape(-1, rows_left.shape[2])
            right = jnp.concatenate(parts, axis=0).reshape(-1, width)
            total = total + dot_tn(left, right)
        return total

    back_grad = weight_sums(jnp.concatenate([attended, active], axis=2), g_all)
    in_grad = weight_sums(jnp.concatenate([qkv_grad, hidden_grad], axis=2), normed_all)
    b_in = jnp.concatenate(
        [
            jnp.sum(qkv_grad.astype(F32), axis=(0, 1)),
            jnp.sum(hidden_grad.astype(F32), axis=(0, 1)),
        ]
    )

    layer_out = (x_sorted + mixed + out_bias + down_bias).astype(BF16)
    layer_out = dot_tn(order_hot, layer_out).astype(BF16)
    e = normed_grad * gain
    input_part = inverse * (
        e
        - jnp.mean(e, axis=-1, keepdims=True)
        - x_hat * jnp.mean(e * x_hat, axis=-1, keepdims=True)
    )
    input_grad = (g_sorted.astype(F32) + input_part).astype(BF16)
    input_grad = dot_tn(order_hot, input_grad).astype(BF16)
    sums = jnp.stack(
        [
            jnp.sum(normed_grad * x_hat, axis=0),
            jnp.sum(normed_grad, axis=0),
            jnp.sum(g_sorted.astype(F32), axis=0),
        ]
    )
    sums = jnp.transpose(sums.reshape(3, count, -1), (1, 0, 2))[absolute]
    sums = reduce_small(sums, stages, count)
    return (
        layer_out,
        input_grad,
        sums[0],
        sums[1],
        in_grad[: 3 * features].reshape(3, features, width),
        b_in[: 3 * features].reshape(3, features),
        back_grad[:features],
        sums[2],
        in_grad[3 * features :],
        b_in[3 * features :],
        back_grad[features:],
        sums[2],
    )


def solution(mesh):
    rows, vector = P(AXES, None), P(AXES)
    qkv, qkv_bias = P(None, AXES, None), P(None, AXES)
    in_specs = (
        rows, rows, vector, vector, qkv, qkv_bias, rows, vector, rows, vector, rows, vector,
        P(), P(),
    )
    out_specs = (
        rows, rows, vector, vector, qkv, qkv_bias, rows, vector, rows, vector, rows, vector,
    )
    return jax.shard_map(
        per_device, mesh=mesh, in_specs=in_specs, out_specs=out_specs, check_vma=False
    )
```

```python
import jax
import jax.numpy as jnp
from jax import lax
from jax.experimental import pallas as pl
from jax.experimental.pallas import tpu as pltpu
from jax.sharding import PartitionSpec as P

HEAD_DIM = 64
ROT = 32
AXES = ("head", "blk")
GROUP = 16
CHUNK = 512
NEG = -1e30
OWN_GATHER = False
OWN_REDUCE = False
F32 = jnp.float32
BF16 = jnp.bfloat16


def swap(block, mask, count):
    return lax.ppermute(block, AXES, [(i, i ^ mask) for i in range(count)])


def dot_nn(a, b):
    return lax.dot_general(a, b, (((1,), (0,)), ((), ())), preferred_element_type=F32)


def dot_nt(a, b):
    return lax.dot_general(a, b, (((1,), (1,)), ((), ())), preferred_element_type=F32)


def dot_tn(a, b):
    return lax.dot_general(a, b, (((0,), (0,)), ((), ())), preferred_element_type=F32)


def opening_of(packed, lengths):
    starts = jnp.cumsum(lengths) - lengths
    inside = packed[..., None] >= starts
    return jnp.max(jnp.where(inside, starts, 0), axis=-1)


def pieces_of(blks, rows, own):
    bits = [1 << i for i in range(blks.bit_length() - 1)][::-1]
    if not own:
        return [((0, rows), bits)]
    half = rows // 2
    if blks == 8:
        z2, z1, y = bits
        return [((0, half), [z2, z1, y]), ((half, rows), [z2, y, z1])]
    return [((0, half), bits), ((half, rows), bits[1:] + bits[:1])]


def slot_masks(order):
    masks = [0]
    for mask in order:
        masks = masks + [m ^ mask for m in masks]
    return masks


def prepare_kernel(z_ref, bias_ref, cos_ref, up_ref, down_ref, out_ref):
    heads = out_ref.shape[0]
    span = heads * HEAD_DIM
    z = z_ref[...] + bias_ref[...]
    lanes = cos_ref.shape[1]
    half = ROT // 2
    turned = []
    for first in range(0, 2 * span, lanes):
        u = z[:, first : first + lanes]
        turned.append(
            u * cos_ref[...]
            + pltpu.roll(u, lanes - half, 1) * up_ref[...]
            + pltpu.roll(u, half, 1) * down_ref[...]
        )
    both = jnp.concatenate(turned, axis=1)
    for r in range(heads):
        a, b = r * HEAD_DIM, (r + 1) * HEAD_DIM
        row = [both[:, a:b], both[:, span + a : span + b], z[:, 2 * span + a : 2 * span + b]]
        out_ref[r] = jnp.concatenate(row, axis=1).astype(BF16)


def prepare(z, bias, place, heads):
    rows, width = z.shape
    lanes = 2 * HEAD_DIM
    block = min(256, rows)
    lane = jnp.arange(lanes, dtype=jnp.int32) % HEAD_DIM
    half = ROT // 2
    frequency = 10000.0 ** (-2.0 * (lane % half).astype(F32) / ROT)
    angles = place.astype(F32)[:, None] * frequency[None, :]
    cosine = jnp.where(lane < ROT, jnp.cos(angles), 1.0)
    sine = jnp.sin(angles)
    up = jnp.where(lane < half, -sine, 0.0)
    down = jnp.where((lane >= half) & (lane < ROT), sine, 0.0)
    table = pl.BlockSpec((block, lanes), lambda i: (i, 0))
    return pl.pallas_call(
        prepare_kernel,
        out_shape=jax.ShapeDtypeStruct((heads, rows, 3 * HEAD_DIM), BF16),
        grid=(rows // block,),
        in_specs=[
            pl.BlockSpec((block, width), lambda i: (i, 0)),
            pl.BlockSpec((1, width), lambda i: (0, 0)),
            table, table, table,
        ],
        out_specs=pl.BlockSpec((heads, block, 3 * HEAD_DIM), lambda i: (0, i, 0)),
        compiler_params=pltpu.CompilerParams(vmem_limit_bytes=32 * 1024 * 1024),
        cost_estimate=pl.CostEstimate(
            flops=rows * width * 8, bytes_accessed=rows * width * 8, transcendentals=0
        ),
        name="rotary",
    )(z, bias, cosine, up, down)


def rope_t(u, cosine, sine):
    half = ROT // 2
    top, low = u[:half], u[half:ROT]
    return jnp.concatenate(
        [top * cosine - low * sine, low * cosine + top * sine, u[ROT:]], axis=0
    )


def rows_of(refs, at=slice(None)):
    found = []
    for ref in refs:
        block = ref[:, at, :]
        found.append(block.reshape(block.shape[0] * block.shape[1], block.shape[2]))
    return jnp.concatenate(found, axis=0)


def forward_kernel(sources, *refs):
    lo_ref, mid_ref = refs[:2]
    in_refs = refs[2 : 2 + sources]
    pq_ref, lq_ref, kp_ref = refs[2 + sources : 5 + sources]
    att_refs = refs[5 + sources : 5 + 2 * sources]
    ot_ref, lse_ref, q_ref, k_ref, v_ref, qt_ref, kt_ref, vt_ref = refs[5 + 2 * sources :]
    t = pl.program_id(0)
    chunk = q_ref.shape[1]
    rows = rows_of(in_refs)
    per = rows.shape[0] // chunk
    for c in range(per):
        index = t * per + c
        part = rows[c * chunk : (c + 1) * chunk]
        q_ref[index] = part[:, :HEAD_DIM]
        k_ref[index] = part[:, HEAD_DIM : 2 * HEAD_DIM]
        v_ref[index] = part[:, 2 * HEAD_DIM :]
        turned = part.astype(F32).T
        qt_ref[index] = (turned[:HEAD_DIM] * HEAD_DIM**-0.5).astype(BF16)
        kt_ref[index] = turned[HEAD_DIM : 2 * HEAD_DIM].astype(BF16)
        vt_ref[index] = turned[2 * HEAD_DIM :].astype(BF16)
    outs = []
    for c in range(per):
        qt = qt_ref[t * per + c]
        query_pos, query_lo = pq_ref[c], lq_ref[c]

        def step(kc, state, masked):
            run_max, run_sum, acc = state
            scores = dot_nn(k_ref[kc], qt)
            if masked:
                key_pos = kp_ref[kc]
                visible = (key_pos <= query_pos) & (key_pos >= query_lo)
                scores = jnp.where(visible, scores, NEG)
            new_max = jnp.maximum(run_max, jnp.max(scores, axis=0, keepdims=True))
            weights = jnp.exp(scores - new_max)
            if masked:
                weights = jnp.where(visible, weights, 0.0)
            rescale = jnp.exp(run_max - new_max)
            run_sum = run_sum * rescale + jnp.sum(weights, axis=0, keepdims=True)
            acc = acc * rescale + dot_nn(vt_ref[kc], weights.astype(BF16))
            return new_max, run_sum, acc

        state = (
            jnp.full((1, chunk), NEG, F32),
            jnp.zeros((1, chunk), F32),
            jnp.zeros((HEAD_DIM, chunk), F32),
        )
        state = lax.fori_loop(lo_ref[t], mid_ref[t], lambda i, s: step(i, s, True), state)
        state = lax.fori_loop(mid_ref[t], t * per, lambda i, s: step(i, s, False), state)
        state = lax.fori_loop(t * per, (t + 1) * per, lambda i, s: step(i, s, True), state)
        run_max, run_sum, acc = state
        out = acc / run_sum
        ot_ref[c] = out
        lse_ref[c] = run_max + jnp.log(run_sum)
        outs.append(out.T.astype(BF16))
    att = outs[0] if per == 1 else jnp.concatenate(outs, axis=0)
    span = att.shape[0] // sources
    for i, ref in enumerate(att_refs):
        ref[...] = att[i * span : (i + 1) * span].reshape(ref.shape)


def backward_kernel(sources, *refs):
    lo_ref, mid_ref = refs[:2]
    g_refs = refs[2 : 2 + sources]
    cos_ref, sin_ref, pq_ref, lq_ref, kp_ref, ot_ref, lse_ref = refs[2 + sources : 9 + sources]
    q_ref, k_ref, v_ref, qt_ref, kt_ref = refs[9 + sources : 14 + sources]
    out_refs = refs[14 + sources : 14 + 2 * sources]
    dk_ref, dv_ref = refs[14 + 2 * sources :]
    t = pl.program_id(0)
    chunk = q_ref.shape[1]
    scaling = HEAD_DIM**-0.5
    grads = rows_of(g_refs)
    per = grads.shape[0] // chunk
    for c in range(per):
        dk_ref[t * per + c] = jnp.zeros((chunk, HEAD_DIM), F32)
        dv_ref[t * per + c] = jnp.zeros((chunk, HEAD_DIM), F32)
    parts = []
    for c in range(per):
        index = t * per + c
        do = grads[c * chunk : (c + 1) * chunk]
        dot32 = do.astype(F32).T
        dot16 = dot32.astype(BF16)
        delta = jnp.sum(dot32 * ot_ref[c], axis=0, keepdims=True)
        lse = lse_ref[c]
        q, qt = q_ref[index], qt_ref[index]
        query_pos, query_lo = pq_ref[c], lq_ref[c]

        def step(kc, dqt, masked):
            probs = jnp.exp(dot_nn(k_ref[kc], qt) - lse)
            if masked:
                key_pos = kp_ref[kc]
                visible = (key_pos <= query_pos) & (key_pos >= query_lo)
                probs = jnp.where(visible, probs, 0.0)
            dv_ref[kc] += dot_nn(probs.astype(BF16), do)
            prob_grad = dot_nn(v_ref[kc], dot16)
            score_grad = (probs * (prob_grad - delta)).astype(BF16)
            dk_ref[kc] += dot_nn(score_grad, q)
            return dqt + dot_nn(kt_ref[kc], score_grad)

        dqt = jnp.zeros((HEAD_DIM, chunk), F32)
        dqt = lax.fori_loop(lo_ref[t], mid_ref[t], lambda i, s: step(i, s, True), dqt)
        dqt = lax.fori_loop(mid_ref[t], t * per, lambda i, s: step(i, s, False), dqt)
        dqt = lax.fori_loop(t * per, (t + 1) * per, lambda i, s: step(i, s, True), dqt)
        parts.append(rope_t(dqt * scaling, cos_ref[index], -sin_ref[index]).T)

    def store(block, u, first):
        span = block.shape[0] // sources
        here = pl.ds(pl.multiple_of(u * GROUP, GROUP), GROUP)
        for i, ref in enumerate(out_refs):
            part = block[i * span : (i + 1) * span].astype(BF16)
            part = part.reshape(ref.shape[0], GROUP, part.shape[1])
            ref[:, here, first : first + part.shape[2]] = part

    store(parts[0] if per == 1 else jnp.concatenate(parts, axis=0), t, 0)

    @pl.when(t == pl.num_programs(0) - 1)
    def _():
        def finish(u, carry):
            found = []
            for c in range(per):
                index = u * per + c
                dkt = rope_t(dk_ref[index].T * scaling, cos_ref[index], -sin_ref[index])
                found.append(jnp.concatenate([dkt.T, dv_ref[index]], axis=1))
            store(found[0] if per == 1 else jnp.concatenate(found, axis=0), u, HEAD_DIM)
            return carry

        lax.fori_loop(0, pl.num_programs(0), finish, 0)


def whole_block(shape):
    zeros = (0,) * len(shape)
    return pl.BlockSpec(tuple(shape), lambda t, *refs: zeros)


def tile_block(shape, axis):
    def place(t, *refs):
        return tuple(t if i == axis else 0 for i in range(len(shape)))

    return pl.BlockSpec(tuple(shape), place)


def attention_meta(positions, seq_lengths, chunk):
    tiles, tile = positions.shape
    count = tiles * tile // chunk
    per = tile // chunk
    opening = opening_of(positions, seq_lengths)
    frequency = 10000.0 ** (-2.0 * jnp.arange(ROT // 2, dtype=F32) / ROT)
    angles = (positions - opening).astype(F32).reshape(count, 1, chunk) * frequency[None, :, None]
    ends = jnp.arange(tiles, dtype=jnp.int32) * tile
    first_open = opening_of(ends, seq_lengths)
    last_open = opening_of(ends + tile - 1, seq_lengths)
    own = jnp.arange(tiles, dtype=jnp.int32) * per
    low = (first_open // tile) * per
    middle = jnp.minimum(((last_open + tile - 1) // tile) * per, own)
    return dict(
        low=low.astype(jnp.int32),
        middle=middle.astype(jnp.int32),
        cosine=jnp.cos(angles),
        sine=jnp.sin(angles),
        query_pos=positions.reshape(count, 1, chunk),
        query_lo=opening.reshape(count, 1, chunk),
        key_pos=positions.reshape(count, chunk, 1),
    )


def attention_forward(parts, meta):
    sources = len(parts)
    slots, rows, width = parts[0].shape
    tile = sources * slots * GROUP
    tiles = rows // GROUP
    count, _, chunk = meta["query_pos"].shape
    per = tile // chunk
    nat = jax.ShapeDtypeStruct((count, chunk, HEAD_DIM), BF16)
    turned = jax.ShapeDtypeStruct((count, HEAD_DIM, chunk), BF16)
    out = jax.ShapeDtypeStruct((slots, rows, HEAD_DIM), BF16)
    found = pl.pallas_call(
        lambda *refs: forward_kernel(sources, *refs),
        out_shape=[out] * sources
        + [
            jax.ShapeDtypeStruct((count, HEAD_DIM, chunk), F32),
            jax.ShapeDtypeStruct((count, 1, chunk), F32),
            nat, nat, nat, turned, turned,
        ],
        grid_spec=pltpu.PrefetchScalarGridSpec(
            num_scalar_prefetch=2,
            grid=(tiles,),
            in_specs=[tile_block((slots, GROUP, width), 1)] * sources
            + [
                tile_block((per, 1, chunk), 0),
                tile_block((per, 1, chunk), 0),
                whole_block((count, chunk, 1)),
            ],
            out_specs=[tile_block((slots, GROUP, HEAD_DIM), 1)] * sources
            + [
                tile_block((per, HEAD_DIM, chunk), 0),
                tile_block((per, 1, chunk), 0),
                whole_block(nat.shape),
                whole_block(nat.shape),
                whole_block(nat.shape),
                whole_block(turned.shape),
                whole_block(turned.shape),
            ],
            scratch_shapes=[pltpu.VMEM(turned.shape, BF16)],
        ),
        compiler_params=pltpu.CompilerParams(
            dimension_semantics=("arbitrary",), vmem_limit_bytes=58 * 1024 * 1024
        ),
        cost_estimate=pl.CostEstimate(
            flops=20_000_000_000, bytes_accessed=12_000_000, transcendentals=6_000_000
        ),
        name="attention_forward",
    )(
        meta["low"], meta["middle"], *parts,
        meta["query_pos"], meta["query_lo"], meta["key_pos"],
    )
    return found[:sources], found[sources:]


def attention_backward(grads, meta, saved):
    sources = len(grads)
    slots, rows, _ = grads[0].shape
    tile = sources * slots * GROUP
    tiles = rows // GROUP
    count, _, chunk = meta["query_pos"].shape
    per = tile // chunk
    half = ROT // 2
    out = jax.ShapeDtypeStruct((slots, rows, 3 * HEAD_DIM), BF16)
    ot, lse, q, k, v, qt, kt = saved
    return pl.pallas_call(
        lambda *refs: backward_kernel(sources, *refs),
        out_shape=[out] * sources,
        grid_spec=pltpu.PrefetchScalarGridSpec(
            num_scalar_prefetch=2,
            grid=(tiles,),
            in_specs=[tile_block((slots, GROUP, HEAD_DIM), 1)] * sources
            + [
                whole_block((count, half, chunk)),
                whole_block((count, half, chunk)),
                tile_block((per, 1, chunk), 0),
                tile_block((per, 1, chunk), 0),
                whole_block((count, chunk, 1)),
                tile_block((per, HEAD_DIM, chunk), 0),
                tile_block((per, 1, chunk), 0),
                whole_block(q.shape),
                whole_block(k.shape),
                whole_block(v.shape),
                whole_block(qt.shape),
                whole_block(kt.shape),
            ],
            out_specs=[whole_block(out.shape)] * sources,
            scratch_shapes=[
                pltpu.VMEM((count, chunk, HEAD_DIM), F32),
                pltpu.VMEM((count, chunk, HEAD_DIM), F32),
            ],
        ),
        compiler_params=pltpu.CompilerParams(
            dimension_semantics=("arbitrary",), vmem_limit_bytes=62 * 1024 * 1024
        ),
        cost_estimate=pl.CostEstimate(
            flops=20_000_000_000, bytes_accessed=12_000_000, transcendentals=6_000_000
        ),
        name="attention_backward",
    )(
        meta["low"], meta["middle"], *grads, meta["cosine"], meta["sine"],
        meta["query_pos"], meta["query_lo"], meta["key_pos"], ot, lse, q, k, v, qt, kt,
    )


def gather_rows(rows, pieces, count, own):
    if not own:
        return lax.all_gather(rows, "blk", axis=0, tiled=False)
    found = []
    for (begin, end), order in pieces:
        held = rows[begin:end][None]
        for mask in order:
            held = jnp.concatenate([held, swap(held, mask, count)], axis=0)
        found.append(held)
    return jnp.concatenate(found, axis=1)


def reduce_rows(product, pieces, count, own):
    if not own:
        total = product(slice(None), slice(None)).astype(BF16)
        return lax.psum_scatter(total, "blk", scatter_dimension=0, tiled=False).astype(F32)
    found = []
    for (begin, end), order in pieces:
        middle = (1 << len(order)) // 2
        here = slice(begin, end)
        sent = product(slice(middle, None), here).astype(BF16)
        kept = product(slice(0, middle), here).astype(BF16)
        for mask in order[::-1][:-1]:
            total = kept.astype(F32) + swap(sent, mask, count).astype(F32)
            middle = middle // 2
            sent, kept = total[middle:].astype(BF16), total[:middle].astype(BF16)
        total = kept.astype(F32) + swap(sent, order[0], count).astype(F32)
        found.append(total[0])
    return jnp.concatenate(found, axis=0)


def gather_small(block, stages, count):
    for masks in stages:
        block = jnp.stack([block if m == 0 else swap(block, m, count) for m in masks])
    return block.reshape((-1,) + block.shape[len(stages) :])


def reduce_small(block, stages, count):
    for masks in stages[::-1]:
        block = block.reshape((len(masks), -1) + block.shape[1:])
        total = block[0]
        for i, m in enumerate(masks):
            if m:
                total = total + swap(block[i], m, count)
        block = total
    return block[0]


def exchange(parts, masks, count):
    return [part if m == 0 else swap(part, m, count) for part, m in zip(parts, masks)]


def gather_heads(block, masks, count):
    held = block[None]
    step = 1
    while step < len(masks):
        held = jnp.concatenate([held, swap(held, masks[step], count)], axis=0)
        step *= 2
    return held


def reduce_heads(product, masks, count):
    half = len(masks) // 2
    sent = product(range(half, 2 * half)).astype(BF16)
    total = product(range(half)) + swap(sent, masks[half], count).astype(F32)
    while half > 1:
        half //= 2
        sent = total[half:].astype(BF16)
        total = total[:half] + swap(sent, masks[half], count).astype(F32)
    return total[0]


def gelu_tanh(values):
    return jax.nn.gelu(values, approximate=True)


def gelu_back(hidden, act_grad):
    _, pullback = jax.vjp(gelu_tanh, hidden)
    return pullback(act_grad)[0]


def per_device(
    layer_in, out_grad, norm_gain, norm_bias, w_qkv, b_qkv, w_out, b_out, w_up, b_up,
    w_down, b_down, seq_lengths, token_place,
):
    heads, blks = lax.axis_size("head"), lax.axis_size("blk")
    count = heads * blks
    my_head, my_blk = lax.axis_index("head"), lax.axis_index("blk")
    me = my_head * blks + my_blk
    rows, width = layer_in.shape
    features = w_qkv.shape[1]
    units = w_up.shape[0]
    owners = HEAD_DIM // features
    member = me % owners
    own_gather = OWN_GATHER
    own_reduce = OWN_REDUCE
    relative = own_gather or own_reduce
    pieces = pieces_of(blks, rows, relative)
    head_bits = [blks << i for i in range(heads.bit_length() - 1)][::-1]
    head_masks = slot_masks(head_bits)
    stages = [list(range(blks)), [r * blks for r in range(heads)]]
    numbers = jnp.arange(count, dtype=jnp.int32)

    place = token_place.reshape(count, rows)
    ranks = place // count
    row_numbers = jnp.arange(rows, dtype=jnp.int32)
    own_ranks = lax.dynamic_slice_in_dim(ranks, me, 1, 0)
    order_hot = (own_ranks == row_numbers[:, None]).astype(BF16)
    x_sorted = dot_nn(order_hot, layer_in).astype(BF16)
    g_sorted = dot_nn(order_hot, out_grad).astype(BF16)
    x_all = gather_rows(x_sorted, pieces, count, own_gather).reshape(blks * rows, width)
    g_all = gather_rows(g_sorted, pieces, count, own_gather).reshape(blks * rows, width)

    vectors = jnp.stack([norm_gain, norm_bias, b_out, b_down])
    vectors = gather_small(vectors, stages, count)
    absolute = me ^ numbers
    choose = (absolute[None, :] == numbers[:, None]).astype(BF16)
    vectors = dot_nn(choose, vectors.reshape(count, -1)).reshape(count, 4, -1)
    vectors = jnp.transpose(vectors, (1, 0, 2)).reshape(4, width)
    gain, offset, out_bias, down_bias = (vectors[i][None] for i in range(4))

    qkv_full, out_full = w_qkv, w_out
    bias_full = b_qkv
    if owners > 1:
        order = member ^ jnp.arange(owners, dtype=jnp.int32)

        def of_owners(block):
            found = [block] + [swap(block, e, count) for e in range(1, owners)]
            return jnp.stack(found)[order]

        qkv_full = jnp.moveaxis(of_owners(w_qkv), 0, 1).reshape(3, HEAD_DIM, width)
        bias_full = jnp.moveaxis(of_owners(b_qkv), 0, 1).reshape(3, HEAD_DIM)
        out_full = of_owners(w_out).reshape(HEAD_DIM, width)
    qkv_heads = gather_heads(qkv_full.reshape(3 * HEAD_DIM, width), head_masks, count)
    up_heads = gather_heads(w_up, head_masks, count).reshape(heads * units, width)
    out_heads = gather_heads(out_full, head_masks, count)
    down_heads = gather_heads(w_down, head_masks, count).reshape(heads * units, width)
    biases = gather_heads(jnp.concatenate([bias_full.reshape(-1), b_up]), head_masks, count)
    qkv_heads = qkv_heads.reshape(heads, 3, HEAD_DIM, width)
    qkv_rows = jnp.swapaxes(qkv_heads, 0, 1).reshape(3 * heads * HEAD_DIM, width)
    qkv_bias = biases[:, : 3 * HEAD_DIM].reshape(heads, 3, HEAD_DIM).astype(F32)
    qkv_bias = jnp.swapaxes(qkv_bias, 0, 1).reshape(1, -1)
    up_bias = biases[:, 3 * HEAD_DIM :].reshape(1, -1).astype(F32)

    sorted_place = jnp.sum(
        jnp.where(ranks[:, None, :] == row_numbers[None, :, None], place[:, None, :], 0), axis=2
    )
    found = []
    for (begin, end), order in pieces:
        masks = jnp.array(slot_masks(order), dtype=jnp.int32)
        slot_blk = (my_blk ^ masks) if relative else jnp.arange(blks, dtype=jnp.int32)
        slot_head = my_head ^ jnp.array([m // blks for m in head_masks], dtype=jnp.int32)
        device = (slot_head[:, None] * blks + slot_blk[None, :]).reshape(-1)
        part = sorted_place[:, begin:end]
        chosen = jnp.where((device[:, None] == numbers[None, :])[:, :, None], part[None], 0)
        found.append(jnp.sum(chosen, axis=1))
    positions = jnp.concatenate(found, axis=1)
    own_positions = positions[:blks].reshape(-1)
    own_place = own_positions - opening_of(own_positions, seq_lengths)
    tiles = rows // GROUP
    positions = jnp.transpose(positions.reshape(count, tiles, GROUP), (1, 0, 2))
    positions = positions.reshape(tiles, count * GROUP)
    meta = attention_meta(positions, seq_lengths, min(CHUNK, count * GROUP))

    def normalize(values):
        values = values.astype(F32)
        center = jnp.mean(values, axis=-1, keepdims=True)
        centered = values - center
        variance = jnp.mean(centered * centered, axis=-1, keepdims=True)
        inverse = lax.rsqrt(variance + 1e-05)
        return centered * inverse, inverse

    normed = (normalize(x_all)[0] * gain + offset).astype(BF16)
    qkv = prepare(dot_nt(normed, qkv_rows), qkv_bias, own_place, heads)
    qkv = [qkv[r].reshape(blks, rows, 3 * HEAD_DIM) for r in range(heads)]
    attended, saved = attention_forward(exchange(qkv, head_masks, count), meta)
    attended = exchange(attended, head_masks, count)
    hidden = dot_nt(normed, up_heads) + up_bias
    active = gelu_tanh(hidden).astype(BF16)

    def own_features(parts, kinds):
        if owners == 1:
            return jnp.concatenate(parts, axis=2)
        found = []
        for part in parts:
            split = part.reshape(blks, rows, kinds, owners, features)
            found.append(lax.dynamic_index_in_dim(split, member, 3, False).reshape(blks, rows, -1))
        return jnp.concatenate(found, axis=2)

    att = own_features(attended, 1)
    out_own = out_heads if owners == 1 else gather_heads(w_out, head_masks, count)
    out_own = out_own.reshape(heads * features, width)
    act = active.reshape(blks, rows, heads * units)

    def flat(block):
        return block.reshape(-1, block.shape[-1])

    def mixed_part(slots, here):
        total = dot_nn(flat(att[slots, here]), out_own)
        total = total + dot_nn(flat(act[slots, here]), down_heads)
        return total.reshape(-1, (rows if here == slice(None) else here.stop - here.start), width)

    mixed = reduce_rows(mixed_part, pieces, count, own_reduce)

    heads_grad = dot_nt(g_all, out_heads.reshape(heads * HEAD_DIM, width)).astype(BF16)
    heads_grad = [
        heads_grad[:, r * HEAD_DIM : (r + 1) * HEAD_DIM].reshape(blks, rows, HEAD_DIM)
        for r in range(heads)
    ]
    qkv_grad = attention_backward(exchange(heads_grad, head_masks, count), meta, saved)
    qkv_grad = own_features(exchange(qkv_grad, head_masks, count), 3)
    hidden_grad = gelu_back(hidden, dot_nt(g_all, down_heads)).astype(BF16)
    hid_grad = hidden_grad.reshape(blks, rows, heads * units)
    qkv_own = qkv_heads if owners == 1 else gather_heads(w_qkv, head_masks, count)
    qkv_own = qkv_own.reshape(heads * 3 * features, width)

    def normed_part(slots, here):
        total = dot_nn(flat(qkv_grad[slots, here]), qkv_own)
        total = total + dot_nn(flat(hid_grad[slots, here]), up_heads)
        return total.reshape(-1, (rows if here == slice(None) else here.stop - here.start), width)

    normed_grad = reduce_rows(normed_part, pieces, count, own_reduce)

    def weight_grads(left, right, per_owner):
        def product(which):
            split = left.reshape(-1, heads, per_owner)
            chosen = jnp.concatenate([split[:, o] for o in which], axis=1)
            return dot_tn(chosen, right).reshape(len(which), per_owner, width)

        return reduce_heads(product, head_masks, count)

    w_down_grad = weight_grads(active, g_all, units)
    w_out_grad = weight_grads(flat(att), g_all, features)
    w_up_grad = weight_grads(hidden_grad, normed, units)
    w_qkv_grad = weight_grads(flat(qkv_grad), normed, 3 * features)
    b_parts = jnp.concatenate(
        [
            jnp.sum(flat(qkv_grad).astype(F32), axis=0).reshape(heads, -1),
            jnp.sum(hidden_grad.astype(F32), axis=0).reshape(heads, -1),
        ],
        axis=1,
    )
    b_grads = sum(exchange([b_parts[r] for r in range(heads)], head_masks, count))

    own_x = x_sorted.astype(F32)
    layer_out = (own_x + mixed + out_bias + down_bias).astype(BF16)
    layer_out = dot_tn(order_hot, layer_out).astype(BF16)
    x_hat, inverse = normalize(x_sorted)
    e = normed_grad * gain
    input_part = inverse * (
        e
        - jnp.mean(e, axis=-1, keepdims=True)
        - x_hat * jnp.mean(e * x_hat, axis=-1, keepdims=True)
    )
    input_grad = (g_sorted.astype(F32) + input_part).astype(BF16)
    input_grad = dot_tn(order_hot, input_grad).astype(BF16)
    sums = jnp.stack(
        [
            jnp.sum(normed_grad * x_hat, axis=0),
            jnp.sum(normed_grad, axis=0),
            jnp.sum(g_sorted.astype(F32), axis=0),
        ]
    )
    chosen = (absolute[:, None] == numbers[None, :]).astype(F32)
    sums = lax.dot_general(
        chosen,
        jnp.transpose(sums.reshape(3, count, -1), (1, 0, 2)).reshape(count, -1),
        (((1,), (0,)), ((), ())),
        precision=lax.Precision.HIGHEST,
        preferred_element_type=F32,
    ).reshape(count, 3, -1)
    sums = reduce_small(sums, stages, count)
    return (
        layer_out,
        input_grad,
        sums[0],
        sums[1],
        w_qkv_grad.reshape(3, features, width),
        b_grads[: 3 * features].reshape(3, features),
        w_out_grad,
        sums[2],
        w_up_grad,
        b_grads[3 * features :],
        w_down_grad,
        sums[2],
    )


def solution(mesh):
    rows, vector = P(AXES, None), P(AXES)
    qkv, qkv_bias = P(None, AXES, None), P(None, AXES)
    in_specs = (
        rows, rows, vector, vector, qkv, qkv_bias, rows, vector, rows, vector, rows, vector,
        P(), P(),
    )
    out_specs = (
        rows, rows, vector, vector, qkv, qkv_bias, rows, vector, rows, vector, rows, vector,
    )
    return jax.shard_map(
        per_device, mesh=mesh, in_specs=in_specs, out_specs=out_specs, check_vma=False
    )
```

```python
import jax
import jax.numpy as jnp
from jax import lax
from jax.experimental import pallas as pl
from jax.experimental.pallas import tpu as pltpu
from jax.sharding import PartitionSpec as P

HEAD_DIM = 64
ROT = 32
AXES = ("head", "blk")
GROUP = 16
CHUNK = 512
NEG = -1e30
F32 = jnp.float32
BF16 = jnp.bfloat16
SMALL = pl.CostEstimate(flops=1, bytes_accessed=1, transcendentals=0)
MIDDLE = pl.CostEstimate(flops=5_000_000_000, bytes_accessed=1_000_000, transcendentals=0)
BROAD = pl.CostEstimate(flops=34_000_000_000, bytes_accessed=1_000_000, transcendentals=0)
LARGE = pl.CostEstimate(flops=120_000_000_000, bytes_accessed=1_000_000, transcendentals=0)


def swap(block, mask, count):
    return lax.ppermute(block, AXES, [(i, i ^ mask) for i in range(count)])


def dot_nn(a, b):
    return lax.dot_general(a, b, (((1,), (0,)), ((), ())), preferred_element_type=F32)


def dot_nt(a, b):
    return lax.dot_general(a, b, (((1,), (1,)), ((), ())), preferred_element_type=F32)


def dot_tn(a, b):
    return lax.dot_general(a, b, (((0,), (0,)), ((), ())), preferred_element_type=F32)


def opening_of(packed, lengths):
    starts = jnp.cumsum(lengths) - lengths
    inside = packed[..., None] >= starts
    return jnp.max(jnp.where(inside, starts, 0), axis=-1)


def pieces_of(blks, rows):
    bits = [1 << i for i in range(blks.bit_length() - 1)]
    half = rows // 2
    return [((0, half), bits), ((half, rows), bits[1:-1] + bits[:1] + bits[-1:])]


def slot_masks(order):
    masks = [0]
    for mask in order:
        masks = masks + [m ^ mask for m in masks]
    return masks


def after_kernel(*refs):
    pass


def after(value, *others):
    anywhere = pl.BlockSpec(memory_space=pl.ANY)
    return pl.pallas_call(
        after_kernel,
        out_shape=jax.ShapeDtypeStruct(value.shape, value.dtype),
        in_specs=[anywhere] * (1 + len(others)),
        out_specs=anywhere,
        input_output_aliases={0: 0},
        compiler_params=pltpu.CompilerParams(vmem_limit_bytes=60 * 1024 * 1024),
        cost_estimate=SMALL,
        name="after",
    )(value, *others)


def whole_block(shape):
    zeros = (0,) * len(shape)
    return pl.BlockSpec(tuple(shape), lambda t, *refs: zeros)


def tile_block(shape, axis):
    def place(t, *refs):
        return tuple(t if i == axis else 0 for i in range(len(shape)))

    return pl.BlockSpec(tuple(shape), place)


def kernel_params(megabytes):
    return pltpu.CompilerParams(
        dimension_semantics=("arbitrary",), vmem_limit_bytes=megabytes * 1024 * 1024
    )


def join_kernel(plans, count, *refs):
    blocks, out_refs = refs[:count], refs[count + 1 :]
    for plan, out_ref in zip(plans, out_refs):
        for which, start, size, to in plan:
            out_ref[to : to + size] = blocks[which][start : start + size]


def join(blocks, plans, token):
    width = blocks[0].shape[1]
    shapes = [(sum(size for _, _, size, _ in plan), width) for plan in plans]
    return pl.pallas_call(
        lambda *refs: join_kernel(plans, len(blocks), *refs),
        out_shape=[jax.ShapeDtypeStruct(shape, BF16) for shape in shapes],
        grid=(1,),
        in_specs=[whole_block(b.shape) for b in blocks] + [pl.BlockSpec(memory_space=pl.ANY)],
        out_specs=[whole_block(shape) for shape in shapes],
        compiler_params=kernel_params(56),
        cost_estimate=SMALL,
        name="join",
    )(*blocks, token)


def rotary_kernel(heads, z_ref, bias_ref, cos_ref, up_ref, down_ref, *out_refs):
    lanes = cos_ref.shape[3]
    half = ROT // 2
    span = heads * lanes
    values = []
    for side in range(2):
        z = z_ref[side, 0] + bias_ref[...]
        for r in range(heads):
            u = z[:, r * lanes : (r + 1) * lanes]
            u = (
                u * cos_ref[side, 0]
                + pltpu.roll(u, lanes - half, 1) * up_ref[side, 0]
                + pltpu.roll(u, half, 1) * down_ref[side, 0]
            )
            out_refs[r][0, side] = u.astype(BF16)
        values.append(z[:, span:])
    for r in range(heads):
        at = slice(r * HEAD_DIM, (r + 1) * HEAD_DIM)
        both = jnp.concatenate([values[0][:, at], values[1][:, at]], axis=1)
        out_refs[r][0, 2] = both.astype(BF16)


def rotary(z, bias, place, heads, blks):
    rows, width = z.shape
    lanes = 2 * HEAD_DIM
    size = rows // blks
    lane = jnp.arange(lanes, dtype=jnp.int32) % HEAD_DIM
    half = ROT // 2
    frequency = 10000.0 ** (-2.0 * (lane % half).astype(F32) / ROT)
    angles = place.astype(F32)[:, None] * frequency[None, :]
    cosine = jnp.where(lane < ROT, jnp.cos(angles), 1.0)
    sine = jnp.sin(angles)
    up = jnp.where(lane < half, -sine, 0.0)
    down = jnp.where((lane >= half) & (lane < ROT), sine, 0.0)
    shape = (2, blks // 2, size)
    table = tile_block((2, 1, size, lanes), 1)
    return pl.pallas_call(
        lambda *refs: rotary_kernel(heads, *refs),
        out_shape=[jax.ShapeDtypeStruct((blks // 2, 3, size, lanes), BF16)] * heads,
        grid=(blks // 2,),
        in_specs=[tile_block((2, 1, size, width), 1), whole_block((1, width)), table, table, table],
        out_specs=[tile_block((1, 3, size, lanes), 0)] * heads,
        compiler_params=kernel_params(32),
        cost_estimate=LARGE,
        name="rotary",
    )(
        z.reshape(shape + (width,)), bias,
        *[t.reshape(shape + (lanes,)) for t in (cosine, up, down)],
    )


def mixed_kernel(heads, *refs):
    act_ref, down_ref, out_w_ref = refs[:3]
    att_refs, out_ref, left_ref = refs[3 : 3 + heads], refs[-2], refs[-1]

    @pl.when(pl.program_id(0) == 0)
    def _():
        parts = [pair_rows(a[...]) for a in att_refs]
        left_ref[...] = jnp.concatenate(parts, axis=1)

    total = dot_nn(act_ref[...], down_ref[...]) + dot_nn(left_ref[...], out_w_ref[...])
    out_ref[...] = total.astype(BF16)


def mixed_rows(active, attended, down_rows, out_rows):
    heads = len(attended)
    rows, span = active.shape
    width = down_rows.shape[1]
    block = 512
    return pl.pallas_call(
        lambda *refs: mixed_kernel(heads, *refs),
        out_shape=jax.ShapeDtypeStruct((rows, width), BF16),
        grid=(width // block,),
        in_specs=[
            whole_block(active.shape),
            tile_block((span, block), 1),
            tile_block((out_rows.shape[0], block), 1),
        ]
        + [whole_block(a.shape) for a in attended],
        out_specs=tile_block((rows, block), 1),
        scratch_shapes=[pltpu.VMEM((rows, heads * HEAD_DIM), BF16)],
        compiler_params=kernel_params(58),
        cost_estimate=SMALL,
        name="mixed",
    )(active, down_rows, out_rows, *attended)


GELU_ROOT = 0.7978845608028654
GELU_CUBE = 0.044715


def hidden_grad_kernel(g_ref, hidden_ref, down_ref, token_ref, grad_ref, sum_ref):
    h = hidden_ref[...]
    square = h * h
    bent = jnp.tanh(GELU_ROOT * (h + GELU_CUBE * (square * h)))
    slope = 0.5 * (1.0 + bent) + (0.5 * GELU_ROOT) * h * (1.0 - bent * bent) * (
        1.0 + (3.0 * GELU_CUBE) * square
    )
    grad = (dot_nt(g_ref[...], down_ref[...]) * slope).astype(BF16)
    grad_ref[...] = grad
    sum_ref[...] = jnp.sum(grad.astype(F32), axis=0, keepdims=True)


def hidden_grads(g_all, hidden, down_rows, token):
    rows, width = g_all.shape
    span = hidden.shape[1]
    block = min(256, span)
    size = min(1024, rows)
    found = pl.pallas_call(
        hidden_grad_kernel,
        out_shape=[
            jax.ShapeDtypeStruct((rows, span), BF16),
            jax.ShapeDtypeStruct((rows // size, 1, span), F32),
        ],
        grid=(rows // size, span // block),
        in_specs=[
            pl.BlockSpec((size, width), lambda i, j: (i, 0)),
            pl.BlockSpec((size, block), lambda i, j: (i, j)),
            pl.BlockSpec((block, width), lambda i, j: (j, 0)),
            pl.BlockSpec(memory_space=pl.ANY),
        ],
        out_specs=[
            pl.BlockSpec((size, block), lambda i, j: (i, j)),
            pl.BlockSpec((None, 1, block), lambda i, j: (i, 0, j)),
        ],
        compiler_params=pltpu.CompilerParams(
            dimension_semantics=("arbitrary", "arbitrary"), vmem_limit_bytes=48 * 1024 * 1024
        ),
        cost_estimate=SMALL,
        name="hidden_grad",
    )(g_all, hidden, down_rows, token)
    return found[0], jnp.sum(found[1], axis=(0, 1))


def shifted_kernel(heads, parts, slots_ref, *refs):
    hid_ref, up_ref, w_ref = refs[:3]
    qkv_refs, out_refs, left_ref = refs[3 : 3 + heads], refs[4 + heads : -1], refs[-1]
    half, _, _, lanes = qkv_refs[0].shape
    units = hid_ref.shape[2]
    span = units + heads * lanes

    @pl.when(pl.program_id(0) == 0)
    def _():
        at, number = 0, 0
        for count, begin, end in parts:
            for i in range(count):
                slot = slots_ref[number]
                number += 1
                side = slot // half
                group = slot - side * half
                rows = slice(at, at + end - begin)
                at += end - begin
                left_ref[rows, :units] = hid_ref[slot, begin:end, :]
                values = []
                for r in range(heads):
                    to = units + r * lanes
                    left_ref[rows, to : to + lanes] = qkv_refs[r][group, side, begin:end, :]
                    both = qkv_refs[r][group, 2, begin:end, :]
                    values.append(jnp.where(side == 0, both[:, :HEAD_DIM], both[:, HEAD_DIM:]))
                left_ref[rows, span:] = jnp.concatenate(values, axis=1)

    total = dot_nn(left_ref[:, :units], up_ref[...]) + dot_nn(left_ref[:, units:], w_ref[...])
    at = 0
    for out_ref, (count, begin, end) in zip(out_refs, parts):
        size = count * (end - begin)
        out_ref[...] = total[at : at + size].astype(BF16).reshape(out_ref.shape)
        at += size


def shifted(hid_grad, qkv_grad, up_rows, w_rows, slots, parts, token):
    heads = len(qkv_grad)
    width = up_rows.shape[1]
    total_rows = sum(n * (end - begin) for n, begin, end in parts)
    depth = up_rows.shape[0] + w_rows.shape[0]
    block = 512
    return pl.pallas_call(
        lambda *refs: shifted_kernel(heads, parts, *refs),
        out_shape=[jax.ShapeDtypeStruct((n, end - begin, width), BF16) for n, begin, end in parts],
        grid_spec=pltpu.PrefetchScalarGridSpec(
            num_scalar_prefetch=1,
            grid=(width // block,),
            in_specs=[
                whole_block(hid_grad.shape),
                tile_block((up_rows.shape[0], block), 1),
                tile_block((w_rows.shape[0], block), 1),
            ]
            + [whole_block(q.shape) for q in qkv_grad]
            + [pl.BlockSpec(memory_space=pl.ANY)],
            out_specs=[tile_block((n, end - begin, block), 2) for n, begin, end in parts],
            scratch_shapes=[pltpu.VMEM((total_rows, depth), BF16)],
        ),
        compiler_params=kernel_params(60),
        cost_estimate=MIDDLE,
        name="shifted",
    )(slots, hid_grad, up_rows, w_rows, *qkv_grad, token)


def turn_left(left_ref, owners_of, units, second_ref, first_refs):
    low, high = owners_of[0] * units, (owners_of[-1] + 1) * units
    left_ref[: high - low, :] = second_ref[:, low:high].T
    at = high - low
    cols = left_ref.shape[1] // 2
    for ref in first_refs:
        if len(ref.shape) == 4:
            half, _, rows, lanes = ref.shape
            for side in range(2):
                block = ref[:, side].reshape(half * rows, lanes).T
                left_ref[at : at + lanes, side * cols : (side + 1) * cols] = block
            at += lanes
            pair = ref[:, 2].reshape(half * rows, lanes).T
        else:
            half, rows, lanes = ref.shape
            pair = ref[...].reshape(half * rows, lanes).T
        left_ref[at : at + HEAD_DIM, :cols] = pair[:HEAD_DIM]
        left_ref[at : at + HEAD_DIM, cols:] = pair[HEAD_DIM:]
        at += HEAD_DIM


def outer_kernel(owners_of, units, *refs):
    second_ref, right_ref = refs[:2]
    first_refs, out_ref, left_ref = refs[2:-3], refs[-2], refs[-1]

    @pl.when(pl.program_id(0) == 0)
    def _():
        turn_left(left_ref, owners_of, units, second_ref, first_refs)

    out_ref[...] = dot_nn(left_ref[...], right_ref[...]).astype(BF16)


def outer_add_kernel(owners_of, units, *refs):
    second_ref, right_ref, there_ref = refs[:3]
    first_refs, own_ref, sent_ref, left_ref = refs[3:-4], refs[-3], refs[-2], refs[-1]

    @pl.when(pl.program_id(0) == 0)
    def _():
        turn_left(left_ref, owners_of, units, second_ref, first_refs)

    total = dot_nn(left_ref[...], right_ref[...]) + there_ref[...].astype(F32)
    span = len(owners_of) * units
    cut = (total.shape[0] - span) // len(owners_of)
    own = len(owners_of) // 2
    low, high = own * units, span + own * cut
    own_ref[...] = jnp.concatenate([total[:low], total[span:high]], axis=0)
    sent_ref[...] = jnp.concatenate([total[low:span], total[high:]], axis=0).astype(BF16)


def outer(firsts, second, right, owners_of, units, token, there=None):
    rows, width = right.shape
    chosen = [firsts[r] for r in owners_of]
    block = min(512, width)
    cut = 3 * HEAD_DIM if len(chosen[0].shape) == 4 else HEAD_DIM
    count = len(owners_of) * (units + cut)
    strip = tile_block((count, block), 1)
    operands, specs = [second, right], [whole_block(second.shape), tile_block((rows, block), 1)]
    if there is None:
        kernel, shapes = outer_kernel, jax.ShapeDtypeStruct((count, width), BF16)
        out_specs = strip
    else:
        kernel = outer_add_kernel
        shapes = [
            jax.ShapeDtypeStruct((count // 2, width), F32),
            jax.ShapeDtypeStruct((count // 2, width), BF16),
        ]
        out_specs = [tile_block((count // 2, block), 1)] * 2
        operands.append(there)
        specs.append(strip)
    return pl.pallas_call(
        lambda *refs: kernel(owners_of, units, *refs),
        out_shape=shapes,
        grid=(width // block,),
        in_specs=specs
        + [whole_block(f.shape) for f in chosen]
        + [pl.BlockSpec(memory_space=pl.ANY)],
        out_specs=out_specs,
        scratch_shapes=[pltpu.VMEM((count, rows), BF16)],
        compiler_params=kernel_params(58),
        cost_estimate=SMALL,
        name="outer",
    )(*operands, *chosen, token)


def sums_kernel(parts, slots_ref, *refs):
    x_ref, mean_ref, inverse_ref = refs[:3]
    part_refs, out_ref = refs[3:-1], refs[-1]
    number = 0
    gain_sum, bias_sum = 0.0, 0.0
    for ref, (count, begin, end) in zip(part_refs, parts):
        for i in range(count):
            slot = slots_ref[number]
            number += 1
            x_hat = x_ref[slot, begin:end, :].astype(F32) - mean_ref[slot, begin:end, :]
            x_hat = x_hat * inverse_ref[slot, begin:end, :]
            part = ref[i].astype(F32)
            gain_sum += jnp.sum(part * x_hat, axis=0, keepdims=True)
            bias_sum += jnp.sum(part, axis=0, keepdims=True)
    out_ref[0:1, :] = gain_sum
    out_ref[1:2, :] = bias_sum


def norm_sums(x_all, mean, inverse, blocks, slots, parts):
    blks, rows, width = x_all.shape
    block = 512
    return pl.pallas_call(
        lambda *refs: sums_kernel(parts, *refs),
        out_shape=jax.ShapeDtypeStruct((2, width), F32),
        grid_spec=pltpu.PrefetchScalarGridSpec(
            num_scalar_prefetch=1,
            grid=(width // block,),
            in_specs=[
                tile_block((blks, rows, block), 2),
                whole_block(mean.shape),
                whole_block(inverse.shape),
            ]
            + [tile_block(b.shape[:2] + (block,), 2) for b in blocks],
            out_specs=tile_block((2, block), 1),
        ),
        compiler_params=kernel_params(56),
        cost_estimate=SMALL,
        name="norm_sums",
    )(slots, x_all, mean, inverse, *blocks)


def total_kernel(own_ref, there_ref, token_ref, top_ref, low_ref):
    cut = top_ref.shape[0]
    total = own_ref[...] + there_ref[...].astype(F32)
    top_ref[...] = total[:cut]
    low_ref[...] = total[cut:]


def totals(own, there, cut, token):
    rows, width = own.shape
    block = 512
    return pl.pallas_call(
        total_kernel,
        out_shape=[
            jax.ShapeDtypeStruct((cut, width), F32),
            jax.ShapeDtypeStruct((rows - cut, width), F32),
        ],
        grid=(width // block,),
        in_specs=[tile_block((rows, block), 1)] * 2 + [pl.BlockSpec(memory_space=pl.ANY)],
        out_specs=[tile_block((cut, block), 1), tile_block((rows - cut, block), 1)],
        compiler_params=kernel_params(32),
        cost_estimate=SMALL,
        name="totals",
    )(own, there, token)


def layer_out_kernel(x_ref, mixed_ref, bias_ref, hot_ref, token_ref, out_ref):
    total = x_ref[...].astype(F32) + mixed_ref[...].astype(F32) + bias_ref[0:1] + bias_ref[1:2]
    out_ref[...] = dot_tn(hot_ref[...], total.astype(BF16)).astype(BF16)


def layer_rows(x, mixed, biases, hot, token):
    operands = (x, mixed, biases, hot)
    return pl.pallas_call(
        layer_out_kernel,
        out_shape=jax.ShapeDtypeStruct(x.shape, BF16),
        grid=(1,),
        in_specs=[whole_block(o.shape) for o in operands] + [pl.BlockSpec(memory_space=pl.ANY)],
        out_specs=whole_block(x.shape),
        compiler_params=kernel_params(32),
        cost_estimate=SMALL,
        name="layer_rows",
    )(*operands, token)


def input_grad_kernel(pieces, *refs):
    x_ref, g_ref, gain_ref, hot_ref = refs[:4]
    kept_refs, there_refs, out_ref = refs[4 : 4 + pieces], refs[4 + pieces : -1], refs[-1]
    grad = jnp.concatenate(
        [k[0] + t[0].astype(F32) for k, t in zip(kept_refs, there_refs)], axis=0
    )
    x = x_ref[...].astype(F32)
    centered = x - jnp.mean(x, axis=1, keepdims=True)
    inverse = lax.rsqrt(jnp.mean(centered * centered, axis=1, keepdims=True) + 1e-05)
    x_hat = centered * inverse
    e = grad * gain_ref[...]
    part = inverse * (
        e
        - jnp.mean(e, axis=1, keepdims=True)
        - x_hat * jnp.mean(e * x_hat, axis=1, keepdims=True)
    )
    total = (g_ref[...].astype(F32) + part).astype(BF16)
    out_ref[...] = dot_tn(hot_ref[...], total).astype(BF16)


def input_rows(x, g, gain, hot, kept, there):
    operands = (x, g, gain, hot, *kept, *there)
    return pl.pallas_call(
        lambda *refs: input_grad_kernel(len(kept), *refs),
        out_shape=jax.ShapeDtypeStruct(x.shape, BF16),
        grid=(1,),
        in_specs=[whole_block(o.shape) for o in operands],
        out_specs=whole_block(x.shape),
        compiler_params=kernel_params(32),
        cost_estimate=SMALL,
        name="input_rows",
    )(*operands)


def rope_t(u, cosine, sine):
    half = ROT // 2
    top, low = u[:half], u[half:ROT]
    return jnp.concatenate(
        [top * cosine - low * sine, low * cosine + top * sine, u[ROT:]], axis=0
    )


def tall(block):
    return block.reshape(block.shape[0] * block.shape[1], block.shape[2])


def pair_rows(block):
    both = tall(block)
    return jnp.concatenate([both[:, :HEAD_DIM], both[:, HEAD_DIM:]], axis=0)


def packed_rows(refs):
    qk, v = [], []
    for ref in refs:
        qk += [tall(ref[:, 0]), tall(ref[:, 1])]
        v.append(pair_rows(ref[:, 2]))
    return jnp.concatenate(qk, axis=0), jnp.concatenate(v, axis=0)


def side_by_side(block):
    middle = block.shape[0] // 2
    return jnp.concatenate([block[:middle], block[middle:]], axis=1)


def forward_kernel(sources, *refs):
    lo_ref, mid_ref = refs[:2]
    in_refs = refs[2 : 2 + sources]
    pq_ref, lq_ref, kp_ref = refs[2 + sources : 5 + sources]
    att_refs = refs[5 + sources : 5 + 2 * sources]
    ot_ref, lse_ref, q_ref, k_ref, v_ref, qt_ref, kt_ref, vt_ref = refs[5 + 2 * sources :]
    t = pl.program_id(0)
    chunk = q_ref.shape[1]
    qk, v = packed_rows(in_refs)
    per = v.shape[0] // chunk
    for c in range(per):
        index = t * per + c
        part, values = qk[c * chunk : (c + 1) * chunk], v[c * chunk : (c + 1) * chunk]
        q_ref[index] = part[:, :HEAD_DIM]
        k_ref[index] = part[:, HEAD_DIM:]
        v_ref[index] = values
        turned = part.astype(F32).T
        qt_ref[index] = (turned[:HEAD_DIM] * HEAD_DIM**-0.5).astype(BF16)
        kt_ref[index] = turned[HEAD_DIM:].astype(BF16)
        vt_ref[index] = values.astype(F32).T.astype(BF16)
    outs = []
    for c in range(per):
        qt = qt_ref[t * per + c]
        query_pos, query_lo = pq_ref[c], lq_ref[c]

        def step(kc, state, masked):
            run_max, run_sum, acc = state
            scores = dot_nn(k_ref[kc], qt)
            if masked:
                key_pos = kp_ref[kc]
                visible = (key_pos <= query_pos) & (key_pos >= query_lo)
                scores = jnp.where(visible, scores, NEG)
            new_max = jnp.maximum(run_max, jnp.max(scores, axis=0, keepdims=True))
            weights = jnp.exp(scores - new_max)
            if masked:
                weights = jnp.where(visible, weights, 0.0)
            rescale = jnp.exp(run_max - new_max)
            run_sum = run_sum * rescale + jnp.sum(weights, axis=0, keepdims=True)
            acc = acc * rescale + dot_nn(vt_ref[kc], weights.astype(BF16))
            return new_max, run_sum, acc

        state = (
            jnp.full((1, chunk), NEG, F32),
            jnp.zeros((1, chunk), F32),
            jnp.zeros((HEAD_DIM, chunk), F32),
        )
        state = lax.fori_loop(lo_ref[t], mid_ref[t], lambda i, s: step(i, s, True), state)
        state = lax.fori_loop(mid_ref[t], t * per, lambda i, s: step(i, s, False), state)
        state = lax.fori_loop(t * per, (t + 1) * per, lambda i, s: step(i, s, True), state)
        run_max, run_sum, acc = state
        out = acc / run_sum
        ot_ref[c] = out
        lse_ref[c] = run_max + jnp.log(run_sum)
        outs.append(out.T.astype(BF16))
    att = outs[0] if per == 1 else jnp.concatenate(outs, axis=0)
    span = att.shape[0] // sources
    for i, ref in enumerate(att_refs):
        ref[...] = side_by_side(att[i * span : (i + 1) * span]).reshape(ref.shape)


def backward_kernel(sources, *refs):
    lo_ref, mid_ref = refs[:2]
    g_refs = refs[2 : 2 + sources]
    cos_ref, sin_ref, pq_ref, lq_ref, kp_ref, ot_ref, lse_ref = refs[2 + sources : 9 + sources]
    q_ref, k_ref, v_ref, qt_ref, kt_ref = refs[9 + sources : 14 + sources]
    out_refs = refs[14 + sources : 14 + 2 * sources]
    sum_ref, dk_ref, dv_ref = refs[14 + 2 * sources :]
    t = pl.program_id(0)
    chunk = q_ref.shape[1]
    scaling = HEAD_DIM**-0.5
    grads = jnp.concatenate([pair_rows(ref[...]) for ref in g_refs], axis=0)
    per = grads.shape[0] // chunk
    for c in range(per):
        dk_ref[t * per + c] = jnp.zeros((chunk, HEAD_DIM), F32)
        dv_ref[t * per + c] = jnp.zeros((chunk, HEAD_DIM), F32)
    parts = []
    for c in range(per):
        index = t * per + c
        do = grads[c * chunk : (c + 1) * chunk]
        dot32 = do.astype(F32).T
        dot16 = dot32.astype(BF16)
        delta = jnp.sum(dot32 * ot_ref[c], axis=0, keepdims=True)
        lse = lse_ref[c]
        q, qt = q_ref[index], qt_ref[index]
        query_pos, query_lo = pq_ref[c], lq_ref[c]

        def step(kc, dqt, masked):
            probs = jnp.exp(dot_nn(k_ref[kc], qt) - lse)
            if masked:
                key_pos = kp_ref[kc]
                visible = (key_pos <= query_pos) & (key_pos >= query_lo)
                probs = jnp.where(visible, probs, 0.0)
            dv_ref[kc] += dot_nn(probs.astype(BF16), do)
            prob_grad = dot_nn(v_ref[kc], dot16)
            score_grad = (probs * (prob_grad - delta)).astype(BF16)
            dk_ref[kc] += dot_nn(score_grad, q)
            return dqt + dot_nn(kt_ref[kc], score_grad)

        dqt = jnp.zeros((HEAD_DIM, chunk), F32)
        dqt = lax.fori_loop(lo_ref[t], mid_ref[t], lambda i, s: step(i, s, True), dqt)
        dqt = lax.fori_loop(mid_ref[t], t * per, lambda i, s: step(i, s, False), dqt)
        dqt = lax.fori_loop(t * per, (t + 1) * per, lambda i, s: step(i, s, True), dqt)
        parts.append(rope_t(dqt * scaling, cos_ref[index], -sin_ref[index]).T)

    def store(block, u, first):
        span = block.shape[0] // sources
        here = pl.ds(pl.multiple_of(u * GROUP, GROUP), GROUP)
        block = block.astype(BF16)
        total = jnp.sum(block.astype(F32), axis=0, keepdims=True)
        if first:
            sum_ref[1:2, :] += total[:, :HEAD_DIM]
            sum_ref[2:3, :] += total[:, HEAD_DIM:]
        else:
            sum_ref[0:1, :] += total
        for i, ref in enumerate(out_refs):
            part = block[i * span : (i + 1) * span]
            half = ref.shape[0]
            shape = (half, GROUP, HEAD_DIM)
            for side in range(2):
                one = part[side * half * GROUP : (side + 1) * half * GROUP, :HEAD_DIM]
                ref[:, side, here, first : first + HEAD_DIM] = one.reshape(shape)
            if first:
                both = side_by_side(part[:, HEAD_DIM:])
                ref[:, 2, here, :] = both.reshape(half, GROUP, 2 * HEAD_DIM)

    @pl.when(t == 0)
    def _():
        sum_ref[...] = jnp.zeros_like(sum_ref)

    store(parts[0] if per == 1 else jnp.concatenate(parts, axis=0), t, 0)

    @pl.when(t == pl.num_programs(0) - 1)
    def _():
        def finish(u, carry):
            found = []
            for c in range(per):
                index = u * per + c
                dkt = rope_t(dk_ref[index].T * scaling, cos_ref[index], -sin_ref[index])
                found.append(jnp.concatenate([dkt.T, dv_ref[index]], axis=1))
            store(found[0] if per == 1 else jnp.concatenate(found, axis=0), u, HEAD_DIM)
            return carry

        lax.fori_loop(0, pl.num_programs(0), finish, 0)


def attention_meta(positions, seq_lengths, chunk):
    tiles, tile = positions.shape
    count = tiles * tile // chunk
    per = tile // chunk
    opening = opening_of(positions, seq_lengths)
    frequency = 10000.0 ** (-2.0 * jnp.arange(ROT // 2, dtype=F32) / ROT)
    angles = (positions - opening).astype(F32).reshape(count, 1, chunk) * frequency[None, :, None]
    ends = jnp.arange(tiles, dtype=jnp.int32) * tile
    first_open = opening_of(ends, seq_lengths)
    last_open = opening_of(ends + tile - 1, seq_lengths)
    own = jnp.arange(tiles, dtype=jnp.int32) * per
    low = (first_open // tile) * per
    middle = jnp.minimum(((last_open + tile - 1) // tile) * per, own)
    return dict(
        low=low.astype(jnp.int32),
        middle=middle.astype(jnp.int32),
        cosine=jnp.cos(angles),
        sine=jnp.sin(angles),
        query_pos=positions.reshape(count, 1, chunk),
        query_lo=opening.reshape(count, 1, chunk),
        key_pos=positions.reshape(count, chunk, 1),
    )


def attention_forward(parts, meta):
    sources = len(parts)
    half, _, rows, lanes = parts[0].shape
    tile = sources * 2 * half * GROUP
    tiles = rows // GROUP
    count, _, chunk = meta["query_pos"].shape
    per = tile // chunk
    nat = jax.ShapeDtypeStruct((count, chunk, HEAD_DIM), BF16)
    turned = jax.ShapeDtypeStruct((count, HEAD_DIM, chunk), BF16)
    out = jax.ShapeDtypeStruct((half, rows, lanes), BF16)
    found = pl.pallas_call(
        lambda *refs: forward_kernel(sources, *refs),
        out_shape=[out] * sources
        + [
            jax.ShapeDtypeStruct((count, HEAD_DIM, chunk), F32),
            jax.ShapeDtypeStruct((count, 1, chunk), F32),
            nat, nat, nat, turned, turned,
        ],
        grid_spec=pltpu.PrefetchScalarGridSpec(
            num_scalar_prefetch=2,
            grid=(tiles,),
            in_specs=[tile_block((half, 3, GROUP, lanes), 2)] * sources
            + [
                tile_block((per, 1, chunk), 0),
                tile_block((per, 1, chunk), 0),
                whole_block((count, chunk, 1)),
            ],
            out_specs=[tile_block((half, GROUP, lanes), 1)] * sources
            + [
                tile_block((per, HEAD_DIM, chunk), 0),
                tile_block((per, 1, chunk), 0),
                whole_block(nat.shape),
                whole_block(nat.shape),
                whole_block(nat.shape),
                whole_block(turned.shape),
                whole_block(turned.shape),
            ],
            scratch_shapes=[pltpu.VMEM(turned.shape, BF16)],
        ),
        compiler_params=pltpu.CompilerParams(
            dimension_semantics=("arbitrary",), vmem_limit_bytes=58 * 1024 * 1024
        ),
        cost_estimate=LARGE,
        name="attention_forward",
    )(
        meta["low"], meta["middle"], *parts,
        meta["query_pos"], meta["query_lo"], meta["key_pos"],
    )
    return found[:sources], found[sources:]


def attention_backward(grads, meta, saved):
    sources = len(grads)
    half, rows, lanes = grads[0].shape
    tile = sources * 2 * half * GROUP
    tiles = rows // GROUP
    count, _, chunk = meta["query_pos"].shape
    per = tile // chunk
    turn = ROT // 2
    out = jax.ShapeDtypeStruct((half, 3, rows, lanes), BF16)
    ot, lse, q, k, v, qt, kt = saved
    found = pl.pallas_call(
        lambda *refs: backward_kernel(sources, *refs),
        out_shape=[out] * sources + [jax.ShapeDtypeStruct((3, HEAD_DIM), F32)],
        grid_spec=pltpu.PrefetchScalarGridSpec(
            num_scalar_prefetch=2,
            grid=(tiles,),
            in_specs=[tile_block((half, GROUP, lanes), 1)] * sources
            + [
                whole_block((count, turn, chunk)),
                whole_block((count, turn, chunk)),
                tile_block((per, 1, chunk), 0),
                tile_block((per, 1, chunk), 0),
                whole_block((count, chunk, 1)),
                tile_block((per, HEAD_DIM, chunk), 0),
                tile_block((per, 1, chunk), 0),
                whole_block(q.shape),
                whole_block(k.shape),
                whole_block(v.shape),
                whole_block(qt.shape),
                whole_block(kt.shape),
            ],
            out_specs=[whole_block(out.shape)] * sources + [whole_block((3, HEAD_DIM))],
            scratch_shapes=[
                pltpu.VMEM((count, chunk, HEAD_DIM), F32),
                pltpu.VMEM((count, chunk, HEAD_DIM), F32),
            ],
        ),
        compiler_params=pltpu.CompilerParams(
            dimension_semantics=("arbitrary",), vmem_limit_bytes=62 * 1024 * 1024
        ),
        cost_estimate=BROAD,
        name="attention_backward",
    )(
        meta["low"], meta["middle"], *grads, meta["cosine"], meta["sine"],
        meta["query_pos"], meta["query_lo"], meta["key_pos"], ot, lse, q, k, v, qt, kt,
    )
    return list(found[:sources]), found[sources]


def doubled(block, masks, count):
    held = block[None]
    for mask in masks:
        held = jnp.concatenate([held, swap(held, mask, count)], axis=0)
    return held


def halved(block, masks, count):
    for mask in masks[::-1]:
        middle = block.shape[0] // 2
        block = block[:middle] + swap(block[middle:], mask, count)
    return block[0]


def gather_list(block, masks, count):
    held = [block]
    for mask in masks:
        held = held + [swap(h, mask, count) for h in held]
    return held


def exchange(parts, masks, count):
    return [part if m == 0 else swap(part, m, count) for part, m in zip(parts, masks)]


def pick(block, axis, index):
    return lax.dynamic_index_in_dim(block, index, axis, False)


def gelu_tanh(values):
    return jax.nn.gelu(values, approximate=True)


def hop_kernel(pieces, *refs):
    refs = refs[2 * pieces :]
    outs = refs[4 * pieces :]
    for i in range(pieces):
        a_ref, b_ref, c_ref, d_ref = refs[4 * i : 4 * i + 4]
        out_ref, own_ref = outs[2 * i : 2 * i + 2]
        out_ref[...] = (a_ref[...].astype(F32) + b_ref[...].astype(F32)).astype(BF16)
        own_ref[...] = c_ref[...].astype(F32) + d_ref[...].astype(F32)


def hop(kept, there, masks, left_bits, my_blk):
    pieces = len(kept)
    count, _, width = kept[0].shape
    picks, in_specs, out_specs, shapes, operands = [], [], [], [], []
    for i in range(pieces):
        numbers = jnp.arange(count, dtype=jnp.int32).reshape((2,) * len(left_bits[i]))
        axis = left_bits[i].index(masks[i])
        mine = (my_blk // masks[i]) % 2
        picks += [pick(numbers, axis, 1 - mine).reshape(-1), pick(numbers, axis, mine).reshape(-1)]
        rows = kept[i].shape[1]
        block = (1, rows, width)
        far = pl.BlockSpec(block, lambda t, *at, i=i: (at[2 * i][t], 0, 0))
        near = pl.BlockSpec(block, lambda t, *at, i=i: (at[2 * i + 1][t], 0, 0))
        in_specs += [far, far, near, near]
        operands += [kept[i], there[i], kept[i], there[i]]
        out_specs += [pl.BlockSpec(block, lambda t, *at: (t, 0, 0))] * 2
        shape = (count // 2, rows, width)
        shapes += [jax.ShapeDtypeStruct(shape, BF16), jax.ShapeDtypeStruct(shape, F32)]
    found = pl.pallas_call(
        lambda *refs: hop_kernel(pieces, *refs),
        out_shape=shapes,
        grid_spec=pltpu.PrefetchScalarGridSpec(
            num_scalar_prefetch=2 * pieces,
            grid=(count // 2,),
            in_specs=in_specs,
            out_specs=out_specs,
        ),
        compiler_params=kernel_params(32),
        cost_estimate=LARGE,
        name="hop",
    )(*picks, *operands)
    return found[0::2], found[1::2]


def per_device(
    layer_in, out_grad, norm_gain, norm_bias, w_qkv, b_qkv, w_out, b_out, w_up, b_up,
    w_down, b_down, seq_lengths, token_place,
):
    heads, blks = lax.axis_size("head"), lax.axis_size("blk")
    count = heads * blks
    my_head, my_blk = lax.axis_index("head"), lax.axis_index("blk")
    me = my_head * blks + my_blk
    rows, width = layer_in.shape
    features = w_qkv.shape[1]
    units = w_up.shape[0]
    owners = HEAD_DIM // features
    member = me % owners
    blk_bits = [1 << i for i in range(blks.bit_length() - 1)][::-1]
    head_bits = [blks << i for i in range(heads.bit_length() - 1)][::-1]
    head_masks = slot_masks(head_bits)
    numbers = jnp.arange(count, dtype=jnp.int32)

    place = token_place.reshape(count, rows)
    ranks = place // count
    row_numbers = jnp.arange(rows, dtype=jnp.int32)
    own_ranks = lax.dynamic_slice_in_dim(ranks, me, 1, 0)
    order_hot = (own_ranks == row_numbers[:, None]).astype(BF16)
    x_sorted = dot_nn(order_hot, layer_in).astype(BF16)
    x_all = lax.all_gather(x_sorted, "blk", axis=0, tiled=True)
    g_sorted = dot_nn(order_hot, out_grad).astype(BF16)

    qkv_full, out_full, bias_full = w_qkv, w_out, b_qkv
    if owners > 1:
        order = member ^ jnp.arange(owners, dtype=jnp.int32)

        def of_owners(block):
            found = [block] + [swap(block, e, count) for e in range(1, owners)]
            return jnp.stack(found)[order]

        qkv_full = jnp.moveaxis(of_owners(w_qkv), 0, 1).reshape(3, HEAD_DIM, width)
        bias_full = jnp.moveaxis(of_owners(b_qkv), 0, 1).reshape(3, HEAD_DIM)
        out_full = of_owners(w_out).reshape(HEAD_DIM, width)
    qkv_cut, lanes = 3 * HEAD_DIM, 2 * HEAD_DIM

    def all_heads(own):
        found = [own]
        for bit in head_bits:
            found = found + [swap(w, bit, count) for w in found]
        return found

    vectors = jnp.stack([norm_gain, norm_bias, b_out, b_down])
    bias_row = jnp.concatenate([bias_full.reshape(-1), b_up])
    piece = vectors.size
    tile = jnp.zeros((16, width), BF16)
    tile = tile.at[0, : qkv_cut + units].set(bias_row).at[1, :piece].set(vectors.reshape(-1))
    w_list = all_heads(jnp.concatenate([qkv_full.reshape(qkv_cut, width), tile], axis=0))
    up_list = all_heads(w_up)
    w_back_list = all_heads(jnp.concatenate([w_down, out_full], axis=0))
    back_over = w_back_list[1]
    g_all = lax.all_gather(after(g_sorted, w_list[1]), "blk", axis=0, tiled=True)
    biases = jnp.stack([w[qkv_cut, : qkv_cut + units] for w in w_list]).astype(F32)

    vectors = jnp.stack([w[qkv_cut + 1, :piece].reshape(vectors.shape) for w in w_list])
    for mask in blk_bits:
        vectors = jnp.concatenate([vectors, swap(vectors, mask, count)], axis=0)
    absolute = me ^ jnp.array(slot_masks(head_bits + blk_bits), dtype=jnp.int32)
    choose = (absolute[None, :] == numbers[:, None]).astype(BF16)
    vectors = dot_nn(choose, vectors.reshape(count, -1)).reshape(count, 4, -1)
    vectors = jnp.transpose(vectors, (1, 0, 2)).reshape(4, width)
    gain, offset, out_bias, down_bias = (vectors[i][None] for i in range(4))

    (qkv_rows,) = join(
        w_list,
        [
            [(r, 0, lanes, r * lanes) for r in range(heads)]
            + [(r, lanes, HEAD_DIM, heads * lanes + r * HEAD_DIM) for r in range(heads)]
        ],
        back_over,
    )
    qkv_bias = jnp.concatenate(
        [biases[:, :lanes].reshape(1, -1), biases[:, lanes:qkv_cut].reshape(1, -1)], axis=1
    )
    up_bias = biases[:, qkv_cut:].reshape(1, -1)

    sorted_place = jnp.sum(
        jnp.where(ranks[:, None, :] == row_numbers[None, :, None], place[:, None, :], 0), axis=2
    )
    slot_head = my_head ^ jnp.array([m // blks for m in head_masks], dtype=jnp.int32)
    device = (slot_head[:, None] * blks + jnp.arange(blks, dtype=jnp.int32)[None, :]).reshape(-1)
    chosen = jnp.where((device[:, None] == numbers[None, :])[:, :, None], sorted_place[None], 0)
    positions = jnp.sum(chosen, axis=1)
    own_positions = positions[:blks].reshape(-1)
    own_place = own_positions - opening_of(own_positions, seq_lengths)
    tiles = rows // GROUP
    positions = jnp.transpose(positions.reshape(count, tiles, GROUP), (1, 0, 2))
    positions = positions.reshape(tiles, count * GROUP)
    meta = attention_meta(positions, seq_lengths, min(CHUNK, count * GROUP))

    x_all = after(x_all, back_over)
    x_rows = x_all.astype(F32)
    center = jnp.mean(x_rows, axis=-1, keepdims=True)
    variance = jnp.mean((x_rows - center) ** 2, axis=-1, keepdims=True)
    inverse = lax.rsqrt(variance + 1e-05)
    normed = ((x_rows - center) * inverse * gain + offset).astype(BF16)
    qkv = rotary(dot_nt(normed, qkv_rows), qkv_bias, own_place, heads, blks)
    qkv_made = qkv[0]
    qkv = exchange(qkv, head_masks, count)
    (up_rows,) = join(
        up_list, [[(r, 0, units, r * units) for r in range(heads)]], qkv_made
    )
    hidden = dot_nt(normed, up_rows) + up_bias
    active = gelu_tanh(hidden).astype(BF16)
    meta["low"] = after(meta["low"], active)
    attended, saved = attention_forward(qkv, meta)
    down_rows, out_rows = join(
        w_back_list,
        [
            [(r, 0, units, r * units) for r in range(heads)],
            [(r, units, HEAD_DIM, r * HEAD_DIM) for r in range(heads)],
        ],
        attended[0],
    )
    def flat(block):
        return block.reshape(-1, block.shape[-1])

    def own_features(part):
        if owners == 1:
            return part
        mine = jnp.arange(lanes, dtype=jnp.int32) % HEAD_DIM // features == member
        return jnp.where(mine, part, 0)

    def packed(part):
        part = part.reshape(2, blks // 2, rows, HEAD_DIM)
        return jnp.concatenate([part[0], part[1]], axis=-1)

    attended = exchange(attended, head_masks, count)
    attended = [own_features(part) for part in attended]
    mixed = mixed_rows(active, attended, down_rows, out_rows)
    g_late = after(g_all, mixed)

    heads_grad = dot_nt(g_late, out_rows).astype(BF16)
    heads_grad = [packed(heads_grad[:, r * HEAD_DIM : (r + 1) * HEAD_DIM]) for r in range(heads)]
    mine, others = list(range(heads // 2)), list(range(heads // 2, heads))
    back_sent = outer(attended, active, g_late, others, units, heads_grad[0])
    back_there = swap(back_sent, head_bits[-1], count)
    heads_grad = exchange(heads_grad, head_masks, count)
    heads_grad[0] = after(heads_grad[0], back_sent)
    mixed = mixed.reshape(blks, rows, width)
    mixed = lax.psum_scatter(mixed, "blk", scatter_dimension=0, tiled=False)

    qkv_grad, qkv_sums = attention_backward(heads_grad, meta, saved)
    g_last = after(g_late, qkv_grad[0])
    qkv_grad = [own_features(part) for part in exchange(qkv_grad, head_masks, count)]
    back_own, back_far = outer(attended, active, g_last, mine, units, g_last, back_there)
    back_there = swap(back_far, head_bits[0], count)
    hidden_grad, up_sums = hidden_grads(g_last, hidden, down_rows, back_far)

    pieces = pieces_of(blks, rows)
    split_shape = (2,) * len(blk_bits)
    slots = jnp.arange(blks, dtype=jnp.int32).reshape(split_shape)
    parts = [(blks // 2, begin, end) for (begin, end), _ in pieces]

    def halves(block, far):
        found = []
        for (begin, end), order in pieces:
            axis = blk_bits.index(order[0])
            mine = (my_blk // order[0]) % 2
            piece = block if block.ndim == len(blk_bits) else block[..., begin:end, :]
            found.append(pick(piece, axis, 1 - mine if far else mine))
        return found

    hid_rows = hidden_grad.reshape(blks, rows, heads * units)

    def sums_of(far, token):
        chosen = jnp.concatenate([p.reshape(-1) for p in halves(slots, far)])
        return shifted(hid_rows, qkv_grad, up_rows, qkv_rows, chosen, parts, token)

    sent = sums_of(True, hidden_grad)
    kept = sums_of(False, sent[0])
    in_sent = outer(qkv_grad, hidden_grad, normed, others, units, kept[0])
    in_there = swap(in_sent, head_bits[-1], count)
    chosen = [p.reshape(-1) for p in halves(slots, True) + halves(slots, False)]
    norm_grads = norm_sums(
        after(x_all, in_sent, back_there).reshape(blks, rows, width),
        center.reshape(blks, rows, 1),
        inverse.reshape(blks, rows, 1),
        list(sent) + list(kept),
        jnp.concatenate(chosen),
        parts + parts,
    )

    own_g = g_sorted.astype(F32)
    sums = jnp.concatenate([norm_grads, jnp.sum(own_g, axis=0)[None]], axis=0)
    sums = sums.reshape(3, heads, blks, -1)
    sums = jnp.transpose(sums, (1, 2, 0, 3)).reshape(heads, -1)
    slot_numbers = jnp.arange(heads, dtype=jnp.int32)
    reached = jnp.where((slot_head[:, None] == slot_numbers[None])[:, :, None], sums[None], 0.0)
    small = jnp.concatenate([jnp.sum(reached, axis=1), up_sums.reshape(heads, units)], axis=1)

    orders = [order for _, order in pieces]
    kept = [after(kept[0], small, mixed), kept[1]]
    there = [swap(sent[i], order[0], count) for i, order in enumerate(orders)]
    left = [[b for b in blk_bits if b != order[0]] for order in orders]
    for step in range(1, len(blk_bits)):
        masks = [order[step] for order in orders]
        far, kept = hop(kept, there, masks, left, my_blk)
        there = [swap(f, mask, count) for f, mask in zip(far, masks)]
        left = [[b for b in bits if b != mask] for bits, mask in zip(left, masks)]
        if step == 1:
            small = after(small, far[0])
            small = sum(exchange([small[r] for r in range(heads)], head_masks, count))
            kept = [after(kept[0], small), kept[1]]
            in_own, in_far = outer(qkv_grad, hidden_grad, normed, mine, units, kept[0], in_there)
            in_there = swap(in_far, head_bits[0], count)
        if step == len(blk_bits) - 2:
            kept = [after(kept[0], in_far), kept[1]]
        last_far = far[0]
    layer_out = layer_rows(
        x_sorted, mixed, jnp.concatenate([out_bias, down_bias], axis=0), order_hot, last_far
    )
    w_down_grad, w_out_grad = totals(back_own, back_there, units, last_far)
    w_up_grad, w_qkv_grad = totals(in_own, in_there, units, last_far)
    w_qkv_grad = w_qkv_grad.reshape(3, owners, features, width)
    w_qkv_grad = lax.dynamic_index_in_dim(w_qkv_grad, member, 1, False)
    w_out_grad = w_out_grad.reshape(owners, features, width)
    w_out_grad = lax.dynamic_index_in_dim(w_out_grad, member, 0, False)
    qkv_sums = qkv_sums.reshape(3, owners, features)
    b_qkv_grad = lax.dynamic_index_in_dim(qkv_sums, member, 1, False)

    sums, b_up_grad = small[:-units].reshape(blks, -1), small[-units:]
    relative = jnp.arange(blks, dtype=jnp.int32) ^ my_blk
    reached = jnp.where((relative[:, None] == slots.reshape(1, -1))[:, :, None], sums[None], 0.0)
    reached = jnp.sum(reached, axis=1)
    sums = sum(exchange([reached[i] for i in range(blks)], list(range(blks)), count))
    vector_grads = sums.reshape(3, -1)

    input_grad = input_rows(x_sorted, g_sorted, gain, order_hot, kept, there)
    return (
        layer_out,
        input_grad,
        vector_grads[0],
        vector_grads[1],
        w_qkv_grad,
        b_qkv_grad,
        w_out_grad,
        vector_grads[2],
        w_up_grad,
        b_up_grad,
        w_down_grad,
        vector_grads[2],
    )


def solution(mesh):
    rows, vector = P(AXES, None), P(AXES)
    qkv, qkv_bias = P(None, AXES, None), P(None, AXES)
    in_specs = (
        rows, rows, vector, vector, qkv, qkv_bias, rows, vector, rows, vector, rows, vector,
        P(), P(),
    )
    out_specs = (
        rows, rows, vector, vector, qkv, qkv_bias, rows, vector, rows, vector, rows, vector,
    )
    return jax.shard_map(
        per_device, mesh=mesh, in_specs=in_specs, out_specs=out_specs, check_vma=False
    )
```

```python
import jax
import jax.numpy as jnp
from jax import lax
from jax.experimental import pallas as pl
from jax.experimental.pallas import tpu as pltpu
from jax.sharding import PartitionSpec as P

HEAD_DIM = 64
ROT = 32
AXES = ("head", "blk")
GROUP = 16
CHUNK = 512
NEG = -1e30
F32 = jnp.float32
BF16 = jnp.bfloat16
SMALL = pl.CostEstimate(flops=1, bytes_accessed=1, transcendentals=0)
MIDDLE = pl.CostEstimate(flops=5_000_000_000, bytes_accessed=1_000_000, transcendentals=0)
BROAD = pl.CostEstimate(flops=34_000_000_000, bytes_accessed=1_000_000, transcendentals=0)
LARGE = pl.CostEstimate(flops=120_000_000_000, bytes_accessed=1_000_000, transcendentals=0)


def swap(block, mask, count):
    return lax.ppermute(block, AXES, [(i, i ^ mask) for i in range(count)])


def dot_nn(a, b):
    return lax.dot_general(a, b, (((1,), (0,)), ((), ())), preferred_element_type=F32)


def dot_nt(a, b):
    return lax.dot_general(a, b, (((1,), (1,)), ((), ())), preferred_element_type=F32)


def dot_tn(a, b):
    return lax.dot_general(a, b, (((0,), (0,)), ((), ())), preferred_element_type=F32)


def opening_of(packed, lengths):
    starts = jnp.cumsum(lengths) - lengths
    inside = packed[..., None] >= starts
    return jnp.max(jnp.where(inside, starts, 0), axis=-1)


def pieces_of(blks, rows):
    bits = [1 << i for i in range(blks.bit_length() - 1)]
    half = rows // 2
    return [((0, half), bits), ((half, rows), bits[1:] + bits[:1])]


def slot_masks(order):
    masks = [0]
    for mask in order:
        masks = masks + [m ^ mask for m in masks]
    return masks


def after_kernel(*refs):
    pass


def after(value, *others):
    anywhere = pl.BlockSpec(memory_space=pl.ANY)
    return pl.pallas_call(
        after_kernel,
        out_shape=jax.ShapeDtypeStruct(value.shape, value.dtype),
        in_specs=[anywhere] * (1 + len(others)),
        out_specs=anywhere,
        input_output_aliases={0: 0},
        compiler_params=pltpu.CompilerParams(vmem_limit_bytes=60 * 1024 * 1024),
        cost_estimate=SMALL,
        name="after",
    )(value, *others)


def whole_block(shape):
    zeros = (0,) * len(shape)
    return pl.BlockSpec(tuple(shape), lambda t, *refs: zeros)


def tile_block(shape, axis):
    def place(t, *refs):
        return tuple(t if i == axis else 0 for i in range(len(shape)))

    return pl.BlockSpec(tuple(shape), place)


def kernel_params(megabytes):
    return pltpu.CompilerParams(
        dimension_semantics=("arbitrary",), vmem_limit_bytes=megabytes * 1024 * 1024
    )


def join_kernel(plans, turned, count, *refs):
    blocks, out_refs = refs[:count], refs[count + 1 :]
    for plan, out_ref in zip(plans, out_refs):
        for which, start, size, to in plan:
            out_ref[to : to + size] = blocks[which][start : start + size]
    if turned:
        for which, start, size, to in plans[0]:
            out_refs[-1][:, to : to + size] = blocks[which][start : start + size].T


def join(blocks, plans, token, turned=False):
    width = blocks[0].shape[1]
    shapes = [(sum(size for _, _, size, _ in plan), width) for plan in plans]
    if turned:
        shapes.append(shapes[0][::-1])
    return pl.pallas_call(
        lambda *refs: join_kernel(plans, turned, len(blocks), *refs),
        out_shape=[jax.ShapeDtypeStruct(shape, BF16) for shape in shapes],
        grid=(1,),
        in_specs=[whole_block(b.shape) for b in blocks] + [pl.BlockSpec(memory_space=pl.ANY)],
        out_specs=[whole_block(shape) for shape in shapes],
        compiler_params=kernel_params(56),
        cost_estimate=SMALL,
        name="join",
    )(*blocks, token)


def sort_kernel(count, me_ref, place_ref, rows_ref, sorted_ref, hot_ref):
    size = rows_ref.shape[0]
    ranks = lax.div(place_ref[0], jnp.int32(count))
    numbers = lax.broadcasted_iota(jnp.int32, (size, size), 0)
    hot = jnp.where(ranks == numbers, 1.0, 0.0).astype(BF16)
    hot_ref[...] = hot
    sorted_ref[...] = dot_nn(hot, rows_ref[...]).astype(BF16)


def sort_rows(rows, token_place, me, count):
    size, width = rows.shape
    return pl.pallas_call(
        lambda *refs: sort_kernel(count, *refs),
        out_shape=[
            jax.ShapeDtypeStruct((size, width), BF16),
            jax.ShapeDtypeStruct((size, size), BF16),
        ],
        grid_spec=pltpu.PrefetchScalarGridSpec(
            num_scalar_prefetch=1,
            grid=(1,),
            in_specs=[
                pl.BlockSpec((1, 1, size), lambda t, at: (at[0], 0, 0)),
                whole_block((size, width)),
            ],
            out_specs=[whole_block((size, width)), whole_block((size, size))],
        ),
        compiler_params=kernel_params(62),
        cost_estimate=SMALL,
        name="sort_rows",
    )(me.reshape(1).astype(jnp.int32), token_place.reshape(count, 1, size), rows)


def project_kernel(heads, *refs):
    x_ref, gain_ref, offset_ref, w_ref, bias_ref, cos_ref, up_ref, down_ref = refs[:8]
    normed_ref, mean_ref, inverse_ref = refs[8:11]
    out_refs = refs[11:]
    _, _, size, width = x_ref.shape
    lanes = cos_ref.shape[3]
    half = ROT // 2
    span = heads * lanes
    x = x_ref[...].reshape(2 * size, width).astype(F32)
    mean = jnp.mean(x, axis=1, keepdims=True)
    centered = x - mean
    inverse = lax.rsqrt(jnp.mean(centered * centered, axis=1, keepdims=True) + 1e-05)
    normed = (centered * inverse * gain_ref[...] + offset_ref[...]).astype(BF16)
    normed_ref[...] = normed.reshape(normed_ref.shape)
    mean_ref[...] = mean.reshape(mean_ref.shape)
    inverse_ref[...] = inverse.reshape(inverse_ref.shape)
    z_both = dot_nn(normed, w_ref[...]) + bias_ref[...]
    values = []
    for side in range(2):
        z = z_both[side * size : (side + 1) * size]
        for r in range(heads):
            u = z[:, r * lanes : (r + 1) * lanes]
            u = (
                u * cos_ref[side, 0]
                + pltpu.roll(u, lanes - half, 1) * up_ref[side, 0]
                + pltpu.roll(u, half, 1) * down_ref[side, 0]
            )
            out_refs[r][0, side] = u.astype(BF16)
        values.append(z[:, span:])
    for r in range(heads):
        at = slice(r * HEAD_DIM, (r + 1) * HEAD_DIM)
        both = jnp.concatenate([values[0][:, at], values[1][:, at]], axis=1)
        out_refs[r][0, 2] = both.astype(BF16)


def project(x_all, gain, offset, w_turned, bias, place, heads, blks):
    rows, width = x_all.shape
    depth = w_turned.shape[1]
    lanes = 2 * HEAD_DIM
    size = rows // blks
    lane = jnp.arange(lanes, dtype=jnp.int32) % HEAD_DIM
    half = ROT // 2
    frequency = 10000.0 ** (-2.0 * (lane % half).astype(F32) / ROT)
    angles = place.astype(F32)[:, None] * frequency[None, :]
    cosine = jnp.where(lane < ROT, jnp.cos(angles), 1.0)
    sine = jnp.sin(angles)
    up = jnp.where(lane < half, -sine, 0.0)
    down = jnp.where((lane >= half) & (lane < ROT), sine, 0.0)
    shape = (2, blks // 2, size)
    strip = tile_block((2, 1, size, width), 1)
    column = tile_block((2, 1, size, 1), 1)
    table = tile_block((2, 1, size, lanes), 1)
    found = pl.pallas_call(
        lambda *refs: project_kernel(heads, *refs),
        out_shape=[
            jax.ShapeDtypeStruct(shape + (width,), BF16),
            jax.ShapeDtypeStruct(shape + (1,), F32),
            jax.ShapeDtypeStruct(shape + (1,), F32),
        ]
        + [jax.ShapeDtypeStruct((blks // 2, 3, size, lanes), BF16)] * heads,
        grid=(blks // 2,),
        in_specs=[
            strip,
            whole_block((1, width)),
            whole_block((1, width)),
            whole_block((width, depth)),
            whole_block((1, depth)),
            table, table, table,
        ],
        out_specs=[strip, column, column] + [tile_block((1, 3, size, lanes), 0)] * heads,
        compiler_params=kernel_params(56),
        cost_estimate=BROAD,
        name="project",
    )(
        x_all.reshape(shape + (width,)), gain, offset, w_turned, bias,
        *[t.reshape(shape + (lanes,)) for t in (cosine, up, down)],
    )
    return found[0].reshape(rows, width), found[1], found[2], found[3:]


def mixed_kernel(heads, *refs):
    act_ref, down_ref, out_w_ref = refs[:3]
    att_refs, out_ref, left_ref = refs[3 : 3 + heads], refs[-2], refs[-1]

    @pl.when(pl.program_id(0) == 0)
    def _():
        parts = [pair_rows(a[...]) for a in att_refs]
        left_ref[...] = jnp.concatenate(parts, axis=1)

    total = dot_nn(act_ref[...], down_ref[...]) + dot_nn(left_ref[...], out_w_ref[...])
    out_ref[...] = total.astype(BF16)


def mixed_rows(active, attended, down_rows, out_rows):
    heads = len(attended)
    rows, span = active.shape
    width = down_rows.shape[1]
    block = 512
    return pl.pallas_call(
        lambda *refs: mixed_kernel(heads, *refs),
        out_shape=jax.ShapeDtypeStruct((rows, width), BF16),
        grid=(width // block,),
        in_specs=[
            whole_block(active.shape),
            tile_block((span, block), 1),
            tile_block((out_rows.shape[0], block), 1),
        ]
        + [whole_block(a.shape) for a in attended],
        out_specs=tile_block((rows, block), 1),
        scratch_shapes=[pltpu.VMEM((rows, heads * HEAD_DIM), BF16)],
        compiler_params=kernel_params(58),
        cost_estimate=SMALL,
        name="mixed",
    )(active, down_rows, out_rows, *attended)


GELU_ROOT = 0.7978845608028654
GELU_CUBE = 0.044715


def hidden_grad_kernel(g_ref, hidden_ref, down_ref, token_ref, grad_ref, sum_ref):
    h = hidden_ref[...]
    square = h * h
    bent = jnp.tanh(GELU_ROOT * (h + GELU_CUBE * (square * h)))
    slope = 0.5 * (1.0 + bent) + (0.5 * GELU_ROOT) * h * (1.0 - bent * bent) * (
        1.0 + (3.0 * GELU_CUBE) * square
    )
    grad = (dot_nn(g_ref[...], down_ref[...]) * slope).astype(BF16)
    grad_ref[...] = grad
    sum_ref[...] = jnp.sum(grad.astype(F32), axis=0, keepdims=True)


def hidden_grads(g_all, hidden, down_turned, token):
    rows, width = g_all.shape
    span = hidden.shape[1]
    block = min(256, span)
    size = min(1024, rows)
    found = pl.pallas_call(
        hidden_grad_kernel,
        out_shape=[
            jax.ShapeDtypeStruct((rows, span), BF16),
            jax.ShapeDtypeStruct((rows // size, 1, span), F32),
        ],
        grid=(rows // size, span // block),
        in_specs=[
            pl.BlockSpec((size, width), lambda i, j: (i, 0)),
            pl.BlockSpec((size, block), lambda i, j: (i, j)),
            pl.BlockSpec((width, block), lambda i, j: (0, j)),
            pl.BlockSpec(memory_space=pl.ANY),
        ],
        out_specs=[
            pl.BlockSpec((size, block), lambda i, j: (i, j)),
            pl.BlockSpec((None, 1, block), lambda i, j: (i, 0, j)),
        ],
        compiler_params=pltpu.CompilerParams(
            dimension_semantics=("arbitrary", "arbitrary"), vmem_limit_bytes=48 * 1024 * 1024
        ),
        cost_estimate=SMALL,
        name="hidden_grad",
    )(g_all, hidden, down_turned, token)
    return found[0], jnp.sum(found[1], axis=(0, 1))


def shifted_kernel(heads, parts, slots_ref, *refs):
    hid_ref, up_ref, w_ref = refs[:3]
    qkv_refs, out_refs, left_ref = refs[3 : 3 + heads], refs[4 + heads : -1], refs[-1]
    half, _, _, lanes = qkv_refs[0].shape
    units = hid_ref.shape[2]
    span = units + heads * lanes

    @pl.when(pl.program_id(0) == 0)
    def _():
        at, number = 0, 0
        for count, begin, end in parts:
            for i in range(count):
                slot = slots_ref[number]
                number += 1
                side = slot // half
                group = slot - side * half
                rows = slice(at, at + end - begin)
                at += end - begin
                left_ref[rows, :units] = hid_ref[slot, begin:end, :]
                values = []
                for r in range(heads):
                    to = units + r * lanes
                    left_ref[rows, to : to + lanes] = qkv_refs[r][group, side, begin:end, :]
                    both = qkv_refs[r][group, 2, begin:end, :]
                    values.append(jnp.where(side == 0, both[:, :HEAD_DIM], both[:, HEAD_DIM:]))
                left_ref[rows, span:] = jnp.concatenate(values, axis=1)

    total = dot_nn(left_ref[:, :units], up_ref[...]) + dot_nn(left_ref[:, units:], w_ref[...])
    at = 0
    for out_ref, (count, begin, end) in zip(out_refs, parts):
        size = count * (end - begin)
        out_ref[...] = total[at : at + size].astype(BF16).reshape(out_ref.shape)
        at += size


def shifted(hid_grad, qkv_grad, up_rows, w_rows, slots, parts, token):
    heads = len(qkv_grad)
    width = up_rows.shape[1]
    total_rows = sum(n * (end - begin) for n, begin, end in parts)
    depth = up_rows.shape[0] + w_rows.shape[0]
    block = 512
    return pl.pallas_call(
        lambda *refs: shifted_kernel(heads, parts, *refs),
        out_shape=[jax.ShapeDtypeStruct((n, end - begin, width), BF16) for n, begin, end in parts],
        grid_spec=pltpu.PrefetchScalarGridSpec(
            num_scalar_prefetch=1,
            grid=(width // block,),
            in_specs=[
                whole_block(hid_grad.shape),
                tile_block((up_rows.shape[0], block), 1),
                tile_block((w_rows.shape[0], block), 1),
            ]
            + [whole_block(q.shape) for q in qkv_grad]
            + [pl.BlockSpec(memory_space=pl.ANY)],
            out_specs=[tile_block((n, end - begin, block), 2) for n, begin, end in parts],
            scratch_shapes=[pltpu.VMEM((total_rows, depth), BF16)],
        ),
        compiler_params=kernel_params(60),
        cost_estimate=MIDDLE,
        name="shifted",
    )(slots, hid_grad, up_rows, w_rows, *qkv_grad, token)


def turn_left(left_ref, owners_of, units, second_ref, first_refs):
    low, high = owners_of[0] * units, (owners_of[-1] + 1) * units
    left_ref[: high - low, :] = second_ref[:, low:high].T
    at = high - low
    cols = left_ref.shape[1] // 2
    for ref in first_refs:
        if len(ref.shape) == 4:
            half, _, rows, lanes = ref.shape
            for side in range(2):
                block = ref[:, side].reshape(half * rows, lanes).T
                left_ref[at : at + lanes, side * cols : (side + 1) * cols] = block
            at += lanes
            pair = ref[:, 2].reshape(half * rows, lanes).T
        else:
            half, rows, lanes = ref.shape
            pair = ref[...].reshape(half * rows, lanes).T
        left_ref[at : at + HEAD_DIM, :cols] = pair[:HEAD_DIM]
        left_ref[at : at + HEAD_DIM, cols:] = pair[HEAD_DIM:]
        at += HEAD_DIM


SHARES = 4


def outer_kernel(owners_of, units, *refs):
    second_ref, right_ref = refs[:2]
    first_refs, left_ref = refs[2 : -2 - SHARES], refs[-1]
    out_refs = refs[-1 - SHARES : -1]

    @pl.when(pl.program_id(0) == 0)
    def _():
        turn_left(left_ref, owners_of, units, second_ref, first_refs)

    total = dot_nn(left_ref[...], right_ref[...]).astype(BF16)
    at = 0
    for ref in out_refs:
        ref[...] = total[at : at + ref.shape[0]]
        at += ref.shape[0]


def outer_add_kernel(owners_of, units, *refs):
    second_ref, right_ref = refs[:2]
    there_refs = refs[2 : 2 + SHARES]
    first_refs, own_ref, sent_ref, left_ref = refs[2 + SHARES : -4], refs[-3], refs[-2], refs[-1]

    @pl.when(pl.program_id(0) == 0)
    def _():
        turn_left(left_ref, owners_of, units, second_ref, first_refs)

    there = jnp.concatenate([ref[...] for ref in there_refs], axis=0)
    total = dot_nn(left_ref[...], right_ref[...]) + there.astype(F32)
    span = len(owners_of) * units
    cut = (total.shape[0] - span) // len(owners_of)
    own = len(owners_of) // 2
    low, high = own * units, span + own * cut
    own_ref[...] = jnp.concatenate([total[:low], total[span:high]], axis=0)
    sent_ref[...] = jnp.concatenate([total[low:span], total[high:]], axis=0).astype(BF16)


def outer(firsts, second, right, owners_of, units, token, there=None):
    rows, width = right.shape
    chosen = [firsts[r] for r in owners_of]
    block = min(512, width)
    cut = 3 * HEAD_DIM if len(chosen[0].shape) == 4 else HEAD_DIM
    count = len(owners_of) * (units + cut)
    strip = tile_block((count // SHARES, block), 1)
    operands, specs = [second, right], [whole_block(second.shape), tile_block((rows, block), 1)]
    if there is None:
        kernel = outer_kernel
        shapes = [jax.ShapeDtypeStruct((count // SHARES, width), BF16)] * SHARES
        out_specs = [strip] * SHARES
    else:
        kernel = outer_add_kernel
        shapes = [
            jax.ShapeDtypeStruct((count // 2, width), F32),
            jax.ShapeDtypeStruct((count // 2, width), BF16),
        ]
        out_specs = [tile_block((count // 2, block), 1)] * 2
        operands += there
        specs += [strip] * SHARES
    return pl.pallas_call(
        lambda *refs: kernel(owners_of, units, *refs),
        out_shape=shapes,
        grid=(width // block,),
        in_specs=specs
        + [whole_block(f.shape) for f in chosen]
        + [pl.BlockSpec(memory_space=pl.ANY)],
        out_specs=out_specs,
        scratch_shapes=[pltpu.VMEM((count, rows), BF16)],
        compiler_params=kernel_params(58),
        cost_estimate=SMALL,
        name="outer",
    )(*operands, *chosen, token)


def sums_kernel(parts, slots_ref, *refs):
    x_ref, mean_ref, inverse_ref = refs[:3]
    part_refs, out_ref = refs[3:-1], refs[-1]
    number = 0
    gain_sum, bias_sum = 0.0, 0.0
    for ref, (count, begin, end) in zip(part_refs, parts):
        for i in range(count):
            slot = slots_ref[number]
            number += 1
            x_hat = x_ref[slot, begin:end, :].astype(F32) - mean_ref[slot, begin:end, :]
            x_hat = x_hat * inverse_ref[slot, begin:end, :]
            part = ref[i].astype(F32)
            gain_sum += jnp.sum(part * x_hat, axis=0, keepdims=True)
            bias_sum += jnp.sum(part, axis=0, keepdims=True)
    out_ref[0:1, :] = gain_sum
    out_ref[1:2, :] = bias_sum


def norm_sums(x_all, mean, inverse, blocks, slots, parts):
    blks, rows, width = x_all.shape
    block = 512
    return pl.pallas_call(
        lambda *refs: sums_kernel(parts, *refs),
        out_shape=jax.ShapeDtypeStruct((2, width), F32),
        grid_spec=pltpu.PrefetchScalarGridSpec(
            num_scalar_prefetch=1,
            grid=(width // block,),
            in_specs=[
                tile_block((blks, rows, block), 2),
                whole_block(mean.shape),
                whole_block(inverse.shape),
            ]
            + [tile_block(b.shape[:2] + (block,), 2) for b in blocks],
            out_specs=tile_block((2, block), 1),
        ),
        compiler_params=kernel_params(56),
        cost_estimate=SMALL,
        name="norm_sums",
    )(slots, x_all, mean, inverse, *blocks)


def total_kernel(own_ref, there_ref, token_ref, top_ref, low_ref):
    cut = top_ref.shape[0]
    total = own_ref[...] + there_ref[...].astype(F32)
    top_ref[...] = total[:cut]
    low_ref[...] = total[cut:]


def totals(own, there, cut, token):
    rows, width = own.shape
    block = 512
    return pl.pallas_call(
        total_kernel,
        out_shape=[
            jax.ShapeDtypeStruct((cut, width), F32),
            jax.ShapeDtypeStruct((rows - cut, width), F32),
        ],
        grid=(width // block,),
        in_specs=[tile_block((rows, block), 1)] * 2 + [pl.BlockSpec(memory_space=pl.ANY)],
        out_specs=[tile_block((cut, block), 1), tile_block((rows - cut, block), 1)],
        compiler_params=kernel_params(32),
        cost_estimate=SMALL,
        name="totals",
    )(own, there, token)


def add_kernel(count, *refs):
    total = refs[0][...]
    for ref in refs[1:count]:
        total += ref[...]
    refs[-1][...] = total


def added(parts, token):
    shape = parts[0].shape
    return pl.pallas_call(
        lambda *refs: add_kernel(len(parts), *refs),
        out_shape=jax.ShapeDtypeStruct(shape, F32),
        grid=(1,),
        in_specs=[whole_block(shape)] * len(parts) + [pl.BlockSpec(memory_space=pl.ANY)],
        out_specs=whole_block(shape),
        compiler_params=kernel_params(16),
        cost_estimate=SMALL,
        name="added",
    )(*parts, token)


def layer_out_kernel(x_ref, mixed_ref, bias_ref, hot_ref, token_ref, out_ref):
    total = x_ref[...].astype(F32) + mixed_ref[...].astype(F32) + bias_ref[0:1] + bias_ref[1:2]
    out_ref[...] = dot_tn(hot_ref[...], total.astype(BF16)).astype(BF16)


def layer_rows(x, mixed, biases, hot, token):
    operands = (x, mixed, biases, hot)
    return pl.pallas_call(
        layer_out_kernel,
        out_shape=jax.ShapeDtypeStruct(x.shape, BF16),
        grid=(1,),
        in_specs=[whole_block(o.shape) for o in operands] + [pl.BlockSpec(memory_space=pl.ANY)],
        out_specs=whole_block(x.shape),
        compiler_params=kernel_params(32),
        cost_estimate=SMALL,
        name="layer_rows",
    )(*operands, token)


def input_grad_kernel(pieces, *refs):
    x_ref, g_ref, gain_ref, hot_ref = refs[:4]
    kept_refs, there_refs, out_ref = refs[4 : 4 + pieces], refs[4 + pieces : -1], refs[-1]
    grad = jnp.concatenate(
        [k[0] + t[0].astype(F32) for k, t in zip(kept_refs, there_refs)], axis=0
    )
    x = x_ref[...].astype(F32)
    centered = x - jnp.mean(x, axis=1, keepdims=True)
    inverse = lax.rsqrt(jnp.mean(centered * centered, axis=1, keepdims=True) + 1e-05)
    x_hat = centered * inverse
    e = grad * gain_ref[...]
    part = inverse * (
        e
        - jnp.mean(e, axis=1, keepdims=True)
        - x_hat * jnp.mean(e * x_hat, axis=1, keepdims=True)
    )
    total = (g_ref[...].astype(F32) + part).astype(BF16)
    out_ref[...] = dot_tn(hot_ref[...], total).astype(BF16)


def input_rows(x, g, gain, hot, kept, there):
    operands = (x, g, gain, hot, *kept, *there)
    return pl.pallas_call(
        lambda *refs: input_grad_kernel(len(kept), *refs),
        out_shape=jax.ShapeDtypeStruct(x.shape, BF16),
        grid=(1,),
        in_specs=[whole_block(o.shape) for o in operands],
        out_specs=whole_block(x.shape),
        compiler_params=kernel_params(32),
        cost_estimate=SMALL,
        name="input_rows",
    )(*operands)


def rope_t(u, cosine, sine):
    half = ROT // 2
    top, low = u[:half], u[half:ROT]
    return jnp.concatenate(
        [top * cosine - low * sine, low * cosine + top * sine, u[ROT:]], axis=0
    )


def tall(block):
    return block.reshape(block.shape[0] * block.shape[1], block.shape[2])


def pair_rows(block):
    both = tall(block)
    return jnp.concatenate([both[:, :HEAD_DIM], both[:, HEAD_DIM:]], axis=0)


def packed_rows(refs):
    qk, v = [], []
    for ref in refs:
        qk += [tall(ref[:, 0]), tall(ref[:, 1])]
        v.append(pair_rows(ref[:, 2]))
    return jnp.concatenate(qk, axis=0), jnp.concatenate(v, axis=0)


def side_by_side(block):
    middle = block.shape[0] // 2
    return jnp.concatenate([block[:middle], block[middle:]], axis=1)


def forward_kernel(sources, *refs):
    lo_ref, mid_ref = refs[:2]
    in_refs = refs[2 : 2 + sources]
    pq_ref, lq_ref, kp_ref = refs[2 + sources : 5 + sources]
    att_refs = refs[5 + sources : 5 + 2 * sources]
    ot_ref, lse_ref, q_ref, k_ref, v_ref, qt_ref, kt_ref, vt_ref = refs[5 + 2 * sources :]
    t = pl.program_id(0)
    chunk = q_ref.shape[1]
    qk, v = packed_rows(in_refs)
    per = v.shape[0] // chunk
    for c in range(per):
        index = t * per + c
        part, values = qk[c * chunk : (c + 1) * chunk], v[c * chunk : (c + 1) * chunk]
        q_ref[index] = part[:, :HEAD_DIM]
        k_ref[index] = part[:, HEAD_DIM:]
        v_ref[index] = values
        turned = part.astype(F32).T
        qt_ref[index] = (turned[:HEAD_DIM] * HEAD_DIM**-0.5).astype(BF16)
        kt_ref[index] = turned[HEAD_DIM:].astype(BF16)
        vt_ref[index] = values.astype(F32).T.astype(BF16)
    outs = []
    for c in range(per):
        qt = qt_ref[t * per + c]
        query_pos, query_lo = pq_ref[c], lq_ref[c]

        def step(kc, state, masked):
            run_max, run_sum, acc = state
            scores = dot_nn(k_ref[kc], qt)
            if masked:
                key_pos = kp_ref[kc]
                visible = (key_pos <= query_pos) & (key_pos >= query_lo)
                scores = jnp.where(visible, scores, NEG)
            new_max = jnp.maximum(run_max, jnp.max(scores, axis=0, keepdims=True))
            weights = jnp.exp(scores - new_max)
            if masked:
                weights = jnp.where(visible, weights, 0.0)
            rescale = jnp.exp(run_max - new_max)
            run_sum = run_sum * rescale + jnp.sum(weights, axis=0, keepdims=True)
            acc = acc * rescale + dot_nn(vt_ref[kc], weights.astype(BF16))
            return new_max, run_sum, acc

        state = (
            jnp.full((1, chunk), NEG, F32),
            jnp.zeros((1, chunk), F32),
            jnp.zeros((HEAD_DIM, chunk), F32),
        )
        state = lax.fori_loop(lo_ref[t], mid_ref[t], lambda i, s: step(i, s, True), state)
        state = lax.fori_loop(mid_ref[t], t * per, lambda i, s: step(i, s, False), state)
        state = lax.fori_loop(t * per, (t + 1) * per, lambda i, s: step(i, s, True), state)
        run_max, run_sum, acc = state
        out = acc / run_sum
        ot_ref[c] = out
        lse_ref[c] = run_max + jnp.log(run_sum)
        outs.append(out.T.astype(BF16))
    att = outs[0] if per == 1 else jnp.concatenate(outs, axis=0)
    span = att.shape[0] // sources
    for i, ref in enumerate(att_refs):
        ref[...] = side_by_side(att[i * span : (i + 1) * span]).reshape(ref.shape)


def backward_kernel(sources, *refs):
    lo_ref, mid_ref = refs[:2]
    g_refs = refs[2 : 2 + sources]
    cos_ref, sin_ref, pq_ref, lq_ref, kp_ref, ot_ref, lse_ref = refs[2 + sources : 9 + sources]
    q_ref, k_ref, v_ref, qt_ref, kt_ref = refs[9 + sources : 14 + sources]
    out_refs = refs[14 + sources : 14 + 2 * sources]
    sum_ref, dk_ref, dv_ref = refs[14 + 2 * sources :]
    t = pl.program_id(0)
    chunk = q_ref.shape[1]
    scaling = HEAD_DIM**-0.5
    grads = jnp.concatenate([pair_rows(ref[...]) for ref in g_refs], axis=0)
    per = grads.shape[0] // chunk
    for c in range(per):
        dk_ref[t * per + c] = jnp.zeros((chunk, HEAD_DIM), F32)
        dv_ref[t * per + c] = jnp.zeros((chunk, HEAD_DIM), F32)
    parts = []
    for c in range(per):
        index = t * per + c
        do = grads[c * chunk : (c + 1) * chunk]
        dot32 = do.astype(F32).T
        dot16 = dot32.astype(BF16)
        delta = jnp.sum(dot32 * ot_ref[c], axis=0, keepdims=True)
        lse = lse_ref[c]
        q, qt = q_ref[index], qt_ref[index]
        query_pos, query_lo = pq_ref[c], lq_ref[c]

        def step(kc, dqt, masked):
            probs = jnp.exp(dot_nn(k_ref[kc], qt) - lse)
            if masked:
                key_pos = kp_ref[kc]
                visible = (key_pos <= query_pos) & (key_pos >= query_lo)
                probs = jnp.where(visible, probs, 0.0)
            dv_ref[kc] += dot_nn(probs.astype(BF16), do)
            prob_grad = dot_nn(v_ref[kc], dot16)
            score_grad = (probs * (prob_grad - delta)).astype(BF16)
            dk_ref[kc] += dot_nn(score_grad, q)
            return dqt + dot_nn(kt_ref[kc], score_grad)

        dqt = jnp.zeros((HEAD_DIM, chunk), F32)
        dqt = lax.fori_loop(lo_ref[t], mid_ref[t], lambda i, s: step(i, s, True), dqt)
        dqt = lax.fori_loop(mid_ref[t], t * per, lambda i, s: step(i, s, False), dqt)
        dqt = lax.fori_loop(t * per, (t + 1) * per, lambda i, s: step(i, s, True), dqt)
        parts.append(rope_t(dqt * scaling, cos_ref[index], -sin_ref[index]).T)

    def store(block, u, first):
        span = block.shape[0] // sources
        here = pl.ds(pl.multiple_of(u * GROUP, GROUP), GROUP)
        block = block.astype(BF16)
        total = jnp.sum(block.astype(F32), axis=0, keepdims=True)
        if first:
            sum_ref[1:2, :] += total[:, :HEAD_DIM]
            sum_ref[2:3, :] += total[:, HEAD_DIM:]
        else:
            sum_ref[0:1, :] += total
        for i, ref in enumerate(out_refs):
            part = block[i * span : (i + 1) * span]
            half = ref.shape[0]
            shape = (half, GROUP, HEAD_DIM)
            for side in range(2):
                one = part[side * half * GROUP : (side + 1) * half * GROUP, :HEAD_DIM]
                ref[:, side, here, first : first + HEAD_DIM] = one.reshape(shape)
            if first:
                both = side_by_side(part[:, HEAD_DIM:])
                ref[:, 2, here, :] = both.reshape(half, GROUP, 2 * HEAD_DIM)

    @pl.when(t == 0)
    def _():
        sum_ref[...] = jnp.zeros_like(sum_ref)

    store(parts[0] if per == 1 else jnp.concatenate(parts, axis=0), t, 0)

    @pl.when(t == pl.num_programs(0) - 1)
    def _():
        def finish(u, carry):
            found = []
            for c in range(per):
                index = u * per + c
                dkt = rope_t(dk_ref[index].T * scaling, cos_ref[index], -sin_ref[index])
                found.append(jnp.concatenate([dkt.T, dv_ref[index]], axis=1))
            store(found[0] if per == 1 else jnp.concatenate(found, axis=0), u, HEAD_DIM)
            return carry

        lax.fori_loop(0, pl.num_programs(0), finish, 0)


def attention_meta(positions, seq_lengths, chunk):
    tiles, tile = positions.shape
    count = tiles * tile // chunk
    per = tile // chunk
    opening = opening_of(positions, seq_lengths)
    frequency = 10000.0 ** (-2.0 * jnp.arange(ROT // 2, dtype=F32) / ROT)
    angles = (positions - opening).astype(F32).reshape(count, 1, chunk) * frequency[None, :, None]
    ends = jnp.arange(tiles, dtype=jnp.int32) * tile
    first_open = opening_of(ends, seq_lengths)
    last_open = opening_of(ends + tile - 1, seq_lengths)
    own = jnp.arange(tiles, dtype=jnp.int32) * per
    low = (first_open // tile) * per
    middle = jnp.minimum(((last_open + tile - 1) // tile) * per, own)
    return dict(
        low=low.astype(jnp.int32),
        middle=middle.astype(jnp.int32),
        cosine=jnp.cos(angles),
        sine=jnp.sin(angles),
        query_pos=positions.reshape(count, 1, chunk),
        query_lo=opening.reshape(count, 1, chunk),
        key_pos=positions.reshape(count, chunk, 1),
    )


def attention_forward(parts, meta):
    sources = len(parts)
    half, _, rows, lanes = parts[0].shape
    tile = sources * 2 * half * GROUP
    tiles = rows // GROUP
    count, _, chunk = meta["query_pos"].shape
    per = tile // chunk
    nat = jax.ShapeDtypeStruct((count, chunk, HEAD_DIM), BF16)
    turned = jax.ShapeDtypeStruct((count, HEAD_DIM, chunk), BF16)
    out = jax.ShapeDtypeStruct((half, rows, lanes), BF16)
    found = pl.pallas_call(
        lambda *refs: forward_kernel(sources, *refs),
        out_shape=[out] * sources
        + [
            jax.ShapeDtypeStruct((count, HEAD_DIM, chunk), F32),
            jax.ShapeDtypeStruct((count, 1, chunk), F32),
            nat, nat, nat, turned, turned,
        ],
        grid_spec=pltpu.PrefetchScalarGridSpec(
            num_scalar_prefetch=2,
            grid=(tiles,),
            in_specs=[tile_block((half, 3, GROUP, lanes), 2)] * sources
            + [
                tile_block((per, 1, chunk), 0),
                tile_block((per, 1, chunk), 0),
                whole_block((count, chunk, 1)),
            ],
            out_specs=[tile_block((half, GROUP, lanes), 1)] * sources
            + [
                tile_block((per, HEAD_DIM, chunk), 0),
                tile_block((per, 1, chunk), 0),
                whole_block(nat.shape),
                whole_block(nat.shape),
                whole_block(nat.shape),
                whole_block(turned.shape),
                whole_block(turned.shape),
            ],
            scratch_shapes=[pltpu.VMEM(turned.shape, BF16)],
        ),
        compiler_params=pltpu.CompilerParams(
            dimension_semantics=("arbitrary",), vmem_limit_bytes=58 * 1024 * 1024
        ),
        cost_estimate=LARGE,
        name="attention_forward",
    )(
        meta["low"], meta["middle"], *parts,
        meta["query_pos"], meta["query_lo"], meta["key_pos"],
    )
    return found[:sources], found[sources:]


def attention_backward(grads, meta, saved):
    sources = len(grads)
    half, rows, lanes = grads[0].shape
    tile = sources * 2 * half * GROUP
    tiles = rows // GROUP
    count, _, chunk = meta["query_pos"].shape
    per = tile // chunk
    turn = ROT // 2
    out = jax.ShapeDtypeStruct((half, 3, rows, lanes), BF16)
    ot, lse, q, k, v, qt, kt = saved
    found = pl.pallas_call(
        lambda *refs: backward_kernel(sources, *refs),
        out_shape=[out] * sources + [jax.ShapeDtypeStruct((3, HEAD_DIM), F32)],
        grid_spec=pltpu.PrefetchScalarGridSpec(
            num_scalar_prefetch=2,
            grid=(tiles,),
            in_specs=[tile_block((half, GROUP, lanes), 1)] * sources
            + [
                whole_block((count, turn, chunk)),
                whole_block((count, turn, chunk)),
                tile_block((per, 1, chunk), 0),
                tile_block((per, 1, chunk), 0),
                whole_block((count, chunk, 1)),
                tile_block((per, HEAD_DIM, chunk), 0),
                tile_block((per, 1, chunk), 0),
                whole_block(q.shape),
                whole_block(k.shape),
                whole_block(v.shape),
                whole_block(qt.shape),
                whole_block(kt.shape),
            ],
            out_specs=[whole_block(out.shape)] * sources + [whole_block((3, HEAD_DIM))],
            scratch_shapes=[
                pltpu.VMEM((count, chunk, HEAD_DIM), F32),
                pltpu.VMEM((count, chunk, HEAD_DIM), F32),
            ],
        ),
        compiler_params=pltpu.CompilerParams(
            dimension_semantics=("arbitrary",), vmem_limit_bytes=62 * 1024 * 1024
        ),
        cost_estimate=BROAD,
        name="attention_backward",
    )(
        meta["low"], meta["middle"], *grads, meta["cosine"], meta["sine"],
        meta["query_pos"], meta["query_lo"], meta["key_pos"], ot, lse, q, k, v, qt, kt,
    )
    return list(found[:sources]), found[sources]


def doubled(block, masks, count):
    held = block[None]
    for mask in masks:
        held = jnp.concatenate([held, swap(held, mask, count)], axis=0)
    return held


def halved(block, masks, count):
    for mask in masks[::-1]:
        middle = block.shape[0] // 2
        block = block[:middle] + swap(block[middle:], mask, count)
    return block[0]


def gather_list(block, masks, count):
    held = [block]
    for mask in masks:
        held = held + [swap(h, mask, count) for h in held]
    return held


def exchange(parts, masks, count):
    return [part if m == 0 else swap(part, m, count) for part, m in zip(parts, masks)]


def pick(block, axis, index):
    return lax.dynamic_index_in_dim(block, index, axis, False)


def gelu_tanh(values):
    return jax.nn.gelu(values, approximate=True)


def hop_kernel(pieces, *refs):
    refs = refs[2 * pieces :]
    outs = refs[4 * pieces :]
    for i in range(pieces):
        a_ref, b_ref, c_ref, d_ref = refs[4 * i : 4 * i + 4]
        out_ref, own_ref = outs[2 * i : 2 * i + 2]
        out_ref[...] = (a_ref[...].astype(F32) + b_ref[...].astype(F32)).astype(BF16)
        own_ref[...] = c_ref[...].astype(F32) + d_ref[...].astype(F32)


def hop(kept, there, masks, left_bits, my_blk, cost):
    pieces = len(kept)
    count, _, width = kept[0].shape
    picks, in_specs, out_specs, shapes, operands = [], [], [], [], []
    for i in range(pieces):
        numbers = jnp.arange(count, dtype=jnp.int32).reshape((2,) * len(left_bits[i]))
        axis = left_bits[i].index(masks[i])
        mine = (my_blk // masks[i]) % 2
        picks += [pick(numbers, axis, 1 - mine).reshape(-1), pick(numbers, axis, mine).reshape(-1)]
        rows = kept[i].shape[1]
        block = (1, rows, width)
        far = pl.BlockSpec(block, lambda t, *at, i=i: (at[2 * i][t], 0, 0))
        near = pl.BlockSpec(block, lambda t, *at, i=i: (at[2 * i + 1][t], 0, 0))
        in_specs += [far, far, near, near]
        operands += [kept[i], there[i], kept[i], there[i]]
        out_specs += [pl.BlockSpec(block, lambda t, *at: (t, 0, 0))] * 2
        shape = (count // 2, rows, width)
        shapes += [jax.ShapeDtypeStruct(shape, BF16), jax.ShapeDtypeStruct(shape, F32)]
    found = pl.pallas_call(
        lambda *refs: hop_kernel(pieces, *refs),
        out_shape=shapes,
        grid_spec=pltpu.PrefetchScalarGridSpec(
            num_scalar_prefetch=2 * pieces,
            grid=(count // 2,),
            in_specs=in_specs,
            out_specs=out_specs,
        ),
        compiler_params=kernel_params(62),
        cost_estimate=cost,
        name="hop",
    )(*picks, *operands)
    return found[0::2], found[1::2]


def per_device(
    layer_in, out_grad, norm_gain, norm_bias, w_qkv, b_qkv, w_out, b_out, w_up, b_up,
    w_down, b_down, seq_lengths, token_place,
):
    heads, blks = lax.axis_size("head"), lax.axis_size("blk")
    count = heads * blks
    my_head, my_blk = lax.axis_index("head"), lax.axis_index("blk")
    me = my_head * blks + my_blk
    rows, width = layer_in.shape
    features = w_qkv.shape[1]
    units = w_up.shape[0]
    owners = HEAD_DIM // features
    member = me % owners
    blk_bits = [1 << i for i in range(blks.bit_length() - 1)][::-1]
    head_bits = [blks << i for i in range(heads.bit_length() - 1)][::-1]
    head_masks = slot_masks(head_bits)
    numbers = jnp.arange(count, dtype=jnp.int32)

    place = token_place.reshape(count, rows)
    ranks = place // count
    row_numbers = jnp.arange(rows, dtype=jnp.int32)
    x_sorted, order_hot = sort_rows(layer_in, token_place, me, count)
    x_all = lax.all_gather(x_sorted, "blk", axis=0, tiled=True)
    g_sorted = dot_nn(order_hot, out_grad).astype(BF16)

    qkv_full, out_full, bias_full = w_qkv, w_out, b_qkv
    if owners > 1:
        order = member ^ jnp.arange(owners, dtype=jnp.int32)

        def of_owners(block):
            found = [block] + [swap(block, e, count) for e in range(1, owners)]
            return jnp.stack(found)[order]

        qkv_full = jnp.moveaxis(of_owners(w_qkv), 0, 1).reshape(3, HEAD_DIM, width)
        bias_full = jnp.moveaxis(of_owners(b_qkv), 0, 1).reshape(3, HEAD_DIM)
        out_full = of_owners(w_out).reshape(HEAD_DIM, width)
    qkv_cut, lanes = 3 * HEAD_DIM, 2 * HEAD_DIM

    def all_heads(own, token=None):
        over = swap(own, head_bits[0], count)
        found = [own, over if token is None else after(over, token)]
        for bit in head_bits[1:]:
            found = found + [swap(w, bit, count) for w in found]
        return found

    vectors = jnp.stack([norm_gain, norm_bias, b_out, b_down])
    bias_row = jnp.concatenate([bias_full.reshape(-1), b_up])
    piece = vectors.size
    tile = jnp.zeros((16, width), BF16)
    tile = tile.at[0, : qkv_cut + units].set(bias_row).at[1, :piece].set(vectors.reshape(-1))
    w_list = all_heads(jnp.concatenate([qkv_full.reshape(qkv_cut, width), tile], axis=0))
    g_all = lax.all_gather(after(g_sorted, w_list[1]), "blk", axis=0, tiled=True)
    biases = jnp.stack([w[qkv_cut, : qkv_cut + units] for w in w_list]).astype(F32)

    vectors = jnp.stack([w[qkv_cut + 1, :piece].reshape(vectors.shape) for w in w_list])
    for mask in blk_bits:
        vectors = jnp.concatenate([vectors, swap(vectors, mask, count)], axis=0)
    absolute = me ^ jnp.array(slot_masks(head_bits + blk_bits), dtype=jnp.int32)
    choose = (absolute[None, :] == numbers[:, None]).astype(BF16)
    vectors = dot_nn(choose, vectors.reshape(count, -1)).reshape(count, 4, -1)
    vectors = jnp.transpose(vectors, (1, 0, 2)).reshape(4, width)
    gain, offset, out_bias, down_bias = (vectors[i][None] for i in range(4))

    up_list = all_heads(w_up, vectors)
    qkv_rows, qkv_turned = join(
        w_list,
        [
            [(r, 0, lanes, r * lanes) for r in range(heads)]
            + [(r, lanes, HEAD_DIM, heads * lanes + r * HEAD_DIM) for r in range(heads)]
        ],
        vectors,
        True,
    )
    qkv_bias = jnp.concatenate(
        [biases[:, :lanes].reshape(1, -1), biases[:, lanes:qkv_cut].reshape(1, -1)], axis=1
    )
    up_bias = biases[:, qkv_cut:].reshape(1, -1)

    sorted_place = jnp.sum(
        jnp.where(ranks[:, None, :] == row_numbers[None, :, None], place[:, None, :], 0), axis=2
    )
    slot_head = my_head ^ jnp.array([m // blks for m in head_masks], dtype=jnp.int32)
    device = (slot_head[:, None] * blks + jnp.arange(blks, dtype=jnp.int32)[None, :]).reshape(-1)
    chosen = jnp.where((device[:, None] == numbers[None, :])[:, :, None], sorted_place[None], 0)
    positions = jnp.sum(chosen, axis=1)
    own_positions = positions[:blks].reshape(-1)
    own_place = own_positions - opening_of(own_positions, seq_lengths)
    tiles = rows // GROUP
    positions = jnp.transpose(positions.reshape(count, tiles, GROUP), (1, 0, 2))
    positions = positions.reshape(tiles, count * GROUP)
    meta = attention_meta(positions, seq_lengths, min(CHUNK, count * GROUP))

    (up_rows,) = join(
        up_list, [[(r, 0, units, r * units) for r in range(heads)]], vectors
    )
    x_all = after(x_all, up_rows)
    normed, center, inverse, qkv = project(
        x_all, gain, offset, qkv_turned, qkv_bias, own_place, heads, blks
    )
    qkv_made = qkv[0]
    qkv = exchange(qkv, head_masks, count)
    w_back_list = all_heads(jnp.concatenate([w_down, out_full], axis=0), qkv_made)

    down_rows, out_rows, down_turned = join(
        w_back_list,
        [
            [(r, 0, units, r * units) for r in range(heads)],
            [(r, units, HEAD_DIM, r * HEAD_DIM) for r in range(heads)],
        ],
        qkv_made,
        True,
    )
    hidden = dot_nt(normed, up_rows) + up_bias
    active = gelu_tanh(hidden).astype(BF16)
    meta["low"] = after(meta["low"], active)
    attended, saved = attention_forward(qkv, meta)
    def flat(block):
        return block.reshape(-1, block.shape[-1])

    def own_features(part):
        if owners == 1:
            return part
        mine = jnp.arange(lanes, dtype=jnp.int32) % HEAD_DIM // features == member
        return jnp.where(mine, part, 0)

    def packed(part):
        part = part.reshape(2, blks // 2, rows, HEAD_DIM)
        return jnp.concatenate([part[0], part[1]], axis=-1)

    attended_here = attended[0]
    attended = exchange(attended, head_masks, count)
    attended = [own_features(part) for part in attended]
    mixed = mixed_rows(active, attended, down_rows, out_rows)
    g_late = after(g_all, attended_here)

    heads_grad = dot_nt(g_late, out_rows).astype(BF16)
    heads_grad = [packed(heads_grad[:, r * HEAD_DIM : (r + 1) * HEAD_DIM]) for r in range(heads)]
    mine, others = list(range(heads // 2)), list(range(heads // 2, heads))
    back_sent = outer(attended, active, g_late, others, units, heads_grad[0])
    back_there = [swap(part, head_bits[-1], count) for part in back_sent]
    back_sent = back_sent[0]
    heads_grad = exchange(heads_grad, head_masks, count)
    heads_grad[0] = after(heads_grad[0], back_sent, mixed)
    mixed = mixed.reshape(blks, rows, width)
    mixed = lax.psum_scatter(mixed, "blk", scatter_dimension=0, tiled=False)

    qkv_grad, qkv_sums = attention_backward(heads_grad, meta, saved)
    g_last = after(g_late, qkv_grad[0])
    qkv_grad = [own_features(part) for part in exchange(qkv_grad, head_masks, count)]
    back_own, back_far = outer(attended, active, g_last, mine, units, g_last, back_there)
    back_there = swap(back_far, head_bits[0], count)
    hidden_grad, up_sums = hidden_grads(g_last, hidden, down_turned, back_far)

    pieces = pieces_of(blks, rows)
    split_shape = (2,) * len(blk_bits)
    slots = jnp.arange(blks, dtype=jnp.int32).reshape(split_shape)
    parts = [(blks // 2, begin, end) for (begin, end), _ in pieces]

    def halves(block, far):
        found = []
        for (begin, end), order in pieces:
            axis = blk_bits.index(order[0])
            mine = (my_blk // order[0]) % 2
            piece = block if block.ndim == len(blk_bits) else block[..., begin:end, :]
            found.append(pick(piece, axis, 1 - mine if far else mine))
        return found

    hid_rows = hidden_grad.reshape(blks, rows, heads * units)

    chosen = jnp.concatenate([p.reshape(-1) for p in halves(slots, True) + halves(slots, False)])
    found = shifted(
        hid_rows, qkv_grad, up_rows, qkv_rows, chosen, parts + parts, hidden_grad
    )
    sent, kept = found[: len(parts)], found[len(parts) :]
    in_sent = outer(qkv_grad, hidden_grad, normed, others, units, kept[0])
    in_there = [swap(part, head_bits[-1], count) for part in in_sent]
    in_sent = in_sent[0]
    norm_grads = norm_sums(
        after(x_all, in_sent, back_there).reshape(blks, rows, width),
        center.reshape(blks, rows, 1),
        inverse.reshape(blks, rows, 1),
        list(sent) + list(kept),
        chosen,
        parts + parts,
    )

    own_g = g_sorted.astype(F32)
    sums = jnp.concatenate([norm_grads, jnp.sum(own_g, axis=0)[None]], axis=0)
    sums = sums.reshape(3, heads, blks, -1)
    sums = jnp.transpose(sums, (1, 2, 0, 3)).reshape(heads, -1)
    slot_numbers = jnp.arange(heads, dtype=jnp.int32)
    reached = jnp.where((slot_head[:, None] == slot_numbers[None])[:, :, None], sums[None], 0.0)
    small = jnp.concatenate([jnp.sum(reached, axis=1), up_sums.reshape(heads, units)], axis=1)

    small = sum(exchange([small[r] for r in range(heads)], head_masks, count))
    orders = [order for _, order in pieces]
    kept = [after(kept[0], small, mixed), kept[1]]
    there = [swap(sent[i], order[0], count) for i, order in enumerate(orders)]
    left = [[b for b in blk_bits if b != order[0]] for order in orders]
    for step in range(1, len(blk_bits)):
        masks = [order[step] for order in orders]
        far, kept = hop(kept, there, masks, left, my_blk, LARGE if step == 1 else MIDDLE)
        there = [swap(f, mask, count) for f, mask in zip(far, masks)]
        left = [[b for b in bits if b != mask] for bits, mask in zip(left, masks)]
        last_far = far[0]
        if step == 1:
            in_own, in_far = outer(qkv_grad, hidden_grad, normed, mine, units, kept[0], in_there)
            in_there = swap(in_far, head_bits[0], count)
            kept = [after(kept[0], in_far), kept[1]]
    layer_out = layer_rows(
        x_sorted, mixed, jnp.concatenate([out_bias, down_bias], axis=0), order_hot, last_far
    )
    w_down_grad, w_out_grad = totals(back_own, back_there, units, last_far)
    w_up_grad, w_qkv_grad = totals(in_own, in_there, units, last_far)
    w_qkv_grad = w_qkv_grad.reshape(3, owners, features, width)
    w_qkv_grad = lax.dynamic_index_in_dim(w_qkv_grad, member, 1, False)
    w_out_grad = w_out_grad.reshape(owners, features, width)
    w_out_grad = lax.dynamic_index_in_dim(w_out_grad, member, 0, False)
    qkv_sums = qkv_sums.reshape(3, owners, features)
    b_qkv_grad = lax.dynamic_index_in_dim(qkv_sums, member, 1, False)

    sums, b_up_grad = small[:-units].reshape(blks, -1), small[-units:]
    relative = jnp.array(slot_masks(blk_bits), dtype=jnp.int32) ^ my_blk
    reached = relative[:, None] == slots.reshape(1, -1)
    reached = jnp.sum(jnp.where(reached[:, :, None], sums[None], 0.0), axis=1)
    reached = after(reached, last_far)
    for mask in blk_bits[::-1][:-1]:
        middle = reached.shape[0] // 2
        reached = reached[:middle] + swap(reached[middle:], mask, count)
    reached = [reached[:1], swap(reached[1:], blk_bits[0], count)]

    input_grad = input_rows(x_sorted, g_sorted, gain, order_hot, kept, there)
    vector_grads = added(reached, input_grad).reshape(3, -1)
    return (
        layer_out,
        input_grad,
        vector_grads[0],
        vector_grads[1],
        w_qkv_grad,
        b_qkv_grad,
        w_out_grad,
        vector_grads[2],
        w_up_grad,
        b_up_grad,
        w_down_grad,
        vector_grads[2],
    )


def solution(mesh):
    rows, vector = P(AXES, None), P(AXES)
    qkv, qkv_bias = P(None, AXES, None), P(None, AXES)
    in_specs = (
        rows, rows, vector, vector, qkv, qkv_bias, rows, vector, rows, vector, rows, vector,
        P(), P(),
    )
    out_specs = (
        rows, rows, vector, vector, qkv, qkv_bias, rows, vector, rows, vector, rows, vector,
    )
    return jax.shard_map(
        per_device, mesh=mesh, in_specs=in_specs, out_specs=out_specs, check_vma=False
    )
```

```python
import jax
import jax.numpy as jnp
from jax import lax
from jax.experimental import pallas as pl
from jax.experimental.pallas import tpu as pltpu
from jax.sharding import PartitionSpec as P

HEAD_DIM = 64
ROT = 32
AXES = ("head", "blk")
GROUP = 16
CHUNK = 512
NEG = -1e30
F32 = jnp.float32
BF16 = jnp.bfloat16
SMALL = pl.CostEstimate(flops=1, bytes_accessed=1, transcendentals=0)
MIDDLE = pl.CostEstimate(flops=5_000_000_000, bytes_accessed=1_000_000, transcendentals=0)
BROAD = pl.CostEstimate(flops=34_000_000_000, bytes_accessed=1_000_000, transcendentals=0)
LAST = pl.CostEstimate(flops=6_000_000_000, bytes_accessed=1_000_000, transcendentals=0)
LARGE = pl.CostEstimate(flops=120_000_000_000, bytes_accessed=1_000_000, transcendentals=0)


def swap(block, mask, count):
    return lax.ppermute(block, AXES, [(i, i ^ mask) for i in range(count)])


def dot_nn(a, b):
    return lax.dot_general(a, b, (((1,), (0,)), ((), ())), preferred_element_type=F32)


def dot_nt(a, b):
    return lax.dot_general(a, b, (((1,), (1,)), ((), ())), preferred_element_type=F32)


def dot_tn(a, b):
    return lax.dot_general(a, b, (((0,), (0,)), ((), ())), preferred_element_type=F32)


def opening_of(packed, lengths):
    starts = jnp.cumsum(lengths) - lengths
    inside = packed[..., None] >= starts
    return jnp.max(jnp.where(inside, starts, 0), axis=-1)


def pieces_of(blks, rows):
    bits = [1 << i for i in range(blks.bit_length() - 1)]
    half = rows // 2
    return [((0, half), bits), ((half, rows), bits[1:] + bits[:1])]


def slot_masks(order):
    masks = [0]
    for mask in order:
        masks = masks + [m ^ mask for m in masks]
    return masks


def after_kernel(*refs):
    pass


def after(value, *others):
    anywhere = pl.BlockSpec(memory_space=pl.ANY)
    return pl.pallas_call(
        after_kernel,
        out_shape=jax.ShapeDtypeStruct(value.shape, value.dtype),
        in_specs=[anywhere] * (1 + len(others)),
        out_specs=anywhere,
        input_output_aliases={0: 0},
        compiler_params=pltpu.CompilerParams(vmem_limit_bytes=60 * 1024 * 1024),
        cost_estimate=SMALL,
        name="after",
    )(value, *others)


def whole_block(shape):
    zeros = (0,) * len(shape)
    return pl.BlockSpec(tuple(shape), lambda t, *refs: zeros)


def tile_block(shape, axis):
    def place(t, *refs):
        return tuple(t if i == axis else 0 for i in range(len(shape)))

    return pl.BlockSpec(tuple(shape), place)


def kernel_params(megabytes):
    return pltpu.CompilerParams(
        dimension_semantics=("arbitrary",), vmem_limit_bytes=megabytes * 1024 * 1024
    )


def join_kernel(plans, turned, count, *refs):
    blocks, out_refs = refs[:count], refs[count + 1 :]
    for plan, out_ref in zip(plans, out_refs):
        for which, start, size, to in plan:
            out_ref[to : to + size] = blocks[which][start : start + size]
    if turned:
        for which, start, size, to in plans[0]:
            out_refs[-1][:, to : to + size] = blocks[which][start : start + size].T


def join(blocks, plans, token, turned=False):
    width = blocks[0].shape[1]
    shapes = [(sum(size for _, _, size, _ in plan), width) for plan in plans]
    if turned:
        shapes.append(shapes[0][::-1])
    return pl.pallas_call(
        lambda *refs: join_kernel(plans, turned, len(blocks), *refs),
        out_shape=[jax.ShapeDtypeStruct(shape, BF16) for shape in shapes],
        grid=(1,),
        in_specs=[whole_block(b.shape) for b in blocks] + [pl.BlockSpec(memory_space=pl.ANY)],
        out_specs=[whole_block(shape) for shape in shapes],
        compiler_params=kernel_params(56),
        cost_estimate=SMALL,
        name="join",
    )(*blocks, token)


def sort_kernel(count, me_ref, place_ref, rows_ref, sorted_ref, hot_ref):
    size = rows_ref.shape[0]
    ranks = lax.div(place_ref[0], jnp.int32(count))
    numbers = lax.broadcasted_iota(jnp.int32, (size, size), 0)
    hot = jnp.where(ranks == numbers, 1.0, 0.0).astype(BF16)
    hot_ref[...] = hot
    sorted_ref[...] = dot_nn(hot, rows_ref[...]).astype(BF16)


def sort_rows(rows, token_place, me, count):
    size, width = rows.shape
    return pl.pallas_call(
        lambda *refs: sort_kernel(count, *refs),
        out_shape=[
            jax.ShapeDtypeStruct((size, width), BF16),
            jax.ShapeDtypeStruct((size, size), BF16),
        ],
        grid_spec=pltpu.PrefetchScalarGridSpec(
            num_scalar_prefetch=1,
            grid=(1,),
            in_specs=[
                pl.BlockSpec((1, 1, size), lambda t, at: (at[0], 0, 0)),
                whole_block((size, width)),
            ],
            out_specs=[whole_block((size, width)), whole_block((size, size))],
        ),
        compiler_params=kernel_params(62),
        cost_estimate=SMALL,
        name="sort_rows",
    )(me.reshape(1).astype(jnp.int32), token_place.reshape(count, 1, size), rows)


def project_kernel(heads, *refs):
    x_ref, gain_ref, offset_ref, w_ref, bias_ref, cos_ref, up_ref, down_ref = refs[:8]
    normed_ref, mean_ref, inverse_ref = refs[8:11]
    out_refs = refs[11:]
    _, _, size, width = x_ref.shape
    lanes = cos_ref.shape[3]
    half = ROT // 2
    span = heads * lanes
    x = x_ref[...].reshape(2 * size, width).astype(F32)
    mean = jnp.mean(x, axis=1, keepdims=True)
    centered = x - mean
    inverse = lax.rsqrt(jnp.mean(centered * centered, axis=1, keepdims=True) + 1e-05)
    normed = (centered * inverse * gain_ref[...] + offset_ref[...]).astype(BF16)
    normed_ref[...] = normed.reshape(normed_ref.shape)
    mean_ref[...] = mean.reshape(mean_ref.shape)
    inverse_ref[...] = inverse.reshape(inverse_ref.shape)
    z_both = dot_nn(normed, w_ref[...]) + bias_ref[...]
    values = []
    for side in range(2):
        z = z_both[side * size : (side + 1) * size]
        for r in range(heads):
            u = z[:, r * lanes : (r + 1) * lanes]
            u = (
                u * cos_ref[side, 0]
                + pltpu.roll(u, lanes - half, 1) * up_ref[side, 0]
                + pltpu.roll(u, half, 1) * down_ref[side, 0]
            )
            out_refs[r][0, side] = u.astype(BF16)
        values.append(z[:, span:])
    for r in range(heads):
        at = slice(r * HEAD_DIM, (r + 1) * HEAD_DIM)
        both = jnp.concatenate([values[0][:, at], values[1][:, at]], axis=1)
        out_refs[r][0, 2] = both.astype(BF16)


def project(x_all, gain, offset, w_turned, bias, place, heads, blks):
    rows, width = x_all.shape
    depth = w_turned.shape[1]
    lanes = 2 * HEAD_DIM
    size = rows // blks
    lane = jnp.arange(lanes, dtype=jnp.int32) % HEAD_DIM
    half = ROT // 2
    frequency = 10000.0 ** (-2.0 * (lane % half).astype(F32) / ROT)
    angles = place.astype(F32)[:, None] * frequency[None, :]
    cosine = jnp.where(lane < ROT, jnp.cos(angles), 1.0)
    sine = jnp.sin(angles)
    up = jnp.where(lane < half, -sine, 0.0)
    down = jnp.where((lane >= half) & (lane < ROT), sine, 0.0)
    shape = (2, blks // 2, size)
    strip = tile_block((2, 1, size, width), 1)
    column = tile_block((2, 1, size, 1), 1)
    table = tile_block((2, 1, size, lanes), 1)
    found = pl.pallas_call(
        lambda *refs: project_kernel(heads, *refs),
        out_shape=[
            jax.ShapeDtypeStruct(shape + (width,), BF16),
            jax.ShapeDtypeStruct(shape + (1,), F32),
            jax.ShapeDtypeStruct(shape + (1,), F32),
        ]
        + [jax.ShapeDtypeStruct((blks // 2, 3, size, lanes), BF16)] * heads,
        grid=(blks // 2,),
        in_specs=[
            strip,
            whole_block((1, width)),
            whole_block((1, width)),
            whole_block((width, depth)),
            whole_block((1, depth)),
            table, table, table,
        ],
        out_specs=[strip, column, column] + [tile_block((1, 3, size, lanes), 0)] * heads,
        compiler_params=kernel_params(56),
        cost_estimate=BROAD,
        name="project",
    )(
        x_all.reshape(shape + (width,)), gain, offset, w_turned, bias,
        *[t.reshape(shape + (lanes,)) for t in (cosine, up, down)],
    )
    return found[0].reshape(rows, width), found[1], found[2], found[3:]


def mixed_kernel(heads, *refs):
    act_ref, down_ref, out_w_ref = refs[:3]
    att_refs, out_ref, left_ref = refs[3 : 3 + heads], refs[-2], refs[-1]

    @pl.when(pl.program_id(0) == 0)
    def _():
        parts = [pair_rows(a[...]) for a in att_refs]
        left_ref[...] = jnp.concatenate(parts, axis=1)

    total = dot_nn(act_ref[...], down_ref[...]) + dot_nn(left_ref[...], out_w_ref[...])
    out_ref[...] = total.astype(BF16)


def mixed_rows(active, attended, down_rows, out_rows):
    heads = len(attended)
    rows, span = active.shape
    width = down_rows.shape[1]
    block = 512
    return pl.pallas_call(
        lambda *refs: mixed_kernel(heads, *refs),
        out_shape=jax.ShapeDtypeStruct((rows, width), BF16),
        grid=(width // block,),
        in_specs=[
            whole_block(active.shape),
            tile_block((span, block), 1),
            tile_block((out_rows.shape[0], block), 1),
        ]
        + [whole_block(a.shape) for a in attended],
        out_specs=tile_block((rows, block), 1),
        scratch_shapes=[pltpu.VMEM((rows, heads * HEAD_DIM), BF16)],
        compiler_params=kernel_params(58),
        cost_estimate=SMALL,
        name="mixed",
    )(active, down_rows, out_rows, *attended)


GELU_ROOT = 0.7978845608028654
GELU_CUBE = 0.044715


def hidden_grad_kernel(g_ref, hidden_ref, down_ref, token_ref, grad_ref, sum_ref):
    h = hidden_ref[...]
    square = h * h
    bent = jnp.tanh(GELU_ROOT * (h + GELU_CUBE * (square * h)))
    slope = 0.5 * (1.0 + bent) + (0.5 * GELU_ROOT) * h * (1.0 - bent * bent) * (
        1.0 + (3.0 * GELU_CUBE) * square
    )
    grad = (dot_nn(g_ref[...], down_ref[...]) * slope).astype(BF16)
    grad_ref[...] = grad
    sum_ref[...] = jnp.sum(grad.astype(F32), axis=0, keepdims=True)


def hidden_grads(g_all, hidden, down_turned, token):
    rows, width = g_all.shape
    span = hidden.shape[1]
    block = min(256, span)
    size = min(1024, rows)
    found = pl.pallas_call(
        hidden_grad_kernel,
        out_shape=[
            jax.ShapeDtypeStruct((rows, span), BF16),
            jax.ShapeDtypeStruct((rows // size, 1, span), F32),
        ],
        grid=(rows // size, span // block),
        in_specs=[
            pl.BlockSpec((size, width), lambda i, j: (i, 0)),
            pl.BlockSpec((size, block), lambda i, j: (i, j)),
            pl.BlockSpec((width, block), lambda i, j: (0, j)),
            pl.BlockSpec(memory_space=pl.ANY),
        ],
        out_specs=[
            pl.BlockSpec((size, block), lambda i, j: (i, j)),
            pl.BlockSpec((None, 1, block), lambda i, j: (i, 0, j)),
        ],
        compiler_params=pltpu.CompilerParams(
            dimension_semantics=("arbitrary", "arbitrary"), vmem_limit_bytes=48 * 1024 * 1024
        ),
        cost_estimate=SMALL,
        name="hidden_grad",
    )(g_all, hidden, down_turned, token)
    return found[0], jnp.sum(found[1], axis=(0, 1))


def shifted_kernel(heads, parts, slots_ref, *refs):
    hid_ref, up_ref, w_ref = refs[:3]
    qkv_refs, out_refs, left_ref = refs[3 : 3 + heads], refs[4 + heads : -1], refs[-1]
    half, _, _, lanes = qkv_refs[0].shape
    units = hid_ref.shape[2]
    span = units + heads * lanes

    @pl.when(pl.program_id(0) == 0)
    def _():
        at, number = 0, 0
        for count, begin, end in parts:
            for i in range(count):
                slot = slots_ref[number]
                number += 1
                side = slot // half
                group = slot - side * half
                rows = slice(at, at + end - begin)
                at += end - begin
                left_ref[rows, :units] = hid_ref[slot, begin:end, :]
                values = []
                for r in range(heads):
                    to = units + r * lanes
                    left_ref[rows, to : to + lanes] = qkv_refs[r][group, side, begin:end, :]
                    both = qkv_refs[r][group, 2, begin:end, :]
                    values.append(jnp.where(side == 0, both[:, :HEAD_DIM], both[:, HEAD_DIM:]))
                left_ref[rows, span:] = jnp.concatenate(values, axis=1)

    total = dot_nn(left_ref[:, :units], up_ref[...]) + dot_nn(left_ref[:, units:], w_ref[...])
    at = 0
    for out_ref, (count, begin, end) in zip(out_refs, parts):
        size = count * (end - begin)
        out_ref[...] = total[at : at + size].astype(BF16).reshape(out_ref.shape)
        at += size


def shifted(hid_grad, qkv_grad, up_rows, w_rows, slots, parts, token):
    heads = len(qkv_grad)
    width = up_rows.shape[1]
    total_rows = sum(n * (end - begin) for n, begin, end in parts)
    depth = up_rows.shape[0] + w_rows.shape[0]
    block = 512
    return pl.pallas_call(
        lambda *refs: shifted_kernel(heads, parts, *refs),
        out_shape=[jax.ShapeDtypeStruct((n, end - begin, width), BF16) for n, begin, end in parts],
        grid_spec=pltpu.PrefetchScalarGridSpec(
            num_scalar_prefetch=1,
            grid=(width // block,),
            in_specs=[
                whole_block(hid_grad.shape),
                tile_block((up_rows.shape[0], block), 1),
                tile_block((w_rows.shape[0], block), 1),
            ]
            + [whole_block(q.shape) for q in qkv_grad]
            + [pl.BlockSpec(memory_space=pl.ANY)],
            out_specs=[tile_block((n, end - begin, block), 2) for n, begin, end in parts],
            scratch_shapes=[pltpu.VMEM((total_rows, depth), BF16)],
        ),
        compiler_params=kernel_params(60),
        cost_estimate=MIDDLE,
        name="shifted",
    )(slots, hid_grad, up_rows, w_rows, *qkv_grad, token)


def turn_left(left_ref, owners_of, units, second_ref, first_refs):
    low, high = owners_of[0] * units, (owners_of[-1] + 1) * units
    left_ref[: high - low, :] = second_ref[:, low:high].T
    at = high - low
    cols = left_ref.shape[1] // 2
    for ref in first_refs:
        if len(ref.shape) == 4:
            half, _, rows, lanes = ref.shape
            for side in range(2):
                block = ref[:, side].reshape(half * rows, lanes).T
                left_ref[at : at + lanes, side * cols : (side + 1) * cols] = block
            at += lanes
            pair = ref[:, 2].reshape(half * rows, lanes).T
        else:
            half, rows, lanes = ref.shape
            pair = ref[...].reshape(half * rows, lanes).T
        left_ref[at : at + HEAD_DIM, :cols] = pair[:HEAD_DIM]
        left_ref[at : at + HEAD_DIM, cols:] = pair[HEAD_DIM:]
        at += HEAD_DIM


SHARES = 4


def outer_kernel(owners_of, units, *refs):
    second_ref, right_ref = refs[:2]
    first_refs, left_ref = refs[2 : -2 - SHARES], refs[-1]
    out_refs = refs[-1 - SHARES : -1]

    @pl.when(pl.program_id(0) == 0)
    def _():
        turn_left(left_ref, owners_of, units, second_ref, first_refs)

    total = dot_nn(left_ref[...], right_ref[...]).astype(BF16)
    at = 0
    for ref in out_refs:
        ref[...] = total[at : at + ref.shape[0]]
        at += ref.shape[0]


def outer_add_kernel(owners_of, units, *refs):
    second_ref, right_ref = refs[:2]
    there_refs = refs[2 : 2 + SHARES]
    first_refs, own_ref, sent_ref, left_ref = refs[2 + SHARES : -4], refs[-3], refs[-2], refs[-1]

    @pl.when(pl.program_id(0) == 0)
    def _():
        turn_left(left_ref, owners_of, units, second_ref, first_refs)

    there = jnp.concatenate([ref[...] for ref in there_refs], axis=0)
    total = dot_nn(left_ref[...], right_ref[...]) + there.astype(F32)
    span = len(owners_of) * units
    cut = (total.shape[0] - span) // len(owners_of)
    own = len(owners_of) // 2
    low, high = own * units, span + own * cut
    own_ref[...] = jnp.concatenate([total[:low], total[span:high]], axis=0)
    sent_ref[...] = jnp.concatenate([total[low:span], total[high:]], axis=0).astype(BF16)


def outer(firsts, second, right, owners_of, units, token, there=None):
    rows, width = right.shape
    chosen = [firsts[r] for r in owners_of]
    block = min(512, width)
    cut = 3 * HEAD_DIM if len(chosen[0].shape) == 4 else HEAD_DIM
    count = len(owners_of) * (units + cut)
    strip = tile_block((count // SHARES, block), 1)
    operands, specs = [second, right], [whole_block(second.shape), tile_block((rows, block), 1)]
    if there is None:
        kernel = outer_kernel
        shapes = [jax.ShapeDtypeStruct((count // SHARES, width), BF16)] * SHARES
        out_specs = [strip] * SHARES
    else:
        kernel = outer_add_kernel
        shapes = [
            jax.ShapeDtypeStruct((count // 2, width), F32),
            jax.ShapeDtypeStruct((count // 2, width), BF16),
        ]
        out_specs = [tile_block((count // 2, block), 1)] * 2
        operands += there
        specs += [strip] * SHARES
    return pl.pallas_call(
        lambda *refs: kernel(owners_of, units, *refs),
        out_shape=shapes,
        grid=(width // block,),
        in_specs=specs
        + [whole_block(f.shape) for f in chosen]
        + [pl.BlockSpec(memory_space=pl.ANY)],
        out_specs=out_specs,
        scratch_shapes=[pltpu.VMEM((count, rows), BF16)],
        compiler_params=kernel_params(58),
        cost_estimate=SMALL,
        name="outer",
    )(*operands, *chosen, token)


def sums_kernel(parts, slots_ref, *refs):
    x_ref, mean_ref, inverse_ref = refs[:3]
    part_refs, out_ref = refs[3:-1], refs[-1]
    number = 0
    gain_sum, bias_sum = 0.0, 0.0
    for ref, (count, begin, end) in zip(part_refs, parts):
        for i in range(count):
            slot = slots_ref[number]
            number += 1
            x_hat = x_ref[slot, begin:end, :].astype(F32) - mean_ref[slot, begin:end, :]
            x_hat = x_hat * inverse_ref[slot, begin:end, :]
            part = ref[i].astype(F32)
            gain_sum += jnp.sum(part * x_hat, axis=0, keepdims=True)
            bias_sum += jnp.sum(part, axis=0, keepdims=True)
    out_ref[0:1, :] = gain_sum
    out_ref[1:2, :] = bias_sum


def norm_sums(x_all, mean, inverse, blocks, slots, parts):
    blks, rows, width = x_all.shape
    block = 512
    return pl.pallas_call(
        lambda *refs: sums_kernel(parts, *refs),
        out_shape=jax.ShapeDtypeStruct((2, width), F32),
        grid_spec=pltpu.PrefetchScalarGridSpec(
            num_scalar_prefetch=1,
            grid=(width // block,),
            in_specs=[
                tile_block((blks, rows, block), 2),
                whole_block(mean.shape),
                whole_block(inverse.shape),
            ]
            + [tile_block(b.shape[:2] + (block,), 2) for b in blocks],
            out_specs=tile_block((2, block), 1),
        ),
        compiler_params=kernel_params(56),
        cost_estimate=SMALL,
        name="norm_sums",
    )(slots, x_all, mean, inverse, *blocks)


def total_kernel(own_ref, there_ref, token_ref, top_ref, low_ref):
    cut = top_ref.shape[0]
    total = own_ref[...] + there_ref[...].astype(F32)
    top_ref[...] = total[:cut]
    low_ref[...] = total[cut:]


def totals(own, there, cut, token):
    rows, width = own.shape
    block = 512
    return pl.pallas_call(
        total_kernel,
        out_shape=[
            jax.ShapeDtypeStruct((cut, width), F32),
            jax.ShapeDtypeStruct((rows - cut, width), F32),
        ],
        grid=(width // block,),
        in_specs=[tile_block((rows, block), 1)] * 2 + [pl.BlockSpec(memory_space=pl.ANY)],
        out_specs=[tile_block((cut, block), 1), tile_block((rows - cut, block), 1)],
        compiler_params=kernel_params(32),
        cost_estimate=SMALL,
        name="totals",
    )(own, there, token)


def fold_kernel(kept_ref, there_ref, near_ref, far_ref):
    middle = near_ref.shape[0]
    total = kept_ref[...] + there_ref[...]
    near_ref[...] = total[:middle]
    far_ref[...] = total[middle:]


def fold(kept, there):
    rows, width = kept.shape
    shape = (rows // 2, width)
    return pl.pallas_call(
        fold_kernel,
        out_shape=[jax.ShapeDtypeStruct(shape, F32)] * 2,
        grid=(1,),
        in_specs=[whole_block((rows, width))] * 2,
        out_specs=[whole_block(shape)] * 2,
        compiler_params=kernel_params(16),
        cost_estimate=SMALL,
        name="fold",
    )(kept, there)


def add_kernel(count, *refs):
    total = refs[0][...]
    for ref in refs[1:count]:
        total += ref[...]
    refs[-1][...] = total


def added(parts, token):
    shape = parts[0].shape
    return pl.pallas_call(
        lambda *refs: add_kernel(len(parts), *refs),
        out_shape=jax.ShapeDtypeStruct(shape, F32),
        grid=(1,),
        in_specs=[whole_block(shape)] * len(parts) + [pl.BlockSpec(memory_space=pl.ANY)],
        out_specs=whole_block(shape),
        compiler_params=kernel_params(16),
        cost_estimate=SMALL,
        name="added",
    )(*parts, token)


def layer_out_kernel(x_ref, mixed_ref, bias_ref, hot_ref, token_ref, out_ref):
    total = x_ref[...].astype(F32) + mixed_ref[...].astype(F32) + bias_ref[0:1] + bias_ref[1:2]
    out_ref[...] = dot_tn(hot_ref[...], total.astype(BF16)).astype(BF16)


def layer_rows(x, mixed, biases, hot, token):
    operands = (x, mixed, biases, hot)
    return pl.pallas_call(
        layer_out_kernel,
        out_shape=jax.ShapeDtypeStruct(x.shape, BF16),
        grid=(1,),
        in_specs=[whole_block(o.shape) for o in operands] + [pl.BlockSpec(memory_space=pl.ANY)],
        out_specs=whole_block(x.shape),
        compiler_params=kernel_params(32),
        cost_estimate=SMALL,
        name="layer_rows",
    )(*operands, token)


def input_grad_kernel(pieces, *refs):
    x_ref, g_ref, gain_ref, hot_ref = refs[:4]
    kept_refs, there_refs, out_ref = refs[4 : 4 + pieces], refs[4 + pieces : -1], refs[-1]
    grad = jnp.concatenate(
        [k[0] + t[0].astype(F32) for k, t in zip(kept_refs, there_refs)], axis=0
    )
    x = x_ref[...].astype(F32)
    centered = x - jnp.mean(x, axis=1, keepdims=True)
    inverse = lax.rsqrt(jnp.mean(centered * centered, axis=1, keepdims=True) + 1e-05)
    x_hat = centered * inverse
    e = grad * gain_ref[...]
    part = inverse * (
        e
        - jnp.mean(e, axis=1, keepdims=True)
        - x_hat * jnp.mean(e * x_hat, axis=1, keepdims=True)
    )
    total = (g_ref[...].astype(F32) + part).astype(BF16)
    out_ref[...] = dot_tn(hot_ref[...], total).astype(BF16)


def input_rows(x, g, gain, hot, kept, there):
    operands = (x, g, gain, hot, *kept, *there)
    return pl.pallas_call(
        lambda *refs: input_grad_kernel(len(kept), *refs),
        out_shape=jax.ShapeDtypeStruct(x.shape, BF16),
        grid=(1,),
        in_specs=[whole_block(o.shape) for o in operands],
        out_specs=whole_block(x.shape),
        compiler_params=kernel_params(32),
        cost_estimate=SMALL,
        name="input_rows",
    )(*operands)


def rope_t(u, cosine, sine):
    half = ROT // 2
    top, low = u[:half], u[half:ROT]
    return jnp.concatenate(
        [top * cosine - low * sine, low * cosine + top * sine, u[ROT:]], axis=0
    )


def tall(block):
    return block.reshape(block.shape[0] * block.shape[1], block.shape[2])


def pair_rows(block):
    both = tall(block)
    return jnp.concatenate([both[:, :HEAD_DIM], both[:, HEAD_DIM:]], axis=0)


def packed_rows(refs):
    qk, v = [], []
    for ref in refs:
        qk += [tall(ref[:, 0]), tall(ref[:, 1])]
        v.append(pair_rows(ref[:, 2]))
    return jnp.concatenate(qk, axis=0), jnp.concatenate(v, axis=0)


def side_by_side(block):
    middle = block.shape[0] // 2
    return jnp.concatenate([block[:middle], block[middle:]], axis=1)


def in_pairs(first, last, step, state):
    pairs = lax.div(last - first, 2)
    state = lax.fori_loop(
        0, pairs, lambda i, s: step(first + 2 * i + 1, step(first + 2 * i, s)), state
    )
    return lax.fori_loop(first + 2 * pairs, last, step, state)


def forward_kernel(sources, *refs):
    lo_ref, mid_ref = refs[:2]
    in_refs = refs[2 : 2 + sources]
    pq_ref, lq_ref, kp_ref = refs[2 + sources : 5 + sources]
    att_refs = refs[5 + sources : 5 + 2 * sources]
    ot_ref, lse_ref, q_ref, k_ref, v_ref, qt_ref, kt_ref, vt_ref = refs[5 + 2 * sources :]
    t = pl.program_id(0)
    chunk = q_ref.shape[1]
    qk, v = packed_rows(in_refs)
    per = v.shape[0] // chunk
    for c in range(per):
        index = t * per + c
        part, values = qk[c * chunk : (c + 1) * chunk], v[c * chunk : (c + 1) * chunk]
        q_ref[index] = part[:, :HEAD_DIM]
        k_ref[index] = part[:, HEAD_DIM:]
        v_ref[index] = values
        turned = part.astype(F32).T
        qt_ref[index] = (turned[:HEAD_DIM] * HEAD_DIM**-0.5).astype(BF16)
        kt_ref[index] = turned[HEAD_DIM:].astype(BF16)
        vt_ref[index] = values.astype(F32).T.astype(BF16)
    outs = []
    for c in range(per):
        qt = qt_ref[t * per + c]
        query_pos, query_lo = pq_ref[c], lq_ref[c]

        def step(kc, state, masked):
            run_max, run_sum, acc = state
            scores = dot_nn(k_ref[kc], qt)
            if masked:
                key_pos = kp_ref[kc]
                visible = (key_pos <= query_pos) & (key_pos >= query_lo)
                scores = jnp.where(visible, scores, NEG)
            new_max = jnp.maximum(run_max, jnp.max(scores, axis=0, keepdims=True))
            weights = jnp.exp(scores - new_max)
            rescale = jnp.exp(run_max - new_max)
            run_sum = run_sum * rescale + jnp.sum(weights, axis=0, keepdims=True)
            acc = acc * rescale + dot_nn(vt_ref[kc], weights.astype(BF16))
            return new_max, run_sum, acc

        state = (
            jnp.full((1, chunk), NEG, F32),
            jnp.zeros((1, chunk), F32),
            jnp.zeros((HEAD_DIM, chunk), F32),
        )
        own = t * per + c
        state = step(own, state, True)
        state = lax.fori_loop(lo_ref[t], mid_ref[t], lambda i, s: step(i, s, True), state)
        state = in_pairs(mid_ref[t], t * per, lambda i, s: step(i, s, False), state)
        if per > 1:
            state = lax.fori_loop(t * per, own, lambda i, s: step(i, s, True), state)
            state = lax.fori_loop(own + 1, (t + 1) * per, lambda i, s: step(i, s, True), state)
        run_max, run_sum, acc = state
        out = acc / run_sum
        ot_ref[c] = out
        lse_ref[c] = run_max + jnp.log(run_sum)
        outs.append(out.T.astype(BF16))
    att = outs[0] if per == 1 else jnp.concatenate(outs, axis=0)
    span = att.shape[0] // sources
    for i, ref in enumerate(att_refs):
        ref[...] = side_by_side(att[i * span : (i + 1) * span]).reshape(ref.shape)


def backward_kernel(sources, *refs):
    lo_ref, mid_ref = refs[:2]
    g_refs = refs[2 : 2 + sources]
    cos_ref, sin_ref, pq_ref, lq_ref, kp_ref, ot_ref, lse_ref = refs[2 + sources : 9 + sources]
    q_ref, k_ref, v_ref, qt_ref, kt_ref = refs[9 + sources : 14 + sources]
    out_refs = refs[14 + sources : 14 + 2 * sources]
    sum_ref, dk_ref, dv_ref = refs[14 + 2 * sources :]
    t = pl.program_id(0)
    chunk = q_ref.shape[1]
    scaling = HEAD_DIM**-0.5
    grads = jnp.concatenate([pair_rows(ref[...]) for ref in g_refs], axis=0)
    per = grads.shape[0] // chunk
    for c in range(per):
        dk_ref[t * per + c] = jnp.zeros((chunk, HEAD_DIM), F32)
        dv_ref[t * per + c] = jnp.zeros((chunk, HEAD_DIM), F32)
    parts = []
    for c in range(per):
        index = t * per + c
        do = grads[c * chunk : (c + 1) * chunk]
        dot32 = do.astype(F32).T
        dot16 = dot32.astype(BF16)
        delta = jnp.sum(dot32 * ot_ref[c], axis=0, keepdims=True)
        lse = lse_ref[c]
        q, qt = q_ref[index], qt_ref[index]
        query_pos, query_lo = pq_ref[c], lq_ref[c]

        def step(kc, dqt, masked):
            probs = jnp.exp(dot_nn(k_ref[kc], qt) - lse)
            if masked:
                key_pos = kp_ref[kc]
                visible = (key_pos <= query_pos) & (key_pos >= query_lo)
                probs = jnp.where(visible, probs, 0.0)
            dv_ref[kc] += dot_nn(probs.astype(BF16), do)
            prob_grad = dot_nn(v_ref[kc], dot16)
            score_grad = (probs * (prob_grad - delta)).astype(BF16)
            dk_ref[kc] += dot_nn(score_grad, q)
            return dqt + dot_nn(kt_ref[kc], score_grad)

        dqt = jnp.zeros((HEAD_DIM, chunk), F32)
        for own in range(per):
            dqt = step(t * per + own, dqt, True)
        dqt = lax.fori_loop(lo_ref[t], mid_ref[t], lambda i, s: step(i, s, True), dqt)
        dqt = in_pairs(mid_ref[t], t * per, lambda i, s: step(i, s, False), dqt)
        parts.append(rope_t(dqt * scaling, cos_ref[index], -sin_ref[index]).T)

    def store(block, u, first):
        span = block.shape[0] // sources
        here = pl.ds(pl.multiple_of(u * GROUP, GROUP), GROUP)
        block = block.astype(BF16)
        total = jnp.sum(block.astype(F32), axis=0, keepdims=True)
        if first:
            sum_ref[1:2, :] += total[:, :HEAD_DIM]
            sum_ref[2:3, :] += total[:, HEAD_DIM:]
        else:
            sum_ref[0:1, :] += total
        for i, ref in enumerate(out_refs):
            part = block[i * span : (i + 1) * span]
            half = ref.shape[0]
            shape = (half, GROUP, HEAD_DIM)
            for side in range(2):
                one = part[side * half * GROUP : (side + 1) * half * GROUP, :HEAD_DIM]
                ref[:, side, here, first : first + HEAD_DIM] = one.reshape(shape)
            if first:
                both = side_by_side(part[:, HEAD_DIM:])
                ref[:, 2, here, :] = both.reshape(half, GROUP, 2 * HEAD_DIM)

    @pl.when(t == 0)
    def _():
        sum_ref[...] = jnp.zeros_like(sum_ref)

    store(parts[0] if per == 1 else jnp.concatenate(parts, axis=0), t, 0)

    @pl.when(t == pl.num_programs(0) - 1)
    def _():
        def finish(u, carry):
            found = []
            for c in range(per):
                index = u * per + c
                dkt = rope_t(dk_ref[index].T * scaling, cos_ref[index], -sin_ref[index])
                found.append(jnp.concatenate([dkt.T, dv_ref[index]], axis=1))
            store(found[0] if per == 1 else jnp.concatenate(found, axis=0), u, HEAD_DIM)
            return carry

        lax.fori_loop(0, pl.num_programs(0), finish, 0)


def attention_meta(positions, seq_lengths, chunk):
    tiles, tile = positions.shape
    count = tiles * tile // chunk
    per = tile // chunk
    opening = opening_of(positions, seq_lengths)
    frequency = 10000.0 ** (-2.0 * jnp.arange(ROT // 2, dtype=F32) / ROT)
    angles = (positions - opening).astype(F32).reshape(count, 1, chunk) * frequency[None, :, None]
    ends = jnp.arange(tiles, dtype=jnp.int32) * tile
    first_open = opening_of(ends, seq_lengths)
    last_open = opening_of(ends + tile - 1, seq_lengths)
    own = jnp.arange(tiles, dtype=jnp.int32) * per
    low = (first_open // tile) * per
    middle = jnp.minimum(((last_open + tile - 1) // tile) * per, own)
    return dict(
        low=low.astype(jnp.int32),
        middle=middle.astype(jnp.int32),
        cosine=jnp.cos(angles),
        sine=jnp.sin(angles),
        query_pos=positions.reshape(count, 1, chunk),
        query_lo=opening.reshape(count, 1, chunk),
        key_pos=positions.reshape(count, chunk, 1),
    )


def attention_forward(parts, meta):
    sources = len(parts)
    half, _, rows, lanes = parts[0].shape
    tile = sources * 2 * half * GROUP
    tiles = rows // GROUP
    count, _, chunk = meta["query_pos"].shape
    per = tile // chunk
    nat = jax.ShapeDtypeStruct((count, chunk, HEAD_DIM), BF16)
    turned = jax.ShapeDtypeStruct((count, HEAD_DIM, chunk), BF16)
    out = jax.ShapeDtypeStruct((half, rows, lanes), BF16)
    found = pl.pallas_call(
        lambda *refs: forward_kernel(sources, *refs),
        out_shape=[out] * sources
        + [
            jax.ShapeDtypeStruct((count, HEAD_DIM, chunk), F32),
            jax.ShapeDtypeStruct((count, 1, chunk), F32),
            nat, nat, nat, turned, turned,
        ],
        grid_spec=pltpu.PrefetchScalarGridSpec(
            num_scalar_prefetch=2,
            grid=(tiles,),
            in_specs=[tile_block((half, 3, GROUP, lanes), 2)] * sources
            + [
                tile_block((per, 1, chunk), 0),
                tile_block((per, 1, chunk), 0),
                whole_block((count, chunk, 1)),
            ],
            out_specs=[tile_block((half, GROUP, lanes), 1)] * sources
            + [
                tile_block((per, HEAD_DIM, chunk), 0),
                tile_block((per, 1, chunk), 0),
                whole_block(nat.shape),
                whole_block(nat.shape),
                whole_block(nat.shape),
                whole_block(turned.shape),
                whole_block(turned.shape),
            ],
            scratch_shapes=[pltpu.VMEM(turned.shape, BF16)],
        ),
        compiler_params=pltpu.CompilerParams(
            dimension_semantics=("arbitrary",), vmem_limit_bytes=58 * 1024 * 1024
        ),
        cost_estimate=LARGE,
        name="attention_forward",
    )(
        meta["low"], meta["middle"], *parts,
        meta["query_pos"], meta["query_lo"], meta["key_pos"],
    )
    return found[:sources], found[sources:]


def attention_backward(grads, meta, saved):
    sources = len(grads)
    half, rows, lanes = grads[0].shape
    tile = sources * 2 * half * GROUP
    tiles = rows // GROUP
    count, _, chunk = meta["query_pos"].shape
    per = tile // chunk
    turn = ROT // 2
    out = jax.ShapeDtypeStruct((half, 3, rows, lanes), BF16)
    ot, lse, q, k, v, qt, kt = saved
    found = pl.pallas_call(
        lambda *refs: backward_kernel(sources, *refs),
        out_shape=[out] * sources + [jax.ShapeDtypeStruct((3, HEAD_DIM), F32)],
        grid_spec=pltpu.PrefetchScalarGridSpec(
            num_scalar_prefetch=2,
            grid=(tiles,),
            in_specs=[tile_block((half, GROUP, lanes), 1)] * sources
            + [
                whole_block((count, turn, chunk)),
                whole_block((count, turn, chunk)),
                tile_block((per, 1, chunk), 0),
                tile_block((per, 1, chunk), 0),
                whole_block((count, chunk, 1)),
                tile_block((per, HEAD_DIM, chunk), 0),
                tile_block((per, 1, chunk), 0),
                whole_block(q.shape),
                whole_block(k.shape),
                whole_block(v.shape),
                whole_block(qt.shape),
                whole_block(kt.shape),
            ],
            out_specs=[whole_block(out.shape)] * sources + [whole_block((3, HEAD_DIM))],
            scratch_shapes=[
                pltpu.VMEM((count, chunk, HEAD_DIM), F32),
                pltpu.VMEM((count, chunk, HEAD_DIM), F32),
            ],
        ),
        compiler_params=pltpu.CompilerParams(
            dimension_semantics=("arbitrary",), vmem_limit_bytes=62 * 1024 * 1024
        ),
        cost_estimate=BROAD,
        name="attention_backward",
    )(
        meta["low"], meta["middle"], *grads, meta["cosine"], meta["sine"],
        meta["query_pos"], meta["query_lo"], meta["key_pos"], ot, lse, q, k, v, qt, kt,
    )
    return list(found[:sources]), found[sources]


def doubled(block, masks, count):
    held = block[None]
    for mask in masks:
        held = jnp.concatenate([held, swap(held, mask, count)], axis=0)
    return held


def halved(block, masks, count):
    for mask in masks[::-1]:
        middle = block.shape[0] // 2
        block = block[:middle] + swap(block[middle:], mask, count)
    return block[0]


def gather_list(block, masks, count):
    held = [block]
    for mask in masks:
        held = held + [swap(h, mask, count) for h in held]
    return held


def exchange(parts, masks, count):
    return [part if m == 0 else swap(part, m, count) for part, m in zip(parts, masks)]


def pick(block, axis, index):
    return lax.dynamic_index_in_dim(block, index, axis, False)


def gelu_tanh(values):
    return jax.nn.gelu(values, approximate=True)


def hop_kernel(pieces, *refs):
    refs = refs[2 * pieces :]
    outs = refs[4 * pieces :]
    for i in range(pieces):
        a_ref, b_ref, c_ref, d_ref = refs[4 * i : 4 * i + 4]
        out_ref, own_ref = outs[2 * i : 2 * i + 2]
        out_ref[...] = (a_ref[...].astype(F32) + b_ref[...].astype(F32)).astype(BF16)
        own_ref[...] = c_ref[...].astype(F32) + d_ref[...].astype(F32)


def hop(kept, there, masks, left_bits, my_blk, cost):
    pieces = len(kept)
    count, _, width = kept[0].shape
    picks, in_specs, out_specs, shapes, operands = [], [], [], [], []
    for i in range(pieces):
        numbers = jnp.arange(count, dtype=jnp.int32).reshape((2,) * len(left_bits[i]))
        axis = left_bits[i].index(masks[i])
        mine = (my_blk // masks[i]) % 2
        picks += [pick(numbers, axis, 1 - mine).reshape(-1), pick(numbers, axis, mine).reshape(-1)]
        rows = kept[i].shape[1]
        block = (1, rows, width)
        far = pl.BlockSpec(block, lambda t, *at, i=i: (at[2 * i][t], 0, 0))
        near = pl.BlockSpec(block, lambda t, *at, i=i: (at[2 * i + 1][t], 0, 0))
        in_specs += [far, far, near, near]
        operands += [kept[i], there[i], kept[i], there[i]]
        out_specs += [pl.BlockSpec(block, lambda t, *at: (t, 0, 0))] * 2
        shape = (count // 2, rows, width)
        shapes += [jax.ShapeDtypeStruct(shape, BF16), jax.ShapeDtypeStruct(shape, F32)]
    found = pl.pallas_call(
        lambda *refs: hop_kernel(pieces, *refs),
        out_shape=shapes,
        grid_spec=pltpu.PrefetchScalarGridSpec(
            num_scalar_prefetch=2 * pieces,
            grid=(count // 2,),
            in_specs=in_specs,
            out_specs=out_specs,
        ),
        compiler_params=kernel_params(62),
        cost_estimate=cost,
        name="hop",
    )(*picks, *operands)
    return found[0::2], found[1::2]


def per_device(
    layer_in, out_grad, norm_gain, norm_bias, w_qkv, b_qkv, w_out, b_out, w_up, b_up,
    w_down, b_down, seq_lengths, token_place,
):
    heads, blks = lax.axis_size("head"), lax.axis_size("blk")
    count = heads * blks
    my_head, my_blk = lax.axis_index("head"), lax.axis_index("blk")
    me = my_head * blks + my_blk
    rows, width = layer_in.shape
    features = w_qkv.shape[1]
    units = w_up.shape[0]
    owners = HEAD_DIM // features
    member = me % owners
    blk_bits = [1 << i for i in range(blks.bit_length() - 1)][::-1]
    head_bits = [blks << i for i in range(heads.bit_length() - 1)][::-1]
    head_masks = slot_masks(head_bits)
    numbers = jnp.arange(count, dtype=jnp.int32)

    place = token_place.reshape(count, rows)
    ranks = place // count
    row_numbers = jnp.arange(rows, dtype=jnp.int32)
    x_sorted, order_hot = sort_rows(layer_in, token_place, me, count)
    x_all = lax.all_gather(x_sorted, "blk", axis=0, tiled=True)
    g_sorted = dot_nn(order_hot, out_grad).astype(BF16)

    qkv_full, out_full, bias_full = w_qkv, w_out, b_qkv
    if owners > 1:
        order = member ^ jnp.arange(owners, dtype=jnp.int32)

        def of_owners(block):
            found = [block] + [swap(block, e, count) for e in range(1, owners)]
            return jnp.stack(found)[order]

        qkv_full = jnp.moveaxis(of_owners(w_qkv), 0, 1).reshape(3, HEAD_DIM, width)
        bias_full = jnp.moveaxis(of_owners(b_qkv), 0, 1).reshape(3, HEAD_DIM)
        out_full = of_owners(w_out).reshape(HEAD_DIM, width)
    qkv_cut, lanes = 3 * HEAD_DIM, 2 * HEAD_DIM

    def all_heads(own, token=None):
        over = swap(own, head_bits[0], count)
        found = [own, over if token is None else after(over, token)]
        for bit in head_bits[1:]:
            found = found + [swap(w, bit, count) for w in found]
        return found

    vectors = jnp.stack([norm_gain, norm_bias, b_out, b_down])
    bias_row = jnp.concatenate([bias_full.reshape(-1), b_up])
    piece = vectors.size
    tile = jnp.zeros((16, width), BF16)
    tile = tile.at[0, : qkv_cut + units].set(bias_row).at[1, :piece].set(vectors.reshape(-1))
    w_list = all_heads(jnp.concatenate([qkv_full.reshape(qkv_cut, width), tile], axis=0))
    g_all = lax.all_gather(after(g_sorted, w_list[1]), "blk", axis=0, tiled=True)
    biases = jnp.stack([w[qkv_cut, : qkv_cut + units] for w in w_list]).astype(F32)

    vectors = jnp.stack([w[qkv_cut + 1, :piece].reshape(vectors.shape) for w in w_list])
    for mask in blk_bits:
        vectors = jnp.concatenate([vectors, swap(vectors, mask, count)], axis=0)
    absolute = me ^ jnp.array(slot_masks(head_bits + blk_bits), dtype=jnp.int32)
    choose = (absolute[None, :] == numbers[:, None]).astype(BF16)
    vectors = dot_nn(choose, vectors.reshape(count, -1)).reshape(count, 4, -1)
    vectors = jnp.transpose(vectors, (1, 0, 2)).reshape(4, width)
    gain, offset, out_bias, down_bias = (vectors[i][None] for i in range(4))

    up_list = all_heads(w_up, vectors)
    qkv_rows, qkv_turned = join(
        w_list,
        [
            [(r, 0, lanes, r * lanes) for r in range(heads)]
            + [(r, lanes, HEAD_DIM, heads * lanes + r * HEAD_DIM) for r in range(heads)]
        ],
        vectors,
        True,
    )
    qkv_bias = jnp.concatenate(
        [biases[:, :lanes].reshape(1, -1), biases[:, lanes:qkv_cut].reshape(1, -1)], axis=1
    )
    up_bias = biases[:, qkv_cut:].reshape(1, -1)

    sorted_place = jnp.sum(
        jnp.where(ranks[:, None, :] == row_numbers[None, :, None], place[:, None, :], 0), axis=2
    )
    slot_head = my_head ^ jnp.array([m // blks for m in head_masks], dtype=jnp.int32)
    device = (slot_head[:, None] * blks + jnp.arange(blks, dtype=jnp.int32)[None, :]).reshape(-1)
    chosen = jnp.where((device[:, None] == numbers[None, :])[:, :, None], sorted_place[None], 0)
    positions = jnp.sum(chosen, axis=1)
    own_positions = positions[:blks].reshape(-1)
    own_place = own_positions - opening_of(own_positions, seq_lengths)
    tiles = rows // GROUP
    positions = jnp.transpose(positions.reshape(count, tiles, GROUP), (1, 0, 2))
    positions = positions.reshape(tiles, count * GROUP)
    meta = attention_meta(positions, seq_lengths, min(CHUNK, count * GROUP))

    (up_rows,) = join(
        up_list, [[(r, 0, units, r * units) for r in range(heads)]], vectors
    )
    x_all = after(x_all, up_rows)
    normed, center, inverse, qkv = project(
        x_all, gain, offset, qkv_turned, qkv_bias, own_place, heads, blks
    )
    qkv_made = qkv[0]
    qkv = exchange(qkv, head_masks, count)
    w_back_list = all_heads(jnp.concatenate([w_down, out_full], axis=0), qkv_made)

    down_rows, out_rows, down_turned = join(
        w_back_list,
        [
            [(r, 0, units, r * units) for r in range(heads)],
            [(r, units, HEAD_DIM, r * HEAD_DIM) for r in range(heads)],
        ],
        qkv_made,
        True,
    )
    hidden = dot_nt(normed, up_rows) + up_bias
    active = gelu_tanh(hidden).astype(BF16)
    meta["low"] = after(meta["low"], active, meta["sine"], meta["cosine"])
    attended, saved = attention_forward(qkv, meta)
    def flat(block):
        return block.reshape(-1, block.shape[-1])

    def own_features(part):
        if owners == 1:
            return part
        mine = jnp.arange(lanes, dtype=jnp.int32) % HEAD_DIM // features == member
        return jnp.where(mine, part, 0)

    def packed(part):
        part = part.reshape(2, blks // 2, rows, HEAD_DIM)
        return jnp.concatenate([part[0], part[1]], axis=-1)

    attended_here = attended[0]
    attended = exchange(attended, head_masks, count)
    attended = [own_features(part) for part in attended]
    mixed = mixed_rows(active, attended, down_rows, out_rows)
    g_late = after(g_all, attended_here)

    heads_grad = dot_nt(g_late, out_rows).astype(BF16)
    heads_grad = [packed(heads_grad[:, r * HEAD_DIM : (r + 1) * HEAD_DIM]) for r in range(heads)]
    mine, others = list(range(heads // 2)), list(range(heads // 2, heads))
    back_sent = outer(attended, active, g_late, others, units, heads_grad[0])
    back_there = [swap(part, head_bits[-1], count) for part in back_sent]
    back_sent = back_sent[0]
    heads_grad = exchange(heads_grad, head_masks, count)
    heads_grad[0] = after(heads_grad[0], back_sent, mixed)
    mixed = mixed.reshape(blks, rows, width)
    mixed = lax.psum_scatter(mixed, "blk", scatter_dimension=0, tiled=False)

    qkv_grad, qkv_sums = attention_backward(heads_grad, meta, saved)
    g_last = after(g_late, qkv_grad[0])
    qkv_grad = [own_features(part) for part in exchange(qkv_grad, head_masks, count)]
    hidden_grad, up_sums = hidden_grads(g_last, hidden, down_turned, g_last)

    pieces = pieces_of(blks, rows)
    split_shape = (2,) * len(blk_bits)
    slots = jnp.arange(blks, dtype=jnp.int32).reshape(split_shape)
    parts = [(blks // 2, begin, end) for (begin, end), _ in pieces]

    def halves(block, far):
        found = []
        for (begin, end), order in pieces:
            axis = blk_bits.index(order[0])
            mine = (my_blk // order[0]) % 2
            piece = block if block.ndim == len(blk_bits) else block[..., begin:end, :]
            found.append(pick(piece, axis, 1 - mine if far else mine))
        return found

    hid_rows = hidden_grad.reshape(blks, rows, heads * units)

    chosen = jnp.concatenate([p.reshape(-1) for p in halves(slots, True) + halves(slots, False)])
    found = shifted(
        hid_rows, qkv_grad, up_rows, qkv_rows, chosen, parts + parts, hidden_grad
    )
    sent, kept = found[: len(parts)], found[len(parts) :]
    back_own, back_far = outer(attended, active, g_last, mine, units, kept[0], back_there)
    back_there = swap(back_far, head_bits[0], count)
    in_sent = outer(qkv_grad, hidden_grad, normed, others, units, back_far)
    in_there = [swap(part, head_bits[-1], count) for part in in_sent]
    in_sent = in_sent[0]
    orders = [order for _, order in pieces]
    norm_grads = norm_sums(
        after(x_all, in_sent).reshape(blks, rows, width),
        center.reshape(blks, rows, 1),
        inverse.reshape(blks, rows, 1),
        list(sent) + list(kept),
        chosen,
        parts + parts,
    )
    own_g = g_sorted.astype(F32)
    sums = jnp.concatenate([norm_grads, jnp.sum(own_g, axis=0)[None]], axis=0)
    sums = jnp.transpose(sums.reshape(3, heads, blks, -1), (2, 1, 0, 3)).reshape(blks, -1)
    relative = jnp.array(slot_masks(blk_bits), dtype=jnp.int32) ^ my_blk
    reached = relative[:, None] == slots.reshape(1, -1)
    reached = jnp.sum(jnp.where(reached[:, :, None], sums[None], 0.0), axis=1)
    kept = [after(kept[0], reached, mixed), kept[1]]
    there = [swap(sent[i], order[0], count) for i, order in enumerate(orders)]
    left = [[b for b in blk_bits if b != order[0]] for order in orders]
    for step in range(1, len(blk_bits)):
        masks = [order[step] for order in orders]
        far, kept = hop(kept, there, masks, left, my_blk, LARGE if step == 1 else LAST)
        there = [swap(f, mask, count) for f, mask in zip(far, masks)]
        left = [[b for b in bits if b != mask] for bits, mask in zip(left, masks)]
        last_far = far[0]
        if step == 1:
            in_own, in_far = outer(qkv_grad, hidden_grad, normed, mine, units, kept[0], in_there)
            in_there = swap(in_far, head_bits[0], count)
            reached = after(reached, in_far, back_there)
            near, away = jnp.split(reached, 2)
            for mask in blk_bits[::-1][:-1]:
                near, away = fold(near, swap(away, mask, count))
            kept = [after(kept[0], in_far, near), kept[1]]

    layer_out = layer_rows(
        x_sorted, mixed, jnp.concatenate([out_bias, down_bias], axis=0), order_hot, last_far
    )
    w_down_grad, w_out_grad = totals(back_own, back_there, units, last_far)
    w_up_grad, w_qkv_grad = totals(in_own, in_there, units, last_far)
    w_qkv_grad = w_qkv_grad.reshape(3, owners, features, width)
    w_qkv_grad = lax.dynamic_index_in_dim(w_qkv_grad, member, 1, False)
    w_out_grad = w_out_grad.reshape(owners, features, width)
    w_out_grad = lax.dynamic_index_in_dim(w_out_grad, member, 0, False)
    qkv_sums = qkv_sums.reshape(3, owners, features)
    b_qkv_grad = lax.dynamic_index_in_dim(qkv_sums, member, 1, False)

    away = after(away, last_far)
    sums = near[0] + swap(away, blk_bits[0], count)[0]
    sums = sums.reshape(heads, -1)
    slot_numbers = jnp.arange(heads, dtype=jnp.int32)
    reached = jnp.where((slot_head[:, None] == slot_numbers[None])[:, :, None], sums[None], 0.0)
    small = jnp.concatenate([jnp.sum(reached, axis=1), up_sums.reshape(heads, units)], axis=1)
    small = exchange([small[r : r + 1] for r in range(heads)], head_masks, count)

    input_grad = input_rows(x_sorted, g_sorted, gain, order_hot, kept, there)
    small = added(small, input_grad)[0]
    vector_grads, b_up_grad = small[:-units].reshape(3, -1), small[-units:]
    return (
        layer_out,
        input_grad,
        vector_grads[0],
        vector_grads[1],
        w_qkv_grad,
        b_qkv_grad,
        w_out_grad,
        vector_grads[2],
        w_up_grad,
        b_up_grad,
        w_down_grad,
        vector_grads[2],
    )


def solution(mesh):
    rows, vector = P(AXES, None), P(AXES)
    qkv, qkv_bias = P(None, AXES, None), P(None, AXES)
    in_specs = (
        rows, rows, vector, vector, qkv, qkv_bias, rows, vector, rows, vector, rows, vector,
        P(), P(),
    )
    out_specs = (
        rows, rows, vector, vector, qkv, qkv_bias, rows, vector, rows, vector, rows, vector,
    )
    return jax.shard_map(
        per_device, mesh=mesh, in_specs=in_specs, out_specs=out_specs, check_vma=False
    )
```

```python
import jax
import jax.numpy as jnp
from jax import lax
from jax.experimental import pallas as pl
from jax.experimental.pallas import tpu as pltpu
from jax.sharding import PartitionSpec as P

HEAD_DIM = 64
ROT = 32
AXES = ("head", "blk")
GROUP = 16
CHUNK = 512
NEG = -1e30
F32 = jnp.float32
BF16 = jnp.bfloat16
SMALL = pl.CostEstimate(flops=1, bytes_accessed=1, transcendentals=0)
MIDDLE = pl.CostEstimate(flops=5_000_000_000, bytes_accessed=1_000_000, transcendentals=0)
BROAD = pl.CostEstimate(flops=34_000_000_000, bytes_accessed=1_000_000, transcendentals=0)
LAST = pl.CostEstimate(flops=6_000_000_000, bytes_accessed=1_000_000, transcendentals=0)
LARGE = pl.CostEstimate(flops=120_000_000_000, bytes_accessed=1_000_000, transcendentals=0)


def swap(block, mask, count):
    return lax.ppermute(block, AXES, [(i, i ^ mask) for i in range(count)])


def dot_nn(a, b):
    return lax.dot_general(a, b, (((1,), (0,)), ((), ())), preferred_element_type=F32)


def dot_nt(a, b):
    return lax.dot_general(a, b, (((1,), (1,)), ((), ())), preferred_element_type=F32)


def dot_tn(a, b):
    return lax.dot_general(a, b, (((0,), (0,)), ((), ())), preferred_element_type=F32)


def opening_of(packed, lengths):
    starts = jnp.cumsum(lengths) - lengths
    inside = packed[..., None] >= starts
    return jnp.max(jnp.where(inside, starts, 0), axis=-1)


def pieces_of(blks, rows):
    bits = [1 << i for i in range(blks.bit_length() - 1)]
    half = rows * 5 // 8
    return [((0, half), bits), ((half, rows), bits[1:] + bits[:1])]


def slot_masks(order):
    masks = [0]
    for mask in order:
        masks = masks + [m ^ mask for m in masks]
    return masks


def after_kernel(*refs):
    pass


def after(value, *others):
    anywhere = pl.BlockSpec(memory_space=pl.ANY)
    return pl.pallas_call(
        after_kernel,
        out_shape=jax.ShapeDtypeStruct(value.shape, value.dtype),
        in_specs=[anywhere] * (1 + len(others)),
        out_specs=anywhere,
        input_output_aliases={0: 0},
        compiler_params=pltpu.CompilerParams(vmem_limit_bytes=60 * 1024 * 1024),
        cost_estimate=SMALL,
        name="after",
    )(value, *others)


def whole_block(shape):
    zeros = (0,) * len(shape)
    return pl.BlockSpec(tuple(shape), lambda t, *refs: zeros)


def tile_block(shape, axis):
    def place(t, *refs):
        return tuple(t if i == axis else 0 for i in range(len(shape)))

    return pl.BlockSpec(tuple(shape), place)


def kernel_params(megabytes):
    return pltpu.CompilerParams(
        dimension_semantics=("arbitrary",), vmem_limit_bytes=megabytes * 1024 * 1024
    )


def join_kernel(plans, turned, count, *refs):
    blocks, out_refs = refs[:count], refs[count + 1 :]
    for plan, out_ref in zip(plans, out_refs):
        for which, start, size, to in plan:
            out_ref[to : to + size] = blocks[which][start : start + size]
    if turned:
        for which, start, size, to in plans[0]:
            out_refs[-1][:, to : to + size] = blocks[which][start : start + size].T


def join(blocks, plans, token, turned=False):
    width = blocks[0].shape[1]
    shapes = [(sum(size for _, _, size, _ in plan), width) for plan in plans]
    if turned:
        shapes.append(shapes[0][::-1])
    return pl.pallas_call(
        lambda *refs: join_kernel(plans, turned, len(blocks), *refs),
        out_shape=[jax.ShapeDtypeStruct(shape, BF16) for shape in shapes],
        grid=(1,),
        in_specs=[whole_block(b.shape) for b in blocks] + [pl.BlockSpec(memory_space=pl.ANY)],
        out_specs=[whole_block(shape) for shape in shapes],
        compiler_params=kernel_params(56),
        cost_estimate=SMALL,
        name="join",
    )(*blocks, token)


def sort_kernel(count, me_ref, place_ref, rows_ref, sorted_ref, hot_ref):
    size = rows_ref.shape[0]
    ranks = lax.div(place_ref[0], jnp.int32(count))
    numbers = lax.broadcasted_iota(jnp.int32, (size, size), 0)
    hot = jnp.where(ranks == numbers, 1.0, 0.0).astype(BF16)
    hot_ref[...] = hot
    sorted_ref[...] = dot_nn(hot, rows_ref[...]).astype(BF16)


def sort_rows(rows, token_place, me, count):
    size, width = rows.shape
    return pl.pallas_call(
        lambda *refs: sort_kernel(count, *refs),
        out_shape=[
            jax.ShapeDtypeStruct((size, width), BF16),
            jax.ShapeDtypeStruct((size, size), BF16),
        ],
        grid_spec=pltpu.PrefetchScalarGridSpec(
            num_scalar_prefetch=1,
            grid=(1,),
            in_specs=[
                pl.BlockSpec((1, 1, size), lambda t, at: (at[0], 0, 0)),
                whole_block((size, width)),
            ],
            out_specs=[whole_block((size, width)), whole_block((size, size))],
        ),
        compiler_params=kernel_params(62),
        cost_estimate=SMALL,
        name="sort_rows",
    )(me.reshape(1).astype(jnp.int32), token_place.reshape(count, 1, size), rows)


def project_kernel(heads, *refs):
    x_ref, gain_ref, offset_ref, w_ref, bias_ref, cos_ref, up_ref, down_ref = refs[:8]
    normed_ref, mean_ref, inverse_ref = refs[8:11]
    out_refs = refs[11:]
    _, _, size, width = x_ref.shape
    lanes = cos_ref.shape[3]
    half = ROT // 2
    span = heads * lanes
    x = x_ref[...].reshape(2 * size, width).astype(F32)
    mean = jnp.mean(x, axis=1, keepdims=True)
    centered = x - mean
    inverse = lax.rsqrt(jnp.mean(centered * centered, axis=1, keepdims=True) + 1e-05)
    normed = (centered * inverse * gain_ref[...] + offset_ref[...]).astype(BF16)
    normed_ref[...] = normed.reshape(normed_ref.shape)
    mean_ref[...] = mean.reshape(mean_ref.shape)
    inverse_ref[...] = inverse.reshape(inverse_ref.shape)
    z_both = dot_nn(normed, w_ref[...]) + bias_ref[...]
    values = []
    for side in range(2):
        z = z_both[side * size : (side + 1) * size]
        for r in range(heads):
            u = z[:, r * lanes : (r + 1) * lanes]
            u = (
                u * cos_ref[side, 0]
                + pltpu.roll(u, lanes - half, 1) * up_ref[side, 0]
                + pltpu.roll(u, half, 1) * down_ref[side, 0]
            )
            out_refs[r][0, side] = u.astype(BF16)
        values.append(z[:, span:])
    for r in range(heads):
        at = slice(r * HEAD_DIM, (r + 1) * HEAD_DIM)
        both = jnp.concatenate([values[0][:, at], values[1][:, at]], axis=1)
        out_refs[r][0, 2] = both.astype(BF16)


def project(x_all, gain, offset, w_turned, bias, place, heads, blks):
    rows, width = x_all.shape
    depth = w_turned.shape[1]
    lanes = 2 * HEAD_DIM
    size = rows // blks
    lane = jnp.arange(lanes, dtype=jnp.int32) % HEAD_DIM
    half = ROT // 2
    frequency = 10000.0 ** (-2.0 * (lane % half).astype(F32) / ROT)
    angles = place.astype(F32)[:, None] * frequency[None, :]
    cosine = jnp.where(lane < ROT, jnp.cos(angles), 1.0)
    sine = jnp.sin(angles)
    up = jnp.where(lane < half, -sine, 0.0)
    down = jnp.where((lane >= half) & (lane < ROT), sine, 0.0)
    shape = (2, blks // 2, size)
    strip = tile_block((2, 1, size, width), 1)
    column = tile_block((2, 1, size, 1), 1)
    table = tile_block((2, 1, size, lanes), 1)
    found = pl.pallas_call(
        lambda *refs: project_kernel(heads, *refs),
        out_shape=[
            jax.ShapeDtypeStruct(shape + (width,), BF16),
            jax.ShapeDtypeStruct(shape + (1,), F32),
            jax.ShapeDtypeStruct(shape + (1,), F32),
        ]
        + [jax.ShapeDtypeStruct((blks // 2, 3, size, lanes), BF16)] * heads,
        grid=(blks // 2,),
        in_specs=[
            strip,
            whole_block((1, width)),
            whole_block((1, width)),
            whole_block((width, depth)),
            whole_block((1, depth)),
            table, table, table,
        ],
        out_specs=[strip, column, column] + [tile_block((1, 3, size, lanes), 0)] * heads,
        compiler_params=kernel_params(56),
        cost_estimate=BROAD,
        name="project",
    )(
        x_all.reshape(shape + (width,)), gain, offset, w_turned, bias,
        *[t.reshape(shape + (lanes,)) for t in (cosine, up, down)],
    )
    return found[0].reshape(rows, width), found[1], found[2], found[3:]


def mixed_kernel(heads, *refs):
    act_ref, down_ref, out_w_ref = refs[:3]
    att_refs, out_ref, left_ref = refs[3 : 3 + heads], refs[-2], refs[-1]

    @pl.when(pl.program_id(0) == 0)
    def _():
        parts = [pair_rows(a[...]) for a in att_refs]
        left_ref[...] = jnp.concatenate(parts, axis=1)

    total = dot_nn(act_ref[...], down_ref[...]) + dot_nn(left_ref[...], out_w_ref[...])
    out_ref[...] = total.astype(BF16)


def mixed_rows(active, attended, down_rows, out_rows):
    heads = len(attended)
    rows, span = active.shape
    width = down_rows.shape[1]
    block = 512
    return pl.pallas_call(
        lambda *refs: mixed_kernel(heads, *refs),
        out_shape=jax.ShapeDtypeStruct((rows, width), BF16),
        grid=(width // block,),
        in_specs=[
            whole_block(active.shape),
            tile_block((span, block), 1),
            tile_block((out_rows.shape[0], block), 1),
        ]
        + [whole_block(a.shape) for a in attended],
        out_specs=tile_block((rows, block), 1),
        scratch_shapes=[pltpu.VMEM((rows, heads * HEAD_DIM), BF16)],
        compiler_params=kernel_params(58),
        cost_estimate=SMALL,
        name="mixed",
    )(active, down_rows, out_rows, *attended)


GELU_ROOT = 0.7978845608028654
GELU_CUBE = 0.044715


def hidden_grad_kernel(g_ref, hidden_ref, down_ref, token_ref, grad_ref, sum_ref):
    h = hidden_ref[...]
    square = h * h
    bent = jnp.tanh(GELU_ROOT * (h + GELU_CUBE * (square * h)))
    slope = 0.5 * (1.0 + bent) + (0.5 * GELU_ROOT) * h * (1.0 - bent * bent) * (
        1.0 + (3.0 * GELU_CUBE) * square
    )
    grad = (dot_nn(g_ref[...], down_ref[...]) * slope).astype(BF16)
    grad_ref[...] = grad
    sum_ref[...] = jnp.sum(grad.astype(F32), axis=0, keepdims=True)


def hidden_grads(g_all, hidden, down_turned, token):
    rows, width = g_all.shape
    span = hidden.shape[1]
    block = min(256, span)
    size = min(1024, rows)
    found = pl.pallas_call(
        hidden_grad_kernel,
        out_shape=[
            jax.ShapeDtypeStruct((rows, span), BF16),
            jax.ShapeDtypeStruct((rows // size, 1, span), F32),
        ],
        grid=(rows // size, span // block),
        in_specs=[
            pl.BlockSpec((size, width), lambda i, j: (i, 0)),
            pl.BlockSpec((size, block), lambda i, j: (i, j)),
            pl.BlockSpec((width, block), lambda i, j: (0, j)),
            pl.BlockSpec(memory_space=pl.ANY),
        ],
        out_specs=[
            pl.BlockSpec((size, block), lambda i, j: (i, j)),
            pl.BlockSpec((None, 1, block), lambda i, j: (i, 0, j)),
        ],
        compiler_params=pltpu.CompilerParams(
            dimension_semantics=("arbitrary", "arbitrary"), vmem_limit_bytes=48 * 1024 * 1024
        ),
        cost_estimate=SMALL,
        name="hidden_grad",
    )(g_all, hidden, down_turned, token)
    return found[0], jnp.sum(found[1], axis=(0, 1))


def shifted_kernel(heads, parts, slots_ref, *refs):
    hid_ref, up_ref, w_ref = refs[:3]
    qkv_refs, out_refs, left_ref = refs[3 : 3 + heads], refs[4 + heads : -1], refs[-1]
    half, _, _, lanes = qkv_refs[0].shape
    units = hid_ref.shape[2]
    span = units + heads * lanes

    @pl.when(pl.program_id(0) == 0)
    def _():
        at, number = 0, 0
        for count, begin, end in parts:
            for i in range(count):
                slot = slots_ref[number]
                number += 1
                side = slot // half
                group = slot - side * half
                rows = slice(at, at + end - begin)
                at += end - begin
                left_ref[rows, :units] = hid_ref[slot, begin:end, :]
                values = []
                for r in range(heads):
                    to = units + r * lanes
                    left_ref[rows, to : to + lanes] = qkv_refs[r][group, side, begin:end, :]
                    both = qkv_refs[r][group, 2, begin:end, :]
                    values.append(jnp.where(side == 0, both[:, :HEAD_DIM], both[:, HEAD_DIM:]))
                left_ref[rows, span:] = jnp.concatenate(values, axis=1)

    total = dot_nn(left_ref[:, :units], up_ref[...]) + dot_nn(left_ref[:, units:], w_ref[...])
    at = 0
    for out_ref, (count, begin, end) in zip(out_refs, parts):
        size = count * (end - begin)
        out_ref[...] = total[at : at + size].astype(BF16).reshape(out_ref.shape)
        at += size


def shifted(hid_grad, qkv_grad, up_rows, w_rows, slots, parts, token):
    heads = len(qkv_grad)
    width = up_rows.shape[1]
    total_rows = sum(n * (end - begin) for n, begin, end in parts)
    depth = up_rows.shape[0] + w_rows.shape[0]
    block = 512
    return pl.pallas_call(
        lambda *refs: shifted_kernel(heads, parts, *refs),
        out_shape=[jax.ShapeDtypeStruct((n, end - begin, width), BF16) for n, begin, end in parts],
        grid_spec=pltpu.PrefetchScalarGridSpec(
            num_scalar_prefetch=1,
            grid=(width // block,),
            in_specs=[
                whole_block(hid_grad.shape),
                tile_block((up_rows.shape[0], block), 1),
                tile_block((w_rows.shape[0], block), 1),
            ]
            + [whole_block(q.shape) for q in qkv_grad]
            + [pl.BlockSpec(memory_space=pl.ANY)],
            out_specs=[tile_block((n, end - begin, block), 2) for n, begin, end in parts],
            scratch_shapes=[pltpu.VMEM((total_rows, depth), BF16)],
        ),
        compiler_params=kernel_params(60),
        cost_estimate=MIDDLE,
        name="shifted",
    )(slots, hid_grad, up_rows, w_rows, *qkv_grad, token)


def turn_left(left_ref, owners_of, units, second_ref, first_refs):
    low, high = owners_of[0] * units, (owners_of[-1] + 1) * units
    left_ref[: high - low, :] = second_ref[:, low:high].T
    at = high - low
    cols = left_ref.shape[1] // 2
    for ref in first_refs:
        if len(ref.shape) == 4:
            half, _, rows, lanes = ref.shape
            for side in range(2):
                block = ref[:, side].reshape(half * rows, lanes).T
                left_ref[at : at + lanes, side * cols : (side + 1) * cols] = block
            at += lanes
            pair = ref[:, 2].reshape(half * rows, lanes).T
        else:
            half, rows, lanes = ref.shape
            pair = ref[...].reshape(half * rows, lanes).T
        left_ref[at : at + HEAD_DIM, :cols] = pair[:HEAD_DIM]
        left_ref[at : at + HEAD_DIM, cols:] = pair[HEAD_DIM:]
        at += HEAD_DIM


SHARES = 4


def outer_kernel(owners_of, units, *refs):
    second_ref, right_ref = refs[:2]
    first_refs, left_ref = refs[2 : -2 - SHARES], refs[-1]
    out_refs = refs[-1 - SHARES : -1]

    @pl.when(pl.program_id(0) == 0)
    def _():
        turn_left(left_ref, owners_of, units, second_ref, first_refs)

    total = dot_nn(left_ref[...], right_ref[...]).astype(BF16)
    at = 0
    for ref in out_refs:
        ref[...] = total[at : at + ref.shape[0]]
        at += ref.shape[0]


def outer_add_kernel(owners_of, units, *refs):
    second_ref, right_ref = refs[:2]
    there_refs = refs[2 : 2 + SHARES]
    first_refs, own_ref, sent_ref, left_ref = refs[2 + SHARES : -4], refs[-3], refs[-2], refs[-1]

    @pl.when(pl.program_id(0) == 0)
    def _():
        turn_left(left_ref, owners_of, units, second_ref, first_refs)

    there = jnp.concatenate([ref[...] for ref in there_refs], axis=0)
    total = dot_nn(left_ref[...], right_ref[...]) + there.astype(F32)
    span = len(owners_of) * units
    cut = (total.shape[0] - span) // len(owners_of)
    own = len(owners_of) // 2
    low, high = own * units, span + own * cut
    own_ref[...] = jnp.concatenate([total[:low], total[span:high]], axis=0)
    sent_ref[...] = jnp.concatenate([total[low:span], total[high:]], axis=0).astype(BF16)


def outer(firsts, second, right, owners_of, units, token, there=None):
    rows, width = right.shape
    chosen = [firsts[r] for r in owners_of]
    block = min(512, width)
    cut = 3 * HEAD_DIM if len(chosen[0].shape) == 4 else HEAD_DIM
    count = len(owners_of) * (units + cut)
    strip = tile_block((count // SHARES, block), 1)
    operands, specs = [second, right], [whole_block(second.shape), tile_block((rows, block), 1)]
    if there is None:
        kernel = outer_kernel
        shapes = [jax.ShapeDtypeStruct((count // SHARES, width), BF16)] * SHARES
        out_specs = [strip] * SHARES
    else:
        kernel = outer_add_kernel
        shapes = [
            jax.ShapeDtypeStruct((count // 2, width), F32),
            jax.ShapeDtypeStruct((count // 2, width), BF16),
        ]
        out_specs = [tile_block((count // 2, block), 1)] * 2
        operands += there
        specs += [strip] * SHARES
    return pl.pallas_call(
        lambda *refs: kernel(owners_of, units, *refs),
        out_shape=shapes,
        grid=(width // block,),
        in_specs=specs
        + [whole_block(f.shape) for f in chosen]
        + [pl.BlockSpec(memory_space=pl.ANY)],
        out_specs=out_specs,
        scratch_shapes=[pltpu.VMEM((count, rows), BF16)],
        compiler_params=kernel_params(58),
        cost_estimate=SMALL,
        name="outer",
    )(*operands, *chosen, token)


def sums_kernel(parts, slots_ref, *refs):
    x_ref, mean_ref, inverse_ref = refs[:3]
    part_refs, out_ref = refs[3:-1], refs[-1]
    number = 0
    gain_sum, bias_sum = 0.0, 0.0
    for ref, (count, begin, end) in zip(part_refs, parts):
        for i in range(count):
            slot = slots_ref[number]
            number += 1
            x_hat = x_ref[slot, begin:end, :].astype(F32) - mean_ref[slot, begin:end, :]
            x_hat = x_hat * inverse_ref[slot, begin:end, :]
            part = ref[i].astype(F32)
            gain_sum += jnp.sum(part * x_hat, axis=0, keepdims=True)
            bias_sum += jnp.sum(part, axis=0, keepdims=True)
    out_ref[0:1, :] = gain_sum
    out_ref[1:2, :] = bias_sum


def norm_sums(x_all, mean, inverse, blocks, slots, parts):
    blks, rows, width = x_all.shape
    block = 512
    return pl.pallas_call(
        lambda *refs: sums_kernel(parts, *refs),
        out_shape=jax.ShapeDtypeStruct((2, width), F32),
        grid_spec=pltpu.PrefetchScalarGridSpec(
            num_scalar_prefetch=1,
            grid=(width // block,),
            in_specs=[
                tile_block((blks, rows, block), 2),
                whole_block(mean.shape),
                whole_block(inverse.shape),
            ]
            + [tile_block(b.shape[:2] + (block,), 2) for b in blocks],
            out_specs=tile_block((2, block), 1),
        ),
        compiler_params=kernel_params(56),
        cost_estimate=SMALL,
        name="norm_sums",
    )(slots, x_all, mean, inverse, *blocks)


def total_kernel(own_ref, there_ref, token_ref, top_ref, low_ref):
    cut = top_ref.shape[0]
    total = own_ref[...] + there_ref[...].astype(F32)
    top_ref[...] = total[:cut]
    low_ref[...] = total[cut:]


def totals(own, there, cut, token):
    rows, width = own.shape
    block = 512
    return pl.pallas_call(
        total_kernel,
        out_shape=[
            jax.ShapeDtypeStruct((cut, width), F32),
            jax.ShapeDtypeStruct((rows - cut, width), F32),
        ],
        grid=(width // block,),
        in_specs=[tile_block((rows, block), 1)] * 2 + [pl.BlockSpec(memory_space=pl.ANY)],
        out_specs=[tile_block((cut, block), 1), tile_block((rows - cut, block), 1)],
        compiler_params=kernel_params(32),
        cost_estimate=SMALL,
        name="totals",
    )(own, there, token)


def fold_kernel(kept_ref, there_ref, near_ref, far_ref):
    middle = near_ref.shape[0]
    total = kept_ref[...] + there_ref[...]
    near_ref[...] = total[:middle]
    far_ref[...] = total[middle:]


def fold(kept, there):
    rows, width = kept.shape
    shape = (rows // 2, width)
    return pl.pallas_call(
        fold_kernel,
        out_shape=[jax.ShapeDtypeStruct(shape, F32)] * 2,
        grid=(1,),
        in_specs=[whole_block((rows, width))] * 2,
        out_specs=[whole_block(shape)] * 2,
        compiler_params=kernel_params(16),
        cost_estimate=SMALL,
        name="fold",
    )(kept, there)


def add_kernel(count, *refs):
    total = refs[0][...]
    for ref in refs[1:count]:
        total += ref[...]
    refs[-1][...] = total


def added(parts, token):
    shape = parts[0].shape
    return pl.pallas_call(
        lambda *refs: add_kernel(len(parts), *refs),
        out_shape=jax.ShapeDtypeStruct(shape, F32),
        grid=(1,),
        in_specs=[whole_block(shape)] * len(parts) + [pl.BlockSpec(memory_space=pl.ANY)],
        out_specs=whole_block(shape),
        compiler_params=kernel_params(16),
        cost_estimate=SMALL,
        name="added",
    )(*parts, token)


def layer_out_kernel(x_ref, mixed_ref, bias_ref, hot_ref, token_ref, out_ref):
    total = x_ref[...].astype(F32) + mixed_ref[...].astype(F32) + bias_ref[0:1] + bias_ref[1:2]
    out_ref[...] = dot_tn(hot_ref[...], total.astype(BF16)).astype(BF16)


def layer_rows(x, mixed, biases, hot, token):
    operands = (x, mixed, biases, hot)
    return pl.pallas_call(
        layer_out_kernel,
        out_shape=jax.ShapeDtypeStruct(x.shape, BF16),
        grid=(1,),
        in_specs=[whole_block(o.shape) for o in operands] + [pl.BlockSpec(memory_space=pl.ANY)],
        out_specs=whole_block(x.shape),
        compiler_params=kernel_params(32),
        cost_estimate=SMALL,
        name="layer_rows",
    )(*operands, token)


def input_grad_kernel(pieces, *refs):
    x_ref, g_ref, gain_ref, hot_ref = refs[:4]
    kept_refs, there_refs, out_ref = refs[4 : 4 + pieces], refs[4 + pieces : -1], refs[-1]
    grad = jnp.concatenate(
        [k[0] + t[0].astype(F32) for k, t in zip(kept_refs, there_refs)], axis=0
    )
    x = x_ref[...].astype(F32)
    centered = x - jnp.mean(x, axis=1, keepdims=True)
    inverse = lax.rsqrt(jnp.mean(centered * centered, axis=1, keepdims=True) + 1e-05)
    x_hat = centered * inverse
    e = grad * gain_ref[...]
    part = inverse * (
        e
        - jnp.mean(e, axis=1, keepdims=True)
        - x_hat * jnp.mean(e * x_hat, axis=1, keepdims=True)
    )
    total = (g_ref[...].astype(F32) + part).astype(BF16)
    out_ref[...] = dot_tn(hot_ref[...], total).astype(BF16)


def input_rows(x, g, gain, hot, kept, there):
    operands = (x, g, gain, hot, *kept, *there)
    return pl.pallas_call(
        lambda *refs: input_grad_kernel(len(kept), *refs),
        out_shape=jax.ShapeDtypeStruct(x.shape, BF16),
        grid=(1,),
        in_specs=[whole_block(o.shape) for o in operands],
        out_specs=whole_block(x.shape),
        compiler_params=kernel_params(32),
        cost_estimate=SMALL,
        name="input_rows",
    )(*operands)


def rope_t(u, cosine, sine):
    half = ROT // 2
    top, low = u[:half], u[half:ROT]
    return jnp.concatenate(
        [top * cosine - low * sine, low * cosine + top * sine, u[ROT:]], axis=0
    )


def tall(block):
    return block.reshape(block.shape[0] * block.shape[1], block.shape[2])


def pair_rows(block):
    both = tall(block)
    return jnp.concatenate([both[:, :HEAD_DIM], both[:, HEAD_DIM:]], axis=0)


def packed_rows(refs):
    qk, v = [], []
    for ref in refs:
        qk += [tall(ref[:, 0]), tall(ref[:, 1])]
        v.append(pair_rows(ref[:, 2]))
    return jnp.concatenate(qk, axis=0), jnp.concatenate(v, axis=0)


def side_by_side(block):
    middle = block.shape[0] // 2
    return jnp.concatenate([block[:middle], block[middle:]], axis=1)


def in_pairs(first, last, step, state):
    pairs = lax.div(last - first, 2)
    state = lax.fori_loop(
        0, pairs, lambda i, s: step(first + 2 * i + 1, step(first + 2 * i, s)), state
    )
    return lax.fori_loop(first + 2 * pairs, last, step, state)


def forward_kernel(sources, *refs):
    lo_ref, mid_ref = refs[:2]
    in_refs = refs[2 : 2 + sources]
    pq_ref, lq_ref, kp_ref = refs[2 + sources : 5 + sources]
    att_refs = refs[5 + sources : 5 + 2 * sources]
    ot_ref, lse_ref, q_ref, k_ref, v_ref, qt_ref, kt_ref, vt_ref = refs[5 + 2 * sources :]
    t = pl.program_id(0)
    chunk = q_ref.shape[1]
    qk, v = packed_rows(in_refs)
    per = v.shape[0] // chunk
    for c in range(per):
        index = t * per + c
        part, values = qk[c * chunk : (c + 1) * chunk], v[c * chunk : (c + 1) * chunk]
        q_ref[index] = part[:, :HEAD_DIM]
        k_ref[index] = part[:, HEAD_DIM:]
        v_ref[index] = values
        turned = part.astype(F32).T
        qt_ref[index] = (turned[:HEAD_DIM] * HEAD_DIM**-0.5).astype(BF16)
        kt_ref[index] = turned[HEAD_DIM:].astype(BF16)
        vt_ref[index] = values.astype(F32).T.astype(BF16)
    outs = []
    for c in range(per):
        qt = qt_ref[t * per + c]
        query_pos, query_lo = pq_ref[c], lq_ref[c]

        def step(kc, state, masked):
            run_max, run_sum, acc = state
            scores = dot_nn(k_ref[kc], qt)
            if masked:
                key_pos = kp_ref[kc]
                visible = (key_pos <= query_pos) & (key_pos >= query_lo)
                scores = jnp.where(visible, scores, NEG)
            new_max = jnp.maximum(run_max, jnp.max(scores, axis=0, keepdims=True))
            weights = jnp.exp(scores - new_max)
            rescale = jnp.exp(run_max - new_max)
            run_sum = run_sum * rescale + jnp.sum(weights, axis=0, keepdims=True)
            acc = acc * rescale + dot_nn(vt_ref[kc], weights.astype(BF16))
            return new_max, run_sum, acc

        state = (
            jnp.full((1, chunk), NEG, F32),
            jnp.zeros((1, chunk), F32),
            jnp.zeros((HEAD_DIM, chunk), F32),
        )
        own = t * per + c
        state = step(own, state, True)
        state = lax.fori_loop(lo_ref[t], mid_ref[t], lambda i, s: step(i, s, True), state)
        state = in_pairs(mid_ref[t], t * per, lambda i, s: step(i, s, False), state)
        if per > 1:
            state = lax.fori_loop(t * per, own, lambda i, s: step(i, s, True), state)
            state = lax.fori_loop(own + 1, (t + 1) * per, lambda i, s: step(i, s, True), state)
        run_max, run_sum, acc = state
        out = acc / run_sum
        ot_ref[c] = out
        lse_ref[c] = run_max + jnp.log(run_sum)
        outs.append(out.T.astype(BF16))
    att = outs[0] if per == 1 else jnp.concatenate(outs, axis=0)
    span = att.shape[0] // sources
    for i, ref in enumerate(att_refs):
        ref[...] = side_by_side(att[i * span : (i + 1) * span]).reshape(ref.shape)


def backward_kernel(sources, *refs):
    lo_ref, mid_ref = refs[:2]
    g_refs = refs[2 : 2 + sources]
    cos_ref, sin_ref, pq_ref, lq_ref, kp_ref, ot_ref, lse_ref = refs[2 + sources : 9 + sources]
    q_ref, k_ref, v_ref, qt_ref, kt_ref = refs[9 + sources : 14 + sources]
    out_refs = refs[14 + sources : 14 + 2 * sources]
    sum_ref, dk_ref, dv_ref = refs[14 + 2 * sources :]
    t = pl.program_id(0)
    chunk = q_ref.shape[1]
    scaling = HEAD_DIM**-0.5
    grads = jnp.concatenate([pair_rows(ref[...]) for ref in g_refs], axis=0)
    per = grads.shape[0] // chunk
    for c in range(per):
        dk_ref[t * per + c] = jnp.zeros((chunk, HEAD_DIM), F32)
        dv_ref[t * per + c] = jnp.zeros((chunk, HEAD_DIM), F32)
    parts = []
    for c in range(per):
        index = t * per + c
        do = grads[c * chunk : (c + 1) * chunk]
        dot32 = do.astype(F32).T
        dot16 = dot32.astype(BF16)
        delta = jnp.sum(dot32 * ot_ref[c], axis=0, keepdims=True)
        lse = lse_ref[c]
        q, qt = q_ref[index], qt_ref[index]
        query_pos, query_lo = pq_ref[c], lq_ref[c]

        def step(kc, dqt, masked):
            probs = jnp.exp(dot_nn(k_ref[kc], qt) - lse)
            if masked:
                key_pos = kp_ref[kc]
                visible = (key_pos <= query_pos) & (key_pos >= query_lo)
                probs = jnp.where(visible, probs, 0.0)
            dv_ref[kc] += dot_nn(probs.astype(BF16), do)
            prob_grad = dot_nn(v_ref[kc], dot16)
            score_grad = (probs * (prob_grad - delta)).astype(BF16)
            dk_ref[kc] += dot_nn(score_grad, q)
            return dqt + dot_nn(kt_ref[kc], score_grad)

        dqt = jnp.zeros((HEAD_DIM, chunk), F32)
        for own in range(per):
            dqt = step(t * per + own, dqt, True)
        dqt = lax.fori_loop(lo_ref[t], mid_ref[t], lambda i, s: step(i, s, True), dqt)
        dqt = in_pairs(mid_ref[t], t * per, lambda i, s: step(i, s, False), dqt)
        parts.append(rope_t(dqt * scaling, cos_ref[index], -sin_ref[index]).T)

    def store(block, u, first):
        span = block.shape[0] // sources
        here = pl.ds(pl.multiple_of(u * GROUP, GROUP), GROUP)
        block = block.astype(BF16)
        total = jnp.sum(block.astype(F32), axis=0, keepdims=True)
        if first:
            sum_ref[1:2, :] += total[:, :HEAD_DIM]
            sum_ref[2:3, :] += total[:, HEAD_DIM:]
        else:
            sum_ref[0:1, :] += total
        for i, ref in enumerate(out_refs):
            part = block[i * span : (i + 1) * span]
            half = ref.shape[0]
            shape = (half, GROUP, HEAD_DIM)
            for side in range(2):
                one = part[side * half * GROUP : (side + 1) * half * GROUP, :HEAD_DIM]
                ref[:, side, here, first : first + HEAD_DIM] = one.reshape(shape)
            if first:
                both = side_by_side(part[:, HEAD_DIM:])
                ref[:, 2, here, :] = both.reshape(half, GROUP, 2 * HEAD_DIM)

    @pl.when(t == 0)
    def _():
        sum_ref[...] = jnp.zeros_like(sum_ref)

    store(parts[0] if per == 1 else jnp.concatenate(parts, axis=0), t, 0)

    @pl.when(t == pl.num_programs(0) - 1)
    def _():
        def finish(u, carry):
            found = []
            for c in range(per):
                index = u * per + c
                dkt = rope_t(dk_ref[index].T * scaling, cos_ref[index], -sin_ref[index])
                found.append(jnp.concatenate([dkt.T, dv_ref[index]], axis=1))
            store(found[0] if per == 1 else jnp.concatenate(found, axis=0), u, HEAD_DIM)
            return carry

        lax.fori_loop(0, pl.num_programs(0), finish, 0)


def attention_meta(positions, seq_lengths, chunk):
    tiles, tile = positions.shape
    count = tiles * tile // chunk
    per = tile // chunk
    opening = opening_of(positions, seq_lengths)
    frequency = 10000.0 ** (-2.0 * jnp.arange(ROT // 2, dtype=F32) / ROT)
    angles = (positions - opening).astype(F32).reshape(count, 1, chunk) * frequency[None, :, None]
    ends = jnp.arange(tiles, dtype=jnp.int32) * tile
    first_open = opening_of(ends, seq_lengths)
    last_open = opening_of(ends + tile - 1, seq_lengths)
    own = jnp.arange(tiles, dtype=jnp.int32) * per
    low = (first_open // tile) * per
    middle = jnp.minimum(((last_open + tile - 1) // tile) * per, own)
    return dict(
        low=low.astype(jnp.int32),
        middle=middle.astype(jnp.int32),
        cosine=jnp.cos(angles),
        sine=jnp.sin(angles),
        query_pos=positions.reshape(count, 1, chunk),
        query_lo=opening.reshape(count, 1, chunk),
        key_pos=positions.reshape(count, chunk, 1),
    )


def attention_forward(parts, meta):
    sources = len(parts)
    half, _, rows, lanes = parts[0].shape
    tile = sources * 2 * half * GROUP
    tiles = rows // GROUP
    count, _, chunk = meta["query_pos"].shape
    per = tile // chunk
    nat = jax.ShapeDtypeStruct((count, chunk, HEAD_DIM), BF16)
    turned = jax.ShapeDtypeStruct((count, HEAD_DIM, chunk), BF16)
    out = jax.ShapeDtypeStruct((half, rows, lanes), BF16)
    found = pl.pallas_call(
        lambda *refs: forward_kernel(sources, *refs),
        out_shape=[out] * sources
        + [
            jax.ShapeDtypeStruct((count, HEAD_DIM, chunk), F32),
            jax.ShapeDtypeStruct((count, 1, chunk), F32),
            nat, nat, nat, turned, turned,
        ],
        grid_spec=pltpu.PrefetchScalarGridSpec(
            num_scalar_prefetch=2,
            grid=(tiles,),
            in_specs=[tile_block((half, 3, GROUP, lanes), 2)] * sources
            + [
                tile_block((per, 1, chunk), 0),
                tile_block((per, 1, chunk), 0),
                whole_block((count, chunk, 1)),
            ],
            out_specs=[tile_block((half, GROUP, lanes), 1)] * sources
            + [
                tile_block((per, HEAD_DIM, chunk), 0),
                tile_block((per, 1, chunk), 0),
                whole_block(nat.shape),
                whole_block(nat.shape),
                whole_block(nat.shape),
                whole_block(turned.shape),
                whole_block(turned.shape),
            ],
            scratch_shapes=[pltpu.VMEM(turned.shape, BF16)],
        ),
        compiler_params=pltpu.CompilerParams(
            dimension_semantics=("arbitrary",), vmem_limit_bytes=58 * 1024 * 1024
        ),
        cost_estimate=LARGE,
        name="attention_forward",
    )(
        meta["low"], meta["middle"], *parts,
        meta["query_pos"], meta["query_lo"], meta["key_pos"],
    )
    return found[:sources], found[sources:]


def attention_backward(grads, meta, saved):
    sources = len(grads)
    half, rows, lanes = grads[0].shape
    tile = sources * 2 * half * GROUP
    tiles = rows // GROUP
    count, _, chunk = meta["query_pos"].shape
    per = tile // chunk
    turn = ROT // 2
    out = jax.ShapeDtypeStruct((half, 3, rows, lanes), BF16)
    ot, lse, q, k, v, qt, kt = saved
    found = pl.pallas_call(
        lambda *refs: backward_kernel(sources, *refs),
        out_shape=[out] * sources + [jax.ShapeDtypeStruct((3, HEAD_DIM), F32)],
        grid_spec=pltpu.PrefetchScalarGridSpec(
            num_scalar_prefetch=2,
            grid=(tiles,),
            in_specs=[tile_block((half, GROUP, lanes), 1)] * sources
            + [
                whole_block((count, turn, chunk)),
                whole_block((count, turn, chunk)),
                tile_block((per, 1, chunk), 0),
                tile_block((per, 1, chunk), 0),
                whole_block((count, chunk, 1)),
                tile_block((per, HEAD_DIM, chunk), 0),
                tile_block((per, 1, chunk), 0),
                whole_block(q.shape),
                whole_block(k.shape),
                whole_block(v.shape),
                whole_block(qt.shape),
                whole_block(kt.shape),
            ],
            out_specs=[whole_block(out.shape)] * sources + [whole_block((3, HEAD_DIM))],
            scratch_shapes=[
                pltpu.VMEM((count, chunk, HEAD_DIM), F32),
                pltpu.VMEM((count, chunk, HEAD_DIM), F32),
            ],
        ),
        compiler_params=pltpu.CompilerParams(
            dimension_semantics=("arbitrary",), vmem_limit_bytes=62 * 1024 * 1024
        ),
        cost_estimate=BROAD,
        name="attention_backward",
    )(
        meta["low"], meta["middle"], *grads, meta["cosine"], meta["sine"],
        meta["query_pos"], meta["query_lo"], meta["key_pos"], ot, lse, q, k, v, qt, kt,
    )
    return list(found[:sources]), found[sources]


def doubled(block, masks, count):
    held = block[None]
    for mask in masks:
        held = jnp.concatenate([held, swap(held, mask, count)], axis=0)
    return held


def halved(block, masks, count):
    for mask in masks[::-1]:
        middle = block.shape[0] // 2
        block = block[:middle] + swap(block[middle:], mask, count)
    return block[0]


def gather_list(block, masks, count):
    held = [block]
    for mask in masks:
        held = held + [swap(h, mask, count) for h in held]
    return held


def exchange(parts, masks, count):
    return [part if m == 0 else swap(part, m, count) for part, m in zip(parts, masks)]


def pick(block, axis, index):
    return lax.dynamic_index_in_dim(block, index, axis, False)


def gelu_tanh(values):
    return jax.nn.gelu(values, approximate=True)


def hop_kernel(pieces, *refs):
    refs = refs[2 * pieces :]
    outs = refs[4 * pieces :]
    for i in range(pieces):
        a_ref, b_ref, c_ref, d_ref = refs[4 * i : 4 * i + 4]
        out_ref, own_ref = outs[2 * i : 2 * i + 2]
        out_ref[...] = (a_ref[...].astype(F32) + b_ref[...].astype(F32)).astype(BF16)
        own_ref[...] = c_ref[...].astype(F32) + d_ref[...].astype(F32)


def hop(kept, there, masks, left_bits, my_blk, cost):
    pieces = len(kept)
    count, _, width = kept[0].shape
    picks, in_specs, out_specs, shapes, operands = [], [], [], [], []
    for i in range(pieces):
        numbers = jnp.arange(count, dtype=jnp.int32).reshape((2,) * len(left_bits[i]))
        axis = left_bits[i].index(masks[i])
        mine = (my_blk // masks[i]) % 2
        picks += [pick(numbers, axis, 1 - mine).reshape(-1), pick(numbers, axis, mine).reshape(-1)]
        rows = kept[i].shape[1]
        block = (1, rows, width)
        far = pl.BlockSpec(block, lambda t, *at, i=i: (at[2 * i][t], 0, 0))
        near = pl.BlockSpec(block, lambda t, *at, i=i: (at[2 * i + 1][t], 0, 0))
        in_specs += [far, far, near, near]
        operands += [kept[i], there[i], kept[i], there[i]]
        out_specs += [pl.BlockSpec(block, lambda t, *at: (t, 0, 0))] * 2
        shape = (count // 2, rows, width)
        shapes += [jax.ShapeDtypeStruct(shape, BF16), jax.ShapeDtypeStruct(shape, F32)]
    found = pl.pallas_call(
        lambda *refs: hop_kernel(pieces, *refs),
        out_shape=shapes,
        grid_spec=pltpu.PrefetchScalarGridSpec(
            num_scalar_prefetch=2 * pieces,
            grid=(count // 2,),
            in_specs=in_specs,
            out_specs=out_specs,
        ),
        compiler_params=kernel_params(62),
        cost_estimate=cost,
        name="hop",
    )(*picks, *operands)
    return found[0::2], found[1::2]


def per_device(
    layer_in, out_grad, norm_gain, norm_bias, w_qkv, b_qkv, w_out, b_out, w_up, b_up,
    w_down, b_down, seq_lengths, token_place,
):
    heads, blks = lax.axis_size("head"), lax.axis_size("blk")
    count = heads * blks
    my_head, my_blk = lax.axis_index("head"), lax.axis_index("blk")
    me = my_head * blks + my_blk
    rows, width = layer_in.shape
    features = w_qkv.shape[1]
    units = w_up.shape[0]
    owners = HEAD_DIM // features
    member = me % owners
    blk_bits = [1 << i for i in range(blks.bit_length() - 1)][::-1]
    head_bits = [blks << i for i in range(heads.bit_length() - 1)][::-1]
    head_masks = slot_masks(head_bits)
    numbers = jnp.arange(count, dtype=jnp.int32)

    place = token_place.reshape(count, rows)
    ranks = place // count
    row_numbers = jnp.arange(rows, dtype=jnp.int32)
    x_sorted, order_hot = sort_rows(layer_in, token_place, me, count)
    x_all = lax.all_gather(x_sorted, "blk", axis=0, tiled=True)
    g_sorted = dot_nn(order_hot, out_grad).astype(BF16)

    qkv_full, out_full, bias_full = w_qkv, w_out, b_qkv
    if owners > 1:
        order = member ^ jnp.arange(owners, dtype=jnp.int32)

        def of_owners(block):
            found = [block] + [swap(block, e, count) for e in range(1, owners)]
            return jnp.stack(found)[order]

        qkv_full = jnp.moveaxis(of_owners(w_qkv), 0, 1).reshape(3, HEAD_DIM, width)
        bias_full = jnp.moveaxis(of_owners(b_qkv), 0, 1).reshape(3, HEAD_DIM)
        out_full = of_owners(w_out).reshape(HEAD_DIM, width)
    qkv_cut, lanes = 3 * HEAD_DIM, 2 * HEAD_DIM

    def all_heads(own, token=None):
        over = swap(own, head_bits[0], count)
        found = [own, over if token is None else after(over, token)]
        for bit in head_bits[1:]:
            found = found + [swap(w, bit, count) for w in found]
        return found

    vectors = jnp.stack([norm_gain, norm_bias, b_out, b_down])
    bias_row = jnp.concatenate([bias_full.reshape(-1), b_up])
    piece = vectors.size
    tile = jnp.zeros((16, width), BF16)
    tile = tile.at[0, : qkv_cut + units].set(bias_row).at[1, :piece].set(vectors.reshape(-1))
    w_list = all_heads(jnp.concatenate([qkv_full.reshape(qkv_cut, width), tile], axis=0))
    g_all = lax.all_gather(after(g_sorted, w_list[1]), "blk", axis=0, tiled=True)
    biases = jnp.stack([w[qkv_cut, : qkv_cut + units] for w in w_list]).astype(F32)

    vectors = jnp.stack([w[qkv_cut + 1, :piece].reshape(vectors.shape) for w in w_list])
    for mask in blk_bits:
        vectors = jnp.concatenate([vectors, swap(vectors, mask, count)], axis=0)
    absolute = me ^ jnp.array(slot_masks(head_bits + blk_bits), dtype=jnp.int32)
    choose = (absolute[None, :] == numbers[:, None]).astype(BF16)
    vectors = dot_nn(choose, vectors.reshape(count, -1)).reshape(count, 4, -1)
    vectors = jnp.transpose(vectors, (1, 0, 2)).reshape(4, width)
    gain, offset, out_bias, down_bias = (vectors[i][None] for i in range(4))

    up_list = all_heads(w_up, vectors)
    qkv_rows, qkv_turned = join(
        w_list,
        [
            [(r, 0, lanes, r * lanes) for r in range(heads)]
            + [(r, lanes, HEAD_DIM, heads * lanes + r * HEAD_DIM) for r in range(heads)]
        ],
        vectors,
        True,
    )
    qkv_bias = jnp.concatenate(
        [biases[:, :lanes].reshape(1, -1), biases[:, lanes:qkv_cut].reshape(1, -1)], axis=1
    )
    up_bias = biases[:, qkv_cut:].reshape(1, -1)

    sorted_place = jnp.sum(
        jnp.where(ranks[:, None, :] == row_numbers[None, :, None], place[:, None, :], 0), axis=2
    )
    slot_head = my_head ^ jnp.array([m // blks for m in head_masks], dtype=jnp.int32)
    device = (slot_head[:, None] * blks + jnp.arange(blks, dtype=jnp.int32)[None, :]).reshape(-1)
    chosen = jnp.where((device[:, None] == numbers[None, :])[:, :, None], sorted_place[None], 0)
    positions = jnp.sum(chosen, axis=1)
    own_positions = positions[:blks].reshape(-1)
    own_place = own_positions - opening_of(own_positions, seq_lengths)
    tiles = rows // GROUP
    positions = jnp.transpose(positions.reshape(count, tiles, GROUP), (1, 0, 2))
    positions = positions.reshape(tiles, count * GROUP)
    meta = attention_meta(positions, seq_lengths, min(CHUNK, count * GROUP))

    (up_rows,) = join(
        up_list, [[(r, 0, units, r * units) for r in range(heads)]], vectors
    )
    x_all = after(x_all, up_rows)
    normed, center, inverse, qkv = project(
        x_all, gain, offset, qkv_turned, qkv_bias, own_place, heads, blks
    )
    qkv_made = qkv[0]
    qkv = exchange(qkv, head_masks, count)
    w_back_list = all_heads(jnp.concatenate([w_down, out_full], axis=0), qkv_made)

    down_rows, out_rows, down_turned = join(
        w_back_list,
        [
            [(r, 0, units, r * units) for r in range(heads)],
            [(r, units, HEAD_DIM, r * HEAD_DIM) for r in range(heads)],
        ],
        qkv_made,
        True,
    )
    hidden = dot_nt(normed, up_rows) + up_bias
    active = gelu_tanh(hidden).astype(BF16)
    meta["low"] = after(meta["low"], active, meta["sine"], meta["cosine"])
    attended, saved = attention_forward(qkv, meta)
    def flat(block):
        return block.reshape(-1, block.shape[-1])

    def own_features(part):
        if owners == 1:
            return part
        mine = jnp.arange(lanes, dtype=jnp.int32) % HEAD_DIM // features == member
        return jnp.where(mine, part, 0)

    def packed(part):
        part = part.reshape(2, blks // 2, rows, HEAD_DIM)
        return jnp.concatenate([part[0], part[1]], axis=-1)

    attended_here = attended[0]
    attended = exchange(attended, head_masks, count)
    attended = [own_features(part) for part in attended]
    mixed = mixed_rows(active, attended, down_rows, out_rows)
    g_late = after(g_all, attended_here)

    heads_grad = dot_nt(g_late, out_rows).astype(BF16)
    heads_grad = [packed(heads_grad[:, r * HEAD_DIM : (r + 1) * HEAD_DIM]) for r in range(heads)]
    mine, others = list(range(heads // 2)), list(range(heads // 2, heads))
    back_sent = outer(attended, active, g_late, others, units, heads_grad[0])
    back_there = [swap(part, head_bits[-1], count) for part in back_sent]
    back_sent = back_sent[0]
    heads_grad = exchange(heads_grad, head_masks, count)
    heads_grad[0] = after(heads_grad[0], back_sent, mixed)
    mixed = mixed.reshape(blks, rows, width)
    mixed = lax.psum_scatter(mixed, "blk", scatter_dimension=0, tiled=False)

    qkv_grad, qkv_sums = attention_backward(heads_grad, meta, saved)
    g_last = after(g_late, qkv_grad[0])
    qkv_grad = [own_features(part) for part in exchange(qkv_grad, head_masks, count)]
    hidden_grad, up_sums = hidden_grads(g_last, hidden, down_turned, g_last)

    pieces = pieces_of(blks, rows)
    split_shape = (2,) * len(blk_bits)
    slots = jnp.arange(blks, dtype=jnp.int32).reshape(split_shape)
    parts = [(blks // 2, begin, end) for (begin, end), _ in pieces]

    def halves(block, far):
        found = []
        for (begin, end), order in pieces:
            axis = blk_bits.index(order[0])
            mine = (my_blk // order[0]) % 2
            piece = block if block.ndim == len(blk_bits) else block[..., begin:end, :]
            found.append(pick(piece, axis, 1 - mine if far else mine))
        return found

    hid_rows = hidden_grad.reshape(blks, rows, heads * units)

    chosen = jnp.concatenate([p.reshape(-1) for p in halves(slots, True) + halves(slots, False)])
    found = shifted(
        hid_rows, qkv_grad, up_rows, qkv_rows, chosen, parts + parts, hidden_grad
    )
    sent, kept = found[: len(parts)], found[len(parts) :]
    back_own, back_far = outer(attended, active, g_last, mine, units, kept[0], back_there)
    back_there = swap(back_far, head_bits[0], count)
    in_sent = outer(qkv_grad, hidden_grad, normed, others, units, back_far)
    in_there = [swap(part, head_bits[-1], count) for part in in_sent]
    in_sent = in_sent[0]
    orders = [order for _, order in pieces]
    norm_grads = norm_sums(
        after(x_all, in_sent).reshape(blks, rows, width),
        center.reshape(blks, rows, 1),
        inverse.reshape(blks, rows, 1),
        list(sent) + list(kept),
        chosen,
        parts + parts,
    )
    own_g = g_sorted.astype(F32)
    sums = jnp.concatenate([norm_grads, jnp.sum(own_g, axis=0)[None]], axis=0)
    sums = jnp.transpose(sums.reshape(3, heads, blks, -1), (2, 1, 0, 3)).reshape(blks, -1)
    relative = jnp.array(slot_masks(blk_bits), dtype=jnp.int32) ^ my_blk
    reached = relative[:, None] == slots.reshape(1, -1)
    reached = jnp.sum(jnp.where(reached[:, :, None], sums[None], 0.0), axis=1)
    kept = [after(kept[0], reached, mixed), kept[1]]
    there = [swap(sent[i], order[0], count) for i, order in enumerate(orders)]
    left = [[b for b in blk_bits if b != order[0]] for order in orders]
    for step in range(1, len(blk_bits)):
        masks = [order[step] for order in orders]
        far, kept = hop(kept, there, masks, left, my_blk, LARGE if step == 1 else LAST)
        there = [swap(f, mask, count) for f, mask in zip(far, masks)]
        left = [[b for b in bits if b != mask] for bits, mask in zip(left, masks)]
        last_far = far[0]
        if step == 1:
            in_own, in_far = outer(qkv_grad, hidden_grad, normed, mine, units, kept[0], in_there)
            in_there = swap(in_far, head_bits[0], count)
            reached = after(reached, in_far, back_there)
            near, away = jnp.split(reached, 2)
            for mask in blk_bits[::-1][:-1]:
                near, away = fold(near, swap(away, mask, count))
            kept = [after(kept[0], in_far, near), kept[1]]

    layer_out = layer_rows(
        x_sorted, mixed, jnp.concatenate([out_bias, down_bias], axis=0), order_hot, last_far
    )
    w_down_grad, w_out_grad = totals(back_own, back_there, units, last_far)
    w_up_grad, w_qkv_grad = totals(in_own, in_there, units, last_far)
    w_qkv_grad = w_qkv_grad.reshape(3, owners, features, width)
    w_qkv_grad = lax.dynamic_index_in_dim(w_qkv_grad, member, 1, False)
    w_out_grad = w_out_grad.reshape(owners, features, width)
    w_out_grad = lax.dynamic_index_in_dim(w_out_grad, member, 0, False)
    qkv_sums = qkv_sums.reshape(3, owners, features)
    b_qkv_grad = lax.dynamic_index_in_dim(qkv_sums, member, 1, False)

    away = after(away, last_far)
    sums = near[0] + swap(away, blk_bits[0], count)[0]
    sums = sums.reshape(heads, -1)
    slot_numbers = jnp.arange(heads, dtype=jnp.int32)
    reached = jnp.where((slot_head[:, None] == slot_numbers[None])[:, :, None], sums[None], 0.0)
    small = jnp.concatenate([jnp.sum(reached, axis=1), up_sums.reshape(heads, units)], axis=1)
    small = exchange([small[r : r + 1] for r in range(heads)], head_masks, count)

    input_grad = input_rows(x_sorted, g_sorted, gain, order_hot, kept, there)
    small = added(small, input_grad)[0]
    vector_grads, b_up_grad = small[:-units].reshape(3, -1), small[-units:]
    return (
        layer_out,
        input_grad,
        vector_grads[0],
        vector_grads[1],
        w_qkv_grad,
        b_qkv_grad,
        w_out_grad,
        vector_grads[2],
        w_up_grad,
        b_up_grad,
        w_down_grad,
        vector_grads[2],
    )


def solution(mesh):
    rows, vector = P(AXES, None), P(AXES)
    qkv, qkv_bias = P(None, AXES, None), P(None, AXES)
    in_specs = (
        rows, rows, vector, vector, qkv, qkv_bias, rows, vector, rows, vector, rows, vector,
        P(), P(),
    )
    out_specs = (
        rows, rows, vector, vector, qkv, qkv_bias, rows, vector, rows, vector, rows, vector,
    )
    return jax.shard_map(
        per_device, mesh=mesh, in_specs=in_specs, out_specs=out_specs, check_vma=False
    )
```

```python
import jax
import jax.numpy as jnp
from jax import lax
from jax.experimental import pallas as pl
from jax.experimental.pallas import tpu as pltpu
from jax.sharding import PartitionSpec as P

HEAD_DIM = 64
ROT = 32
AXES = ("head", "blk")
GROUP = 16
CHUNK = 512
NEG = -1e30
F32 = jnp.float32
BF16 = jnp.bfloat16
SMALL = pl.CostEstimate(flops=1, bytes_accessed=1, transcendentals=0)
MIDDLE = pl.CostEstimate(flops=5_000_000_000, bytes_accessed=1_000_000, transcendentals=0)
BROAD = pl.CostEstimate(flops=34_000_000_000, bytes_accessed=1_000_000, transcendentals=0)
LAST = pl.CostEstimate(flops=6_000_000_000, bytes_accessed=1_000_000, transcendentals=0)
LARGE = pl.CostEstimate(flops=120_000_000_000, bytes_accessed=1_000_000, transcendentals=0)


def swap(block, mask, count):
    return lax.ppermute(block, AXES, [(i, i ^ mask) for i in range(count)])


def dot_nn(a, b):
    return lax.dot_general(a, b, (((1,), (0,)), ((), ())), preferred_element_type=F32)


def dot_nt(a, b):
    return lax.dot_general(a, b, (((1,), (1,)), ((), ())), preferred_element_type=F32)


def dot_tn(a, b):
    return lax.dot_general(a, b, (((0,), (0,)), ((), ())), preferred_element_type=F32)


def opening_of(packed, lengths):
    starts = jnp.cumsum(lengths) - lengths
    inside = packed[..., None] >= starts
    return jnp.max(jnp.where(inside, starts, 0), axis=-1)


def pieces_of(blks, rows):
    bits = [1 << i for i in range(blks.bit_length() - 1)]
    half = rows // 2
    return [((0, half), bits), ((half, rows), bits[1:] + bits[:1])]


def slot_masks(order):
    masks = [0]
    for mask in order:
        masks = masks + [m ^ mask for m in masks]
    return masks


def after_kernel(*refs):
    pass


def after(value, *others):
    anywhere = pl.BlockSpec(memory_space=pl.ANY)
    return pl.pallas_call(
        after_kernel,
        out_shape=jax.ShapeDtypeStruct(value.shape, value.dtype),
        in_specs=[anywhere] * (1 + len(others)),
        out_specs=anywhere,
        input_output_aliases={0: 0},
        compiler_params=pltpu.CompilerParams(vmem_limit_bytes=60 * 1024 * 1024),
        cost_estimate=SMALL,
        name="after",
    )(value, *others)


def whole_block(shape):
    zeros = (0,) * len(shape)
    return pl.BlockSpec(tuple(shape), lambda t, *refs: zeros)


def tile_block(shape, axis):
    def place(t, *refs):
        return tuple(t if i == axis else 0 for i in range(len(shape)))

    return pl.BlockSpec(tuple(shape), place)


def kernel_params(megabytes):
    return pltpu.CompilerParams(
        dimension_semantics=("arbitrary",), vmem_limit_bytes=megabytes * 1024 * 1024
    )


def join_kernel(plans, turned, count, *refs):
    blocks, out_refs = refs[:count], refs[count + 1 :]
    for plan, out_ref in zip(plans, out_refs):
        for which, start, size, to in plan:
            out_ref[to : to + size] = blocks[which][start : start + size]
    if turned:
        for which, start, size, to in plans[0]:
            out_refs[-1][:, to : to + size] = blocks[which][start : start + size].T


def join(blocks, plans, token, turned=False):
    width = blocks[0].shape[1]
    shapes = [(sum(size for _, _, size, _ in plan), width) for plan in plans]
    if turned:
        shapes.append(shapes[0][::-1])
    return pl.pallas_call(
        lambda *refs: join_kernel(plans, turned, len(blocks), *refs),
        out_shape=[jax.ShapeDtypeStruct(shape, BF16) for shape in shapes],
        grid=(1,),
        in_specs=[whole_block(b.shape) for b in blocks] + [pl.BlockSpec(memory_space=pl.ANY)],
        out_specs=[whole_block(shape) for shape in shapes],
        compiler_params=kernel_params(56),
        cost_estimate=SMALL,
        name="join",
    )(*blocks, token)


def sort_kernel(count, me_ref, place_ref, rows_ref, sorted_ref, hot_ref):
    size = rows_ref.shape[0]
    ranks = lax.div(place_ref[0], jnp.int32(count))
    numbers = lax.broadcasted_iota(jnp.int32, (size, size), 0)
    hot = jnp.where(ranks == numbers, 1.0, 0.0).astype(BF16)
    hot_ref[...] = hot
    sorted_ref[...] = dot_nn(hot, rows_ref[...]).astype(BF16)


def sort_rows(rows, token_place, me, count):
    size, width = rows.shape
    return pl.pallas_call(
        lambda *refs: sort_kernel(count, *refs),
        out_shape=[
            jax.ShapeDtypeStruct((size, width), BF16),
            jax.ShapeDtypeStruct((size, size), BF16),
        ],
        grid_spec=pltpu.PrefetchScalarGridSpec(
            num_scalar_prefetch=1,
            grid=(1,),
            in_specs=[
                pl.BlockSpec((1, 1, size), lambda t, at: (at[0], 0, 0)),
                whole_block((size, width)),
            ],
            out_specs=[whole_block((size, width)), whole_block((size, size))],
        ),
        compiler_params=kernel_params(62),
        cost_estimate=SMALL,
        name="sort_rows",
    )(me.reshape(1).astype(jnp.int32), token_place.reshape(count, 1, size), rows)


def project_kernel(heads, *refs):
    x_ref, gain_ref, offset_ref, w_ref, bias_ref, cos_ref, up_ref, down_ref = refs[:8]
    normed_ref, mean_ref, inverse_ref = refs[8:11]
    out_refs = refs[11:]
    _, _, size, width = x_ref.shape
    lanes = cos_ref.shape[3]
    half = ROT // 2
    span = heads * lanes
    x = x_ref[...].reshape(2 * size, width).astype(F32)
    mean = jnp.mean(x, axis=1, keepdims=True)
    centered = x - mean
    inverse = lax.rsqrt(jnp.mean(centered * centered, axis=1, keepdims=True) + 1e-05)
    normed = (centered * inverse * gain_ref[...] + offset_ref[...]).astype(BF16)
    normed_ref[...] = normed.reshape(normed_ref.shape)
    mean_ref[...] = mean.reshape(mean_ref.shape)
    inverse_ref[...] = inverse.reshape(inverse_ref.shape)
    z_both = dot_nn(normed, w_ref[...]) + bias_ref[...]
    values = []
    for side in range(2):
        z = z_both[side * size : (side + 1) * size]
        for r in range(heads):
            u = z[:, r * lanes : (r + 1) * lanes]
            u = (
                u * cos_ref[side, 0]
                + pltpu.roll(u, lanes - half, 1) * up_ref[side, 0]
                + pltpu.roll(u, half, 1) * down_ref[side, 0]
            )
            out_refs[r][0, side] = u.astype(BF16)
        values.append(z[:, span:])
    for r in range(heads):
        at = slice(r * HEAD_DIM, (r + 1) * HEAD_DIM)
        both = jnp.concatenate([values[0][:, at], values[1][:, at]], axis=1)
        out_refs[r][0, 2] = both.astype(BF16)


def project(x_all, gain, offset, w_turned, bias, place, heads, blks):
    rows, width = x_all.shape
    depth = w_turned.shape[1]
    lanes = 2 * HEAD_DIM
    size = rows // blks
    lane = jnp.arange(lanes, dtype=jnp.int32) % HEAD_DIM
    half = ROT // 2
    frequency = 10000.0 ** (-2.0 * (lane % half).astype(F32) / ROT)
    angles = place.astype(F32)[:, None] * frequency[None, :]
    cosine = jnp.where(lane < ROT, jnp.cos(angles), 1.0)
    sine = jnp.sin(angles)
    up = jnp.where(lane < half, -sine, 0.0)
    down = jnp.where((lane >= half) & (lane < ROT), sine, 0.0)
    shape = (2, blks // 2, size)
    strip = tile_block((2, 1, size, width), 1)
    column = tile_block((2, 1, size, 1), 1)
    table = tile_block((2, 1, size, lanes), 1)
    found = pl.pallas_call(
        lambda *refs: project_kernel(heads, *refs),
        out_shape=[
            jax.ShapeDtypeStruct(shape + (width,), BF16),
            jax.ShapeDtypeStruct(shape + (1,), F32),
            jax.ShapeDtypeStruct(shape + (1,), F32),
        ]
        + [jax.ShapeDtypeStruct((blks // 2, 3, size, lanes), BF16)] * heads,
        grid=(blks // 2,),
        in_specs=[
            strip,
            whole_block((1, width)),
            whole_block((1, width)),
            whole_block((width, depth)),
            whole_block((1, depth)),
            table, table, table,
        ],
        out_specs=[strip, column, column] + [tile_block((1, 3, size, lanes), 0)] * heads,
        compiler_params=kernel_params(56),
        cost_estimate=BROAD,
        name="project",
    )(
        x_all.reshape(shape + (width,)), gain, offset, w_turned, bias,
        *[t.reshape(shape + (lanes,)) for t in (cosine, up, down)],
    )
    return found[0].reshape(rows, width), found[1], found[2], found[3:]


def mixed_kernel(heads, *refs):
    act_ref, down_ref, out_w_ref = refs[:3]
    att_refs, out_ref, left_ref = refs[3 : 3 + heads], refs[-2], refs[-1]

    @pl.when(pl.program_id(0) == 0)
    def _():
        parts = [pair_rows(a[...]) for a in att_refs]
        left_ref[...] = jnp.concatenate(parts, axis=1)

    total = dot_nn(act_ref[...], down_ref[...]) + dot_nn(left_ref[...], out_w_ref[...])
    out_ref[...] = total.astype(BF16)


def mixed_rows(active, attended, down_rows, out_rows):
    heads = len(attended)
    rows, span = active.shape
    width = down_rows.shape[1]
    block = 512
    return pl.pallas_call(
        lambda *refs: mixed_kernel(heads, *refs),
        out_shape=jax.ShapeDtypeStruct((rows, width), BF16),
        grid=(width // block,),
        in_specs=[
            whole_block(active.shape),
            tile_block((span, block), 1),
            tile_block((out_rows.shape[0], block), 1),
        ]
        + [whole_block(a.shape) for a in attended],
        out_specs=tile_block((rows, block), 1),
        scratch_shapes=[pltpu.VMEM((rows, heads * HEAD_DIM), BF16)],
        compiler_params=kernel_params(58),
        cost_estimate=SMALL,
        name="mixed",
    )(active, down_rows, out_rows, *attended)


GELU_ROOT = 0.7978845608028654
GELU_CUBE = 0.044715


def hidden_grad_kernel(g_ref, hidden_ref, down_ref, token_ref, grad_ref, sum_ref):
    h = hidden_ref[...]
    square = h * h
    bent = jnp.tanh(GELU_ROOT * (h + GELU_CUBE * (square * h)))
    slope = 0.5 * (1.0 + bent) + (0.5 * GELU_ROOT) * h * (1.0 - bent * bent) * (
        1.0 + (3.0 * GELU_CUBE) * square
    )
    grad = (dot_nn(g_ref[...], down_ref[...]) * slope).astype(BF16)
    grad_ref[...] = grad
    sum_ref[...] = jnp.sum(grad.astype(F32), axis=0, keepdims=True)


def hidden_grads(g_all, hidden, down_turned, token):
    rows, width = g_all.shape
    span = hidden.shape[1]
    block = min(256, span)
    size = min(1024, rows)
    found = pl.pallas_call(
        hidden_grad_kernel,
        out_shape=[
            jax.ShapeDtypeStruct((rows, span), BF16),
            jax.ShapeDtypeStruct((rows // size, 1, span), F32),
        ],
        grid=(rows // size, span // block),
        in_specs=[
            pl.BlockSpec((size, width), lambda i, j: (i, 0)),
            pl.BlockSpec((size, block), lambda i, j: (i, j)),
            pl.BlockSpec((width, block), lambda i, j: (0, j)),
            pl.BlockSpec(memory_space=pl.ANY),
        ],
        out_specs=[
            pl.BlockSpec((size, block), lambda i, j: (i, j)),
            pl.BlockSpec((None, 1, block), lambda i, j: (i, 0, j)),
        ],
        compiler_params=pltpu.CompilerParams(
            dimension_semantics=("arbitrary", "arbitrary"), vmem_limit_bytes=48 * 1024 * 1024
        ),
        cost_estimate=SMALL,
        name="hidden_grad",
    )(g_all, hidden, down_turned, token)
    return found[0], jnp.sum(found[1], axis=(0, 1))


def shifted_kernel(heads, parts, slots_ref, *refs):
    hid_ref, up_ref, w_ref = refs[:3]
    qkv_refs, out_refs, left_ref = refs[3 : 3 + heads], refs[4 + heads : -1], refs[-1]
    half, _, _, lanes = qkv_refs[0].shape
    units = hid_ref.shape[2]
    span = units + heads * lanes

    @pl.when(pl.program_id(0) == 0)
    def _():
        at, number = 0, 0
        for count, begin, end in parts:
            for i in range(count):
                slot = slots_ref[number]
                number += 1
                side = slot // half
                group = slot - side * half
                rows = slice(at, at + end - begin)
                at += end - begin
                left_ref[rows, :units] = hid_ref[slot, begin:end, :]
                values = []
                for r in range(heads):
                    to = units + r * lanes
                    left_ref[rows, to : to + lanes] = qkv_refs[r][group, side, begin:end, :]
                    both = qkv_refs[r][group, 2, begin:end, :]
                    values.append(jnp.where(side == 0, both[:, :HEAD_DIM], both[:, HEAD_DIM:]))
                left_ref[rows, span:] = jnp.concatenate(values, axis=1)

    total = dot_nn(left_ref[:, :units], up_ref[...]) + dot_nn(left_ref[:, units:], w_ref[...])
    at = 0
    for out_ref, (count, begin, end) in zip(out_refs, parts):
        size = count * (end - begin)
        out_ref[...] = total[at : at + size].astype(BF16).reshape(out_ref.shape)
        at += size


def shifted(hid_grad, qkv_grad, up_rows, w_rows, slots, parts, token):
    heads = len(qkv_grad)
    width = up_rows.shape[1]
    total_rows = sum(n * (end - begin) for n, begin, end in parts)
    depth = up_rows.shape[0] + w_rows.shape[0]
    block = 512
    return pl.pallas_call(
        lambda *refs: shifted_kernel(heads, parts, *refs),
        out_shape=[jax.ShapeDtypeStruct((n, end - begin, width), BF16) for n, begin, end in parts],
        grid_spec=pltpu.PrefetchScalarGridSpec(
            num_scalar_prefetch=1,
            grid=(width // block,),
            in_specs=[
                whole_block(hid_grad.shape),
                tile_block((up_rows.shape[0], block), 1),
                tile_block((w_rows.shape[0], block), 1),
            ]
            + [whole_block(q.shape) for q in qkv_grad]
            + [pl.BlockSpec(memory_space=pl.ANY)],
            out_specs=[tile_block((n, end - begin, block), 2) for n, begin, end in parts],
            scratch_shapes=[pltpu.VMEM((total_rows, depth), BF16)],
        ),
        compiler_params=kernel_params(60),
        cost_estimate=MIDDLE,
        name="shifted",
    )(slots, hid_grad, up_rows, w_rows, *qkv_grad, token)


def turn_left(left_ref, owners_of, units, second_ref, first_refs):
    low, high = owners_of[0] * units, (owners_of[-1] + 1) * units
    left_ref[: high - low, :] = second_ref[:, low:high].T
    at = high - low
    cols = left_ref.shape[1] // 2
    for ref in first_refs:
        if len(ref.shape) == 4:
            half, _, rows, lanes = ref.shape
            for side in range(2):
                block = ref[:, side].reshape(half * rows, lanes).T
                left_ref[at : at + lanes, side * cols : (side + 1) * cols] = block
            at += lanes
            pair = ref[:, 2].reshape(half * rows, lanes).T
        else:
            half, rows, lanes = ref.shape
            pair = ref[...].reshape(half * rows, lanes).T
        left_ref[at : at + HEAD_DIM, :cols] = pair[:HEAD_DIM]
        left_ref[at : at + HEAD_DIM, cols:] = pair[HEAD_DIM:]
        at += HEAD_DIM


SHARES = 4


def outer_kernel(owners_of, units, *refs):
    second_ref, right_ref = refs[:2]
    first_refs, left_ref = refs[2 : -2 - SHARES], refs[-1]
    out_refs = refs[-1 - SHARES : -1]

    @pl.when(pl.program_id(0) == 0)
    def _():
        turn_left(left_ref, owners_of, units, second_ref, first_refs)

    total = dot_nn(left_ref[...], right_ref[...]).astype(BF16)
    at = 0
    for ref in out_refs:
        ref[...] = total[at : at + ref.shape[0]]
        at += ref.shape[0]


def outer_add_kernel(owners_of, units, *refs):
    second_ref, right_ref = refs[:2]
    there_refs = refs[2 : 2 + SHARES]
    first_refs, own_ref, sent_ref, left_ref = refs[2 + SHARES : -4], refs[-3], refs[-2], refs[-1]

    @pl.when(pl.program_id(0) == 0)
    def _():
        turn_left(left_ref, owners_of, units, second_ref, first_refs)

    there = jnp.concatenate([ref[...] for ref in there_refs], axis=0)
    total = dot_nn(left_ref[...], right_ref[...]) + there.astype(F32)
    span = len(owners_of) * units
    cut = (total.shape[0] - span) // len(owners_of)
    own = len(owners_of) // 2
    low, high = own * units, span + own * cut
    own_ref[...] = jnp.concatenate([total[:low], total[span:high]], axis=0)
    sent_ref[...] = jnp.concatenate([total[low:span], total[high:]], axis=0).astype(BF16)


def outer(firsts, second, right, owners_of, units, token, there=None):
    rows, width = right.shape
    chosen = [firsts[r] for r in owners_of]
    block = min(512, width)
    cut = 3 * HEAD_DIM if len(chosen[0].shape) == 4 else HEAD_DIM
    count = len(owners_of) * (units + cut)
    strip = tile_block((count // SHARES, block), 1)
    operands, specs = [second, right], [whole_block(second.shape), tile_block((rows, block), 1)]
    if there is None:
        kernel = outer_kernel
        shapes = [jax.ShapeDtypeStruct((count // SHARES, width), BF16)] * SHARES
        out_specs = [strip] * SHARES
    else:
        kernel = outer_add_kernel
        shapes = [
            jax.ShapeDtypeStruct((count // 2, width), F32),
            jax.ShapeDtypeStruct((count // 2, width), BF16),
        ]
        out_specs = [tile_block((count // 2, block), 1)] * 2
        operands += there
        specs += [strip] * SHARES
    return pl.pallas_call(
        lambda *refs: kernel(owners_of, units, *refs),
        out_shape=shapes,
        grid=(width // block,),
        in_specs=specs
        + [whole_block(f.shape) for f in chosen]
        + [pl.BlockSpec(memory_space=pl.ANY)],
        out_specs=out_specs,
        scratch_shapes=[pltpu.VMEM((count, rows), BF16)],
        compiler_params=kernel_params(58),
        cost_estimate=SMALL,
        name="outer",
    )(*operands, *chosen, token)


def sums_kernel(parts, slots_ref, *refs):
    x_ref, mean_ref, inverse_ref = refs[:3]
    part_refs, out_ref = refs[3:-1], refs[-1]
    number = 0
    gain_sum, bias_sum = 0.0, 0.0
    for ref, (count, begin, end) in zip(part_refs, parts):
        for i in range(count):
            slot = slots_ref[number]
            number += 1
            x_hat = x_ref[slot, begin:end, :].astype(F32) - mean_ref[slot, begin:end, :]
            x_hat = x_hat * inverse_ref[slot, begin:end, :]
            part = ref[i].astype(F32)
            gain_sum += jnp.sum(part * x_hat, axis=0, keepdims=True)
            bias_sum += jnp.sum(part, axis=0, keepdims=True)
    out_ref[0:1, :] = gain_sum
    out_ref[1:2, :] = bias_sum


def norm_sums(x_all, mean, inverse, blocks, slots, parts):
    blks, rows, width = x_all.shape
    block = 512
    return pl.pallas_call(
        lambda *refs: sums_kernel(parts, *refs),
        out_shape=jax.ShapeDtypeStruct((2, width), F32),
        grid_spec=pltpu.PrefetchScalarGridSpec(
            num_scalar_prefetch=1,
            grid=(width // block,),
            in_specs=[
                tile_block((blks, rows, block), 2),
                whole_block(mean.shape),
                whole_block(inverse.shape),
            ]
            + [tile_block(b.shape[:2] + (block,), 2) for b in blocks],
            out_specs=tile_block((2, block), 1),
        ),
        compiler_params=kernel_params(56),
        cost_estimate=SMALL,
        name="norm_sums",
    )(slots, x_all, mean, inverse, *blocks)


def total_kernel(own_ref, there_ref, token_ref, top_ref, low_ref):
    cut = top_ref.shape[0]
    total = own_ref[...] + there_ref[...].astype(F32)
    top_ref[...] = total[:cut]
    low_ref[...] = total[cut:]


def totals(own, there, cut, token):
    rows, width = own.shape
    block = 512
    return pl.pallas_call(
        total_kernel,
        out_shape=[
            jax.ShapeDtypeStruct((cut, width), F32),
            jax.ShapeDtypeStruct((rows - cut, width), F32),
        ],
        grid=(width // block,),
        in_specs=[tile_block((rows, block), 1)] * 2 + [pl.BlockSpec(memory_space=pl.ANY)],
        out_specs=[tile_block((cut, block), 1), tile_block((rows - cut, block), 1)],
        compiler_params=kernel_params(32),
        cost_estimate=SMALL,
        name="totals",
    )(own, there, token)


def fold_kernel(kept_ref, there_ref, near_ref, far_ref):
    middle = near_ref.shape[0]
    total = kept_ref[...] + there_ref[...]
    near_ref[...] = total[:middle]
    far_ref[...] = total[middle:]


def fold(kept, there):
    rows, width = kept.shape
    shape = (rows // 2, width)
    return pl.pallas_call(
        fold_kernel,
        out_shape=[jax.ShapeDtypeStruct(shape, F32)] * 2,
        grid=(1,),
        in_specs=[whole_block((rows, width))] * 2,
        out_specs=[whole_block(shape)] * 2,
        compiler_params=kernel_params(16),
        cost_estimate=SMALL,
        name="fold",
    )(kept, there)


def add_kernel(count, *refs):
    total = refs[0][...]
    for ref in refs[1:count]:
        total += ref[...]
    refs[-1][...] = total


def added(parts, token):
    shape = parts[0].shape
    return pl.pallas_call(
        lambda *refs: add_kernel(len(parts), *refs),
        out_shape=jax.ShapeDtypeStruct(shape, F32),
        grid=(1,),
        in_specs=[whole_block(shape)] * len(parts) + [pl.BlockSpec(memory_space=pl.ANY)],
        out_specs=whole_block(shape),
        compiler_params=kernel_params(16),
        cost_estimate=SMALL,
        name="added",
    )(*parts, token)


def layer_out_kernel(x_ref, mixed_ref, bias_ref, hot_ref, token_ref, out_ref):
    total = x_ref[...].astype(F32) + mixed_ref[...].astype(F32) + bias_ref[0:1] + bias_ref[1:2]
    out_ref[...] = dot_tn(hot_ref[...], total.astype(BF16)).astype(BF16)


def layer_rows(x, mixed, biases, hot, token):
    operands = (x, mixed, biases, hot)
    return pl.pallas_call(
        layer_out_kernel,
        out_shape=jax.ShapeDtypeStruct(x.shape, BF16),
        grid=(1,),
        in_specs=[whole_block(o.shape) for o in operands] + [pl.BlockSpec(memory_space=pl.ANY)],
        out_specs=whole_block(x.shape),
        compiler_params=kernel_params(32),
        cost_estimate=SMALL,
        name="layer_rows",
    )(*operands, token)


def input_grad_kernel(pieces, *refs):
    x_ref, g_ref, gain_ref, hot_ref = refs[:4]
    kept_refs, there_refs, out_ref = refs[4 : 4 + pieces], refs[4 + pieces : -1], refs[-1]
    grad = jnp.concatenate(
        [k[0] + t[0].astype(F32) for k, t in zip(kept_refs, there_refs)], axis=0
    )
    x = x_ref[...].astype(F32)
    centered = x - jnp.mean(x, axis=1, keepdims=True)
    inverse = lax.rsqrt(jnp.mean(centered * centered, axis=1, keepdims=True) + 1e-05)
    x_hat = centered * inverse
    e = grad * gain_ref[...]
    part = inverse * (
        e
        - jnp.mean(e, axis=1, keepdims=True)
        - x_hat * jnp.mean(e * x_hat, axis=1, keepdims=True)
    )
    total = (g_ref[...].astype(F32) + part).astype(BF16)
    out_ref[...] = dot_tn(hot_ref[...], total).astype(BF16)


def input_rows(x, g, gain, hot, kept, there):
    operands = (x, g, gain, hot, *kept, *there)
    return pl.pallas_call(
        lambda *refs: input_grad_kernel(len(kept), *refs),
        out_shape=jax.ShapeDtypeStruct(x.shape, BF16),
        grid=(1,),
        in_specs=[whole_block(o.shape) for o in operands],
        out_specs=whole_block(x.shape),
        compiler_params=kernel_params(32),
        cost_estimate=SMALL,
        name="input_rows",
    )(*operands)


def rope_t(u, cosine, sine):
    half = ROT // 2
    top, low = u[:half], u[half:ROT]
    return jnp.concatenate(
        [top * cosine - low * sine, low * cosine + top * sine, u[ROT:]], axis=0
    )


def tall(block):
    return block.reshape(block.shape[0] * block.shape[1], block.shape[2])


def pair_rows(block):
    both = tall(block)
    return jnp.concatenate([both[:, :HEAD_DIM], both[:, HEAD_DIM:]], axis=0)


def packed_rows(refs):
    qk, v = [], []
    for ref in refs:
        qk += [tall(ref[:, 0]), tall(ref[:, 1])]
        v.append(pair_rows(ref[:, 2]))
    return jnp.concatenate(qk, axis=0), jnp.concatenate(v, axis=0)


def side_by_side(block):
    middle = block.shape[0] // 2
    return jnp.concatenate([block[:middle], block[middle:]], axis=1)


def in_pairs(first, last, step, state):
    pairs = lax.div(last - first, 2)
    state = lax.fori_loop(
        0, pairs, lambda i, s: step(first + 2 * i + 1, step(first + 2 * i, s)), state
    )
    return lax.fori_loop(first + 2 * pairs, last, step, state)


def forward_kernel(sources, *refs):
    lo_ref, mid_ref = refs[:2]
    in_refs = refs[2 : 2 + sources]
    pq_ref, lq_ref, kp_ref = refs[2 + sources : 5 + sources]
    att_refs = refs[5 + sources : 5 + 2 * sources]
    ot_ref, lse_ref, q_ref, k_ref, v_ref, qt_ref, kt_ref, vt_ref = refs[5 + 2 * sources :]
    t = pl.program_id(0)
    chunk = q_ref.shape[1]
    qk, v = packed_rows(in_refs)
    per = v.shape[0] // chunk
    for c in range(per):
        index = t * per + c
        part, values = qk[c * chunk : (c + 1) * chunk], v[c * chunk : (c + 1) * chunk]
        q_ref[index] = part[:, :HEAD_DIM]
        k_ref[index] = part[:, HEAD_DIM:]
        v_ref[index] = values
        turned = part.astype(F32).T
        qt_ref[index] = (turned[:HEAD_DIM] * HEAD_DIM**-0.5).astype(BF16)
        kt_ref[index] = turned[HEAD_DIM:].astype(BF16)
        vt_ref[index] = values.astype(F32).T.astype(BF16)
    outs = []
    for c in range(per):
        qt = qt_ref[t * per + c]
        query_pos, query_lo = pq_ref[c], lq_ref[c]

        def step(kc, state, masked):
            run_max, run_sum, acc = state
            scores = dot_nn(k_ref[kc], qt)
            if masked:
                key_pos = kp_ref[kc]
                visible = (key_pos <= query_pos) & (key_pos >= query_lo)
                scores = jnp.where(visible, scores, NEG)
            new_max = jnp.maximum(run_max, jnp.max(scores, axis=0, keepdims=True))
            weights = jnp.exp(scores - new_max)
            rescale = jnp.exp(run_max - new_max)
            run_sum = run_sum * rescale + jnp.sum(weights, axis=0, keepdims=True)
            acc = acc * rescale + dot_nn(vt_ref[kc], weights.astype(BF16))
            return new_max, run_sum, acc

        state = (
            jnp.full((1, chunk), NEG, F32),
            jnp.zeros((1, chunk), F32),
            jnp.zeros((HEAD_DIM, chunk), F32),
        )
        own = t * per + c
        state = step(own, state, True)
        state = in_pairs(lo_ref[t], mid_ref[t], lambda i, s: step(i, s, True), state)
        state = in_pairs(mid_ref[t], t * per, lambda i, s: step(i, s, False), state)
        if per > 1:
            state = lax.fori_loop(t * per, own, lambda i, s: step(i, s, True), state)
            state = lax.fori_loop(own + 1, (t + 1) * per, lambda i, s: step(i, s, True), state)
        run_max, run_sum, acc = state
        out = acc / run_sum
        ot_ref[c] = out
        lse_ref[c] = run_max + jnp.log(run_sum)
        outs.append(out.T.astype(BF16))
    att = outs[0] if per == 1 else jnp.concatenate(outs, axis=0)
    span = att.shape[0] // sources
    for i, ref in enumerate(att_refs):
        ref[...] = side_by_side(att[i * span : (i + 1) * span]).reshape(ref.shape)


def backward_kernel(sources, *refs):
    lo_ref, mid_ref = refs[:2]
    g_refs = refs[2 : 2 + sources]
    cos_ref, sin_ref, pq_ref, lq_ref, kp_ref, ot_ref, lse_ref = refs[2 + sources : 9 + sources]
    q_ref, k_ref, v_ref, qt_ref, kt_ref = refs[9 + sources : 14 + sources]
    out_refs = refs[14 + sources : 14 + 2 * sources]
    sum_ref, dk_ref, dv_ref = refs[14 + 2 * sources :]
    t = pl.program_id(0)
    chunk = q_ref.shape[1]
    scaling = HEAD_DIM**-0.5
    grads = jnp.concatenate([pair_rows(ref[...]) for ref in g_refs], axis=0)
    per = grads.shape[0] // chunk
    for c in range(per):
        dk_ref[t * per + c] = jnp.zeros((chunk, HEAD_DIM), F32)
        dv_ref[t * per + c] = jnp.zeros((chunk, HEAD_DIM), F32)
    parts = []
    for c in range(per):
        index = t * per + c
        do = grads[c * chunk : (c + 1) * chunk]
        dot32 = do.astype(F32).T
        dot16 = dot32.astype(BF16)
        delta = jnp.sum(dot32 * ot_ref[c], axis=0, keepdims=True)
        lse = lse_ref[c]
        q, qt = q_ref[index], qt_ref[index]
        query_pos, query_lo = pq_ref[c], lq_ref[c]

        def step(kc, dqt, masked):
            probs = jnp.exp(dot_nn(k_ref[kc], qt) - lse)
            if masked:
                key_pos = kp_ref[kc]
                visible = (key_pos <= query_pos) & (key_pos >= query_lo)
                probs = jnp.where(visible, probs, 0.0)
            dv_ref[kc] += dot_nn(probs.astype(BF16), do)
            prob_grad = dot_nn(v_ref[kc], dot16)
            score_grad = (probs * (prob_grad - delta)).astype(BF16)
            dk_ref[kc] += dot_nn(score_grad, q)
            return dqt + dot_nn(kt_ref[kc], score_grad)

        dqt = jnp.zeros((HEAD_DIM, chunk), F32)
        for own in range(per):
            dqt = step(t * per + own, dqt, True)
        dqt = in_pairs(lo_ref[t], mid_ref[t], lambda i, s: step(i, s, True), dqt)
        dqt = in_pairs(mid_ref[t], t * per, lambda i, s: step(i, s, False), dqt)
        parts.append(rope_t(dqt * scaling, cos_ref[index], -sin_ref[index]).T)

    def store(block, u, first):
        span = block.shape[0] // sources
        here = pl.ds(pl.multiple_of(u * GROUP, GROUP), GROUP)
        block = block.astype(BF16)
        total = jnp.sum(block.astype(F32), axis=0, keepdims=True)
        if first:
            sum_ref[1:2, :] += total[:, :HEAD_DIM]
            sum_ref[2:3, :] += total[:, HEAD_DIM:]
        else:
            sum_ref[0:1, :] += total
        for i, ref in enumerate(out_refs):
            part = block[i * span : (i + 1) * span]
            half = ref.shape[0]
            shape = (half, GROUP, HEAD_DIM)
            for side in range(2):
                one = part[side * half * GROUP : (side + 1) * half * GROUP, :HEAD_DIM]
                ref[:, side, here, first : first + HEAD_DIM] = one.reshape(shape)
            if first:
                both = side_by_side(part[:, HEAD_DIM:])
                ref[:, 2, here, :] = both.reshape(half, GROUP, 2 * HEAD_DIM)

    @pl.when(t == 0)
    def _():
        sum_ref[...] = jnp.zeros_like(sum_ref)

    store(parts[0] if per == 1 else jnp.concatenate(parts, axis=0), t, 0)

    @pl.when(t == pl.num_programs(0) - 1)
    def _():
        def finish(u, carry):
            found = []
            for c in range(per):
                index = u * per + c
                dkt = rope_t(dk_ref[index].T * scaling, cos_ref[index], -sin_ref[index])
                found.append(jnp.concatenate([dkt.T, dv_ref[index]], axis=1))
            store(found[0] if per == 1 else jnp.concatenate(found, axis=0), u, HEAD_DIM)
            return carry

        lax.fori_loop(0, pl.num_programs(0), finish, 0)


def attention_meta(positions, seq_lengths, chunk):
    tiles, tile = positions.shape
    count = tiles * tile // chunk
    per = tile // chunk
    opening = opening_of(positions, seq_lengths)
    frequency = 10000.0 ** (-2.0 * jnp.arange(ROT // 2, dtype=F32) / ROT)
    angles = (positions - opening).astype(F32).reshape(count, 1, chunk) * frequency[None, :, None]
    ends = jnp.arange(tiles, dtype=jnp.int32) * tile
    first_open = opening_of(ends, seq_lengths)
    last_open = opening_of(ends + tile - 1, seq_lengths)
    own = jnp.arange(tiles, dtype=jnp.int32) * per
    low = (first_open // tile) * per
    middle = jnp.minimum(((last_open + tile - 1) // tile) * per, own)
    return dict(
        low=low.astype(jnp.int32),
        middle=middle.astype(jnp.int32),
        cosine=jnp.cos(angles),
        sine=jnp.sin(angles),
        query_pos=positions.reshape(count, 1, chunk),
        query_lo=opening.reshape(count, 1, chunk),
        key_pos=positions.reshape(count, chunk, 1),
    )


def attention_forward(parts, meta):
    sources = len(parts)
    half, _, rows, lanes = parts[0].shape
    tile = sources * 2 * half * GROUP
    tiles = rows // GROUP
    count, _, chunk = meta["query_pos"].shape
    per = tile // chunk
    nat = jax.ShapeDtypeStruct((count, chunk, HEAD_DIM), BF16)
    turned = jax.ShapeDtypeStruct((count, HEAD_DIM, chunk), BF16)
    out = jax.ShapeDtypeStruct((half, rows, lanes), BF16)
    found = pl.pallas_call(
        lambda *refs: forward_kernel(sources, *refs),
        out_shape=[out] * sources
        + [
            jax.ShapeDtypeStruct((count, HEAD_DIM, chunk), F32),
            jax.ShapeDtypeStruct((count, 1, chunk), F32),
            nat, nat, nat, turned, turned,
        ],
        grid_spec=pltpu.PrefetchScalarGridSpec(
            num_scalar_prefetch=2,
            grid=(tiles,),
            in_specs=[tile_block((half, 3, GROUP, lanes), 2)] * sources
            + [
                tile_block((per, 1, chunk), 0),
                tile_block((per, 1, chunk), 0),
                whole_block((count, chunk, 1)),
            ],
            out_specs=[tile_block((half, GROUP, lanes), 1)] * sources
            + [
                tile_block((per, HEAD_DIM, chunk), 0),
                tile_block((per, 1, chunk), 0),
                whole_block(nat.shape),
                whole_block(nat.shape),
                whole_block(nat.shape),
                whole_block(turned.shape),
                whole_block(turned.shape),
            ],
            scratch_shapes=[pltpu.VMEM(turned.shape, BF16)],
        ),
        compiler_params=pltpu.CompilerParams(
            dimension_semantics=("arbitrary",), vmem_limit_bytes=58 * 1024 * 1024
        ),
        cost_estimate=LARGE,
        name="attention_forward",
    )(
        meta["low"], meta["middle"], *parts,
        meta["query_pos"], meta["query_lo"], meta["key_pos"],
    )
    return found[:sources], found[sources:]


def attention_backward(grads, meta, saved):
    sources = len(grads)
    half, rows, lanes = grads[0].shape
    tile = sources * 2 * half * GROUP
    tiles = rows // GROUP
    count, _, chunk = meta["query_pos"].shape
    per = tile // chunk
    turn = ROT // 2
    out = jax.ShapeDtypeStruct((half, 3, rows, lanes), BF16)
    ot, lse, q, k, v, qt, kt = saved
    found = pl.pallas_call(
        lambda *refs: backward_kernel(sources, *refs),
        out_shape=[out] * sources + [jax.ShapeDtypeStruct((3, HEAD_DIM), F32)],
        grid_spec=pltpu.PrefetchScalarGridSpec(
            num_scalar_prefetch=2,
            grid=(tiles,),
            in_specs=[tile_block((half, GROUP, lanes), 1)] * sources
            + [
                whole_block((count, turn, chunk)),
                whole_block((count, turn, chunk)),
                tile_block((per, 1, chunk), 0),
                tile_block((per, 1, chunk), 0),
                whole_block((count, chunk, 1)),
                tile_block((per, HEAD_DIM, chunk), 0),
                tile_block((per, 1, chunk), 0),
                whole_block(q.shape),
                whole_block(k.shape),
                whole_block(v.shape),
                whole_block(qt.shape),
                whole_block(kt.shape),
            ],
            out_specs=[whole_block(out.shape)] * sources + [whole_block((3, HEAD_DIM))],
            scratch_shapes=[
                pltpu.VMEM((count, chunk, HEAD_DIM), F32),
                pltpu.VMEM((count, chunk, HEAD_DIM), F32),
            ],
        ),
        compiler_params=pltpu.CompilerParams(
            dimension_semantics=("arbitrary",), vmem_limit_bytes=62 * 1024 * 1024
        ),
        cost_estimate=BROAD,
        name="attention_backward",
    )(
        meta["low"], meta["middle"], *grads, meta["cosine"], meta["sine"],
        meta["query_pos"], meta["query_lo"], meta["key_pos"], ot, lse, q, k, v, qt, kt,
    )
    return list(found[:sources]), found[sources]


def doubled(block, masks, count):
    held = block[None]
    for mask in masks:
        held = jnp.concatenate([held, swap(held, mask, count)], axis=0)
    return held


def halved(block, masks, count):
    for mask in masks[::-1]:
        middle = block.shape[0] // 2
        block = block[:middle] + swap(block[middle:], mask, count)
    return block[0]


def gather_list(block, masks, count):
    held = [block]
    for mask in masks:
        held = held + [swap(h, mask, count) for h in held]
    return held


def exchange(parts, masks, count):
    return [part if m == 0 else swap(part, m, count) for part, m in zip(parts, masks)]


def pick(block, axis, index):
    return lax.dynamic_index_in_dim(block, index, axis, False)


def gelu_tanh(values):
    return jax.nn.gelu(values, approximate=True)


def hop_kernel(pieces, *refs):
    refs = refs[2 * pieces :]
    outs = refs[4 * pieces :]
    for i in range(pieces):
        a_ref, b_ref, c_ref, d_ref = refs[4 * i : 4 * i + 4]
        out_ref, own_ref = outs[2 * i : 2 * i + 2]
        out_ref[...] = (a_ref[...].astype(F32) + b_ref[...].astype(F32)).astype(BF16)
        own_ref[...] = c_ref[...].astype(F32) + d_ref[...].astype(F32)


def hop(kept, there, masks, left_bits, my_blk, cost):
    pieces = len(kept)
    count, _, width = kept[0].shape
    picks, in_specs, out_specs, shapes, operands = [], [], [], [], []
    for i in range(pieces):
        numbers = jnp.arange(count, dtype=jnp.int32).reshape((2,) * len(left_bits[i]))
        axis = left_bits[i].index(masks[i])
        mine = (my_blk // masks[i]) % 2
        picks += [pick(numbers, axis, 1 - mine).reshape(-1), pick(numbers, axis, mine).reshape(-1)]
        rows = kept[i].shape[1]
        block = (1, rows, width)
        far = pl.BlockSpec(block, lambda t, *at, i=i: (at[2 * i][t], 0, 0))
        near = pl.BlockSpec(block, lambda t, *at, i=i: (at[2 * i + 1][t], 0, 0))
        in_specs += [far, far, near, near]
        operands += [kept[i], there[i], kept[i], there[i]]
        out_specs += [pl.BlockSpec(block, lambda t, *at: (t, 0, 0))] * 2
        shape = (count // 2, rows, width)
        shapes += [jax.ShapeDtypeStruct(shape, BF16), jax.ShapeDtypeStruct(shape, F32)]
    found = pl.pallas_call(
        lambda *refs: hop_kernel(pieces, *refs),
        out_shape=shapes,
        grid_spec=pltpu.PrefetchScalarGridSpec(
            num_scalar_prefetch=2 * pieces,
            grid=(count // 2,),
            in_specs=in_specs,
            out_specs=out_specs,
        ),
        compiler_params=kernel_params(62),
        cost_estimate=cost,
        name="hop",
    )(*picks, *operands)
    return found[0::2], found[1::2]


def per_device(
    layer_in, out_grad, norm_gain, norm_bias, w_qkv, b_qkv, w_out, b_out, w_up, b_up,
    w_down, b_down, seq_lengths, token_place,
):
    heads, blks = lax.axis_size("head"), lax.axis_size("blk")
    count = heads * blks
    my_head, my_blk = lax.axis_index("head"), lax.axis_index("blk")
    me = my_head * blks + my_blk
    rows, width = layer_in.shape
    features = w_qkv.shape[1]
    units = w_up.shape[0]
    owners = HEAD_DIM // features
    member = me % owners
    blk_bits = [1 << i for i in range(blks.bit_length() - 1)][::-1]
    head_bits = [blks << i for i in range(heads.bit_length() - 1)][::-1]
    head_masks = slot_masks(head_bits)
    numbers = jnp.arange(count, dtype=jnp.int32)

    place = token_place.reshape(count, rows)
    ranks = place // count
    row_numbers = jnp.arange(rows, dtype=jnp.int32)
    x_sorted, order_hot = sort_rows(layer_in, token_place, me, count)
    x_all = lax.all_gather(x_sorted, "blk", axis=0, tiled=True)
    g_sorted = dot_nn(order_hot, out_grad).astype(BF16)

    qkv_full, out_full, bias_full = w_qkv, w_out, b_qkv
    if owners > 1:
        order = member ^ jnp.arange(owners, dtype=jnp.int32)

        def of_owners(block):
            found = [block] + [swap(block, e, count) for e in range(1, owners)]
            return jnp.stack(found)[order]

        qkv_full = jnp.moveaxis(of_owners(w_qkv), 0, 1).reshape(3, HEAD_DIM, width)
        bias_full = jnp.moveaxis(of_owners(b_qkv), 0, 1).reshape(3, HEAD_DIM)
        out_full = of_owners(w_out).reshape(HEAD_DIM, width)
    qkv_cut, lanes = 3 * HEAD_DIM, 2 * HEAD_DIM

    def all_heads(own, token=None):
        over = swap(own, head_bits[0], count)
        found = [own, over if token is None else after(over, token)]
        for bit in head_bits[1:]:
            found = found + [swap(w, bit, count) for w in found]
        return found

    vectors = jnp.stack([norm_gain, norm_bias, b_out, b_down])
    bias_row = jnp.concatenate([bias_full.reshape(-1), b_up])
    piece = vectors.size
    tile = jnp.zeros((16, width), BF16)
    tile = tile.at[0, : qkv_cut + units].set(bias_row).at[1, :piece].set(vectors.reshape(-1))
    w_list = all_heads(jnp.concatenate([qkv_full.reshape(qkv_cut, width), tile], axis=0))
    g_all = lax.all_gather(after(g_sorted, w_list[1]), "blk", axis=0, tiled=True)
    biases = jnp.stack([w[qkv_cut, : qkv_cut + units] for w in w_list]).astype(F32)

    vectors = jnp.stack([w[qkv_cut + 1, :piece].reshape(vectors.shape) for w in w_list])
    for mask in blk_bits:
        vectors = jnp.concatenate([vectors, swap(vectors, mask, count)], axis=0)
    absolute = me ^ jnp.array(slot_masks(head_bits + blk_bits), dtype=jnp.int32)
    choose = (absolute[None, :] == numbers[:, None]).astype(BF16)
    vectors = dot_nn(choose, vectors.reshape(count, -1)).reshape(count, 4, -1)
    vectors = jnp.transpose(vectors, (1, 0, 2)).reshape(4, width)
    gain, offset, out_bias, down_bias = (vectors[i][None] for i in range(4))

    up_list = all_heads(w_up, vectors)
    qkv_rows, qkv_turned = join(
        w_list,
        [
            [(r, 0, lanes, r * lanes) for r in range(heads)]
            + [(r, lanes, HEAD_DIM, heads * lanes + r * HEAD_DIM) for r in range(heads)]
        ],
        vectors,
        True,
    )
    qkv_bias = jnp.concatenate(
        [biases[:, :lanes].reshape(1, -1), biases[:, lanes:qkv_cut].reshape(1, -1)], axis=1
    )
    up_bias = biases[:, qkv_cut:].reshape(1, -1)

    sorted_place = jnp.sum(
        jnp.where(ranks[:, None, :] == row_numbers[None, :, None], place[:, None, :], 0), axis=2
    )
    slot_head = my_head ^ jnp.array([m // blks for m in head_masks], dtype=jnp.int32)
    device = (slot_head[:, None] * blks + jnp.arange(blks, dtype=jnp.int32)[None, :]).reshape(-1)
    chosen = jnp.where((device[:, None] == numbers[None, :])[:, :, None], sorted_place[None], 0)
    positions = jnp.sum(chosen, axis=1)
    own_positions = positions[:blks].reshape(-1)
    own_place = own_positions - opening_of(own_positions, seq_lengths)
    tiles = rows // GROUP
    positions = jnp.transpose(positions.reshape(count, tiles, GROUP), (1, 0, 2))
    positions = positions.reshape(tiles, count * GROUP)
    meta = attention_meta(positions, seq_lengths, min(CHUNK, count * GROUP))

    (up_rows,) = join(
        up_list, [[(r, 0, units, r * units) for r in range(heads)]], vectors
    )
    x_all = after(x_all, up_rows)
    normed, center, inverse, qkv = project(
        x_all, gain, offset, qkv_turned, qkv_bias, own_place, heads, blks
    )
    qkv_made = qkv[0]
    qkv = exchange(qkv, head_masks, count)
    w_back_list = all_heads(jnp.concatenate([w_down, out_full], axis=0), qkv_made)

    down_rows, out_rows, down_turned = join(
        w_back_list,
        [
            [(r, 0, units, r * units) for r in range(heads)],
            [(r, units, HEAD_DIM, r * HEAD_DIM) for r in range(heads)],
        ],
        qkv_made,
        True,
    )
    hidden = dot_nt(normed, up_rows) + up_bias
    active = gelu_tanh(hidden).astype(BF16)
    meta["low"] = after(meta["low"], active, meta["sine"], meta["cosine"])
    attended, saved = attention_forward(qkv, meta)
    def flat(block):
        return block.reshape(-1, block.shape[-1])

    def own_features(part):
        if owners == 1:
            return part
        mine = jnp.arange(lanes, dtype=jnp.int32) % HEAD_DIM // features == member
        return jnp.where(mine, part, 0)

    def packed(part):
        part = part.reshape(2, blks // 2, rows, HEAD_DIM)
        return jnp.concatenate([part[0], part[1]], axis=-1)

    attended_here = attended[0]
    attended = exchange(attended, head_masks, count)
    attended = [own_features(part) for part in attended]
    mixed = mixed_rows(active, attended, down_rows, out_rows)
    g_late = after(g_all, attended_here)

    heads_grad = dot_nt(g_late, out_rows).astype(BF16)
    heads_grad = [packed(heads_grad[:, r * HEAD_DIM : (r + 1) * HEAD_DIM]) for r in range(heads)]
    mine, others = list(range(heads // 2)), list(range(heads // 2, heads))
    back_sent = outer(attended, active, g_late, others, units, heads_grad[0])
    back_there = [swap(part, head_bits[-1], count) for part in back_sent]
    back_sent = back_sent[0]
    heads_grad = exchange(heads_grad, head_masks, count)
    heads_grad[0] = after(heads_grad[0], back_sent, mixed)
    mixed = mixed.reshape(blks, rows, width)
    mixed = lax.psum_scatter(mixed, "blk", scatter_dimension=0, tiled=False)

    qkv_grad, qkv_sums = attention_backward(heads_grad, meta, saved)
    g_last = after(g_late, qkv_grad[0])
    qkv_grad = [own_features(part) for part in exchange(qkv_grad, head_masks, count)]
    hidden_grad, up_sums = hidden_grads(g_last, hidden, down_turned, g_last)

    pieces = pieces_of(blks, rows)
    split_shape = (2,) * len(blk_bits)
    slots = jnp.arange(blks, dtype=jnp.int32).reshape(split_shape)
    parts = [(blks // 2, begin, end) for (begin, end), _ in pieces]

    def halves(block, far):
        found = []
        for (begin, end), order in pieces:
            axis = blk_bits.index(order[0])
            mine = (my_blk // order[0]) % 2
            piece = block if block.ndim == len(blk_bits) else block[..., begin:end, :]
            found.append(pick(piece, axis, 1 - mine if far else mine))
        return found

    hid_rows = hidden_grad.reshape(blks, rows, heads * units)

    chosen = jnp.concatenate([p.reshape(-1) for p in halves(slots, True) + halves(slots, False)])
    found = shifted(
        hid_rows, qkv_grad, up_rows, qkv_rows, chosen, parts + parts, hidden_grad
    )
    sent, kept = found[: len(parts)], found[len(parts) :]
    back_own, back_far = outer(attended, active, g_last, mine, units, kept[0], back_there)
    back_there = swap(back_far, head_bits[0], count)
    in_sent = outer(qkv_grad, hidden_grad, normed, others, units, back_far)
    in_there = [swap(part, head_bits[-1], count) for part in in_sent]
    in_sent = in_sent[0]
    orders = [order for _, order in pieces]
    norm_grads = norm_sums(
        after(x_all, in_sent).reshape(blks, rows, width),
        center.reshape(blks, rows, 1),
        inverse.reshape(blks, rows, 1),
        list(sent) + list(kept),
        chosen,
        parts + parts,
    )
    own_g = g_sorted.astype(F32)
    sums = jnp.concatenate([norm_grads, jnp.sum(own_g, axis=0)[None]], axis=0)
    sums = jnp.transpose(sums.reshape(3, heads, blks, -1), (2, 1, 0, 3)).reshape(blks, -1)
    relative = jnp.array(slot_masks(blk_bits), dtype=jnp.int32) ^ my_blk
    reached = relative[:, None] == slots.reshape(1, -1)
    reached = jnp.sum(jnp.where(reached[:, :, None], sums[None], 0.0), axis=1)
    kept = [after(kept[0], reached, mixed), kept[1]]
    there = [swap(sent[i], order[0], count) for i, order in enumerate(orders)]
    left = [[b for b in blk_bits if b != order[0]] for order in orders]
    for step in range(1, len(blk_bits)):
        masks = [order[step] for order in orders]
        far, kept = hop(kept, there, masks, left, my_blk, LARGE if step == 1 else LAST)
        there = [swap(f, mask, count) for f, mask in zip(far, masks)]
        left = [[b for b in bits if b != mask] for bits, mask in zip(left, masks)]
        last_far = far[0]
        if step == 1:
            in_own, in_far = outer(qkv_grad, hidden_grad, normed, mine, units, kept[0], in_there)
            in_there = swap(in_far, head_bits[0], count)
            reached = after(reached, in_far, back_there)
            near, away = jnp.split(reached, 2)
            for mask in blk_bits[::-1][:-1]:
                near, away = fold(near, swap(away, mask, count))
            kept = [after(kept[0], in_far, near), kept[1]]

    layer_out = layer_rows(
        x_sorted, mixed, jnp.concatenate([out_bias, down_bias], axis=0), order_hot, last_far
    )
    w_down_grad, w_out_grad = totals(back_own, back_there, units, last_far)
    w_up_grad, w_qkv_grad = totals(in_own, in_there, units, last_far)
    w_qkv_grad = w_qkv_grad.reshape(3, owners, features, width)
    w_qkv_grad = lax.dynamic_index_in_dim(w_qkv_grad, member, 1, False)
    w_out_grad = w_out_grad.reshape(owners, features, width)
    w_out_grad = lax.dynamic_index_in_dim(w_out_grad, member, 0, False)
    qkv_sums = qkv_sums.reshape(3, owners, features)
    b_qkv_grad = lax.dynamic_index_in_dim(qkv_sums, member, 1, False)

    away = after(away, last_far)
    sums = near[0] + swap(away, blk_bits[0], count)[0]
    sums = sums.reshape(heads, -1)
    slot_numbers = jnp.arange(heads, dtype=jnp.int32)
    reached = jnp.where((slot_head[:, None] == slot_numbers[None])[:, :, None], sums[None], 0.0)
    small = jnp.concatenate([jnp.sum(reached, axis=1), up_sums.reshape(heads, units)], axis=1)
    small = exchange([small[r : r + 1] for r in range(heads)], head_masks, count)

    input_grad = input_rows(x_sorted, g_sorted, gain, order_hot, kept, there)
    small = added(small, input_grad)[0]
    vector_grads, b_up_grad = small[:-units].reshape(3, -1), small[-units:]
    return (
        layer_out,
        input_grad,
        vector_grads[0],
        vector_grads[1],
        w_qkv_grad,
        b_qkv_grad,
        w_out_grad,
        vector_grads[2],
        w_up_grad,
        b_up_grad,
        w_down_grad,
        vector_grads[2],
    )


def solution(mesh):
    rows, vector = P(AXES, None), P(AXES)
    qkv, qkv_bias = P(None, AXES, None), P(None, AXES)
    in_specs = (
        rows, rows, vector, vector, qkv, qkv_bias, rows, vector, rows, vector, rows, vector,
        P(), P(),
    )
    out_specs = (
        rows, rows, vector, vector, qkv, qkv_bias, rows, vector, rows, vector, rows, vector,
    )
    return jax.shard_map(
        per_device, mesh=mesh, in_specs=in_specs, out_specs=out_specs, check_vma=False
    )
```
